32 devices in a mesh: wide: 8 (over z, x), narrow: 4 (over y, core).
Axes of the slice: x: 2, y: 2, z: 4, core: 2. Of those that a mesh axis runs over, the one named last changes fastest.
Arguments:
- tokens: bfloat16 [32768, 768], P(('wide', 'narrow')), may hold values from -6 to 6
- features: bfloat16 [32, 24, 24, 1024], P(('wide', 'narrow'))
- segments: int32 [32, 1024], P(('wide', 'narrow')), may hold values from 0 to 7, never falling along the last dimension, each value on 1 to 512 neighbouring positions
- positions: int32 [32, 576], P(('wide', 'narrow')), may hold values from 0 to 1023, as said below
- w_qkv: bfloat16 [768, 2304], P(('wide', 'narrow')), may hold values from -0.21875 to 0.21875
- w_out: bfloat16 [768, 768], P(('wide', 'narrow')), may hold values from -0.21875 to 0.21875
- w_up: bfloat16 [768, 3072], P(('wide', 'narrow')), may hold values from -0.21875 to 0.21875
- w_down: bfloat16 [3072, 768], P(('wide', 'narrow')), may hold values from -0.109375 to 0.109375
- gain_pre: bfloat16 [768], P(('wide', 'narrow')), may hold values from 0.099609375 to 1.8984375
- gain_attn: bfloat16 [768], P(('wide', 'narrow')), may hold values from 0.099609375 to 1.8984375
- gain_mid: bfloat16 [768], P(('wide', 'narrow')), may hold values from 0.099609375 to 1.8984375
- gain_ffn: bfloat16 [3072], P(('wide', 'narrow')), may hold values from 0.099609375 to 1.8984375
- rel_table: bfloat16 [12, 256], P(None, ('wide', 'narrow')), may hold values from -4 to 4
- head_scale: float32 [12], replicated, may hold values from 0.3 to 3
- w_reduce: bfloat16 [1024, 256], P(('wide', 'narrow')), may hold values from -0.1875 to 0.1875
- w_spatial: bfloat16 [2304, 256], P(('wide', 'narrow')), may hold values from -0.125 to 0.125
- w_expand: bfloat16 [256, 1024], P(('wide', 'narrow')), may hold values from -0.375 to 0.375
- w_embed: bfloat16 [1024, 768], P(('wide', 'narrow')), may hold values from -0.1875 to 0.1875
- bn_gain: bfloat16 [1024], P(('wide', 'narrow')), may hold values from 0.099609375 to 1.8984375
- bn_shift: bfloat16 [1024], P(('wide', 'narrow')), may hold values from -3 to 3
- d_out: bfloat16 [32768, 768], P(('wide', 'narrow')), may hold values from -6 to 6
Outputs:
- mixed: bfloat16 [32768, 768], P(('wide', 'narrow'))
- d_tokens: float32 [32768, 768], P(('wide', 'narrow'))
- d_features: float32 [32, 24, 24, 1024], P(('wide', 'narrow'))
- d_w_qkv: float32 [768, 2304], P('wide', 'narrow')
- d_w_out: float32 [768, 768], P(('wide', 'narrow'))
- d_w_up: float32 [768, 3072], P('wide', 'narrow')
- d_w_down: float32 [3072, 768], P('narrow', 'wide')
- d_gain_pre: float32 [768], P(('wide', 'narrow'))
- d_gain_attn: float32 [768], P(('wide', 'narrow'))
- d_gain_mid: float32 [768], P(('wide', 'narrow'))
- d_gain_ffn: float32 [3072], P(('wide', 'narrow'))
- d_rel_table: float32 [12, 256], P(None, ('wide', 'narrow'))
- d_head_scale: float32 [12], replicated
- d_w_reduce: float32 [1024, 256], P(('wide', 'narrow'))
- d_w_spatial: float32 [2304, 256], P(('wide', 'narrow'))
- d_w_expand: float32 [256, 1024], P(('wide', 'narrow'))
- d_w_embed: float32 [1024, 768], P(('wide', 'narrow'))
- d_bn_gain: float32 [1024], P(('wide', 'narrow'))
- d_bn_shift: float32 [1024], P(('wide', 'narrow'))
The draws below stay inside these ranges and needn't reach their ends.
Inputs may be any that keep to these rules, and one draw needn't show every extreme that they name: `segments`: each row's segment numbers never fall; a segment has 1 to 512 tokens. Each image's patches take 576 consecutive positions of its own row, in row-major order; the first row's image begins at 0 and the last row's ends at 1023.
All inputs are finite; a program needn't handle non-finite values.
Results may differ from the reference program's by a relative error of at most 0.017.
Values may be sent and summed in bfloat16 or wider, within the bound.
A program may use at most 320 MiB of HBM per device.

```python
import math
import jax
import jax.numpy as jnp
import numpy as np
from jax import lax

D = 768
HEADS = 12
HDIM = 64
FF = 3072
STEM_IN = 1024
STEM_MID = 256
RSPAN = 128
SEQ = 1024
GRID = 24
SEGS = 8
ROWS = 32
TOKENS = 32768
PATCHES = 576


def draw_features(key, part):
    key = jax.random.fold_in(key, 7)
    order = jnp.arange(ROWS, dtype=jnp.float32) / max(ROWS - 1, 1)
    base = jnp.clip(jax.random.normal(key, (ROWS, GRID, GRID, STEM_IN), jnp.float32), -4.0, 4.0)
    factor = 3.0 ** order
    return (base * factor[:, None, None, None]).astype(jnp.bfloat16)


def draw_positions(key, part):
    key = jax.random.fold_in(key, 11)
    offsets = jax.random.randint(key, (ROWS,), 0, SEQ - PATCHES + 1, jnp.int32)
    offsets = offsets.at[0].set(0).at[ROWS - 1].set(SEQ - PATCHES)
    return (offsets[:, None] + jnp.arange(PATCHES, dtype=jnp.int32)[None, :]).astype(jnp.int32)


def shard_levels(key, dims, shards, low, high):
    loudness, own = 1.0, jax.random.fold_in(key, 6)
    for dim, shards_of in shards:
        draws = jnp.exp(jax.random.uniform(jax.random.fold_in(own, dim), (shards_of,), jnp.float32, low / len(shards), high / len(shards)))
        loudness = loudness * jnp.repeat(draws, dims[dim] // shards_of).reshape([-1 if axis == dim else 1 for axis in range(len(dims))])
    return loudness


def profile(amount, total, reach, skew):
    portions = [(1 << 20) // math.isqrt(grade ** skew) + 1 for grade in range(2, amount + 1)]
    spare, holding = total - reach - (amount - 1), [1] * (amount - 1)
    while spare > 0:
        free = [i for i in range(amount - 1) if holding[i] < reach]
        mass, budget = sum([portions[i] for i in free]), spare
        for i in free:
            more = min(reach - holding[i], max(1, budget * portions[i] // mass), spare)
            holding[i] = holding[i] + more
            spare = spare - more
    return np.array([reach] + holding)


def ragged_sizes(key, number_of, total, limit, lean):
    if number_of == 2:
        one = jax.random.randint(key, (), max(1, total - limit), min(limit, total - 1) + 1)
        return jnp.stack([one, total - one])
    lengths = jnp.asarray(profile(number_of, total, limit, lean), jnp.int32)
    pairs = (number_of - 1) // 2
    donor, sink = lengths[1:1 + 2 * pairs:2], lengths[2:2 + 2 * pairs:2]
    slack = jnp.minimum(donor - 1, limit - sink)
    moved = jax.random.randint(jax.random.fold_in(key, 1), (pairs,), 0, 1 << 20) % (slack + 1)
    lengths = lengths.at[1:1 + 2 * pairs:2].set(donor - moved).at[2:2 + 2 * pairs:2].set(sink + moved)
    return lengths[jax.random.permutation(jax.random.fold_in(key, 2), number_of)]


def noise(rng, shape, scale, reach, cuts=(), held_as=jnp.bfloat16):
    factor_of = shard_levels(rng, shape, cuts, -0.22, 0.18) if cuts else 1.0
    entries = jax.random.normal(rng, shape, jnp.float32) * scale * factor_of
    return jnp.minimum(jnp.maximum(entries, -reach), reach).astype(held_as)


def setup_inputs(seed: int = 0) -> dict:
    arg_keys = jax.random.split(jax.random.key(seed), 22)
    tokens = noise(arg_keys[0], (TOKENS, D), 1.0, 6.0, ((0, 32),))
    features = draw_features(jax.random.fold_in(arg_keys[21], 71), 0)
    segments = jax.vmap(lambda own: jnp.searchsorted(jnp.cumsum(ragged_sizes(own, SEGS, SEQ, SEQ // 2, 2)), jnp.arange(SEQ), side="right"))(jax.random.split(arg_keys[2], ROWS)).reshape((ROWS, SEQ)).astype(jnp.int32)
    positions = draw_positions(jax.random.fold_in(arg_keys[21], 71), 0)
    w_qkv = noise(arg_keys[4], (D, 3 * D), D ** -0.5, 0.21875, ((0, 32),))
    w_out = noise(arg_keys[5], (D, D), D ** -0.5, 0.21875, ((0, 32),))
    w_up = noise(arg_keys[6], (D, FF), D ** -0.5, 0.21875, ((0, 32),))
    w_down = noise(arg_keys[7], (FF, D), FF ** -0.5, 0.109375, ((0, 32),))
    gain_pre = jnp.clip(1.0 + 0.18 * jax.random.normal(arg_keys[8], (D,), jnp.float32), 0.099609375, 1.8984375).astype(jnp.bfloat16)
    gain_attn = jnp.clip(1.0 + 0.18 * jax.random.normal(arg_keys[9], (D,), jnp.float32), 0.099609375, 1.8984375).astype(jnp.bfloat16)
    gain_mid = jnp.clip(1.0 + 0.18 * jax.random.normal(arg_keys[10], (D,), jnp.float32), 0.099609375, 1.8984375).astype(jnp.bfloat16)
    gain_ffn = jnp.clip(1.0 + 0.18 * jax.random.normal(arg_keys[11], (FF,), jnp.float32), 0.099609375, 1.8984375).astype(jnp.bfloat16)
    rel_table = noise(arg_keys[12], (HEADS, 2 * RSPAN), 1.0, 4.0, ((1, 32),))
    head_scale = jnp.clip(jnp.exp(jax.random.uniform(arg_keys[13], (HEADS,), jnp.float32, math.log(0.3), math.log(3.0))), 0.3, 3.0)
    w_reduce = noise(arg_keys[14], (STEM_IN, STEM_MID), STEM_IN ** -0.5, 0.1875, ((0, 32),))
    w_spatial = noise(arg_keys[15], (9 * STEM_MID, STEM_MID), (9 * STEM_MID) ** -0.5, 0.125, ((0, 32),))
    w_expand = noise(arg_keys[16], (STEM_MID, STEM_IN), STEM_MID ** -0.5, 0.375, ((0, 32),))
    w_embed = noise(arg_keys[17], (STEM_IN, D), STEM_IN ** -0.5, 0.1875, ((0, 32),))
    bn_gain = jnp.clip(1.0 + 0.18 * jax.random.normal(arg_keys[18], (STEM_IN,), jnp.float32), 0.099609375, 1.8984375).astype(jnp.bfloat16)
    bn_shift = noise(arg_keys[19], (STEM_IN,), 0.5, 3.0, ((0, 32),))
    d_out = noise(arg_keys[20], (TOKENS, D), 1.0, 6.0, ((0, 32),))
    return dict(tokens=tokens, features=features, segments=segments, positions=positions, w_qkv=w_qkv, w_out=w_out, w_up=w_up, w_down=w_down, gain_pre=gain_pre, gain_attn=gain_attn, gain_mid=gain_mid, gain_ffn=gain_ffn, rel_table=rel_table, head_scale=head_scale, w_reduce=w_reduce, w_spatial=w_spatial, w_expand=w_expand, w_embed=w_embed, bn_gain=bn_gain, bn_shift=bn_shift, d_out=d_out)


@jax.custom_vjp
def low(v):
    return lax.optimization_barrier(v.astype(jnp.bfloat16)).astype(jnp.float32)

@jax.custom_vjp
def low_back(v):
    return v

def low_keep(v):
    return (low(v), None)

def low_pass(kept, grad):
    return (grad,)

def back_keep(v):
    return (v, None)

def back_low(kept, grad):
    return (low(grad),)
low.defvjp(low_keep, low_pass)
low_back.defvjp(back_keep, back_low)
epsilon = 1e-05
highest = lax.Precision.HIGHEST

def product(lhs_matrix, rhs_matrix):
    return jnp.dot(lhs_matrix, rhs_matrix, precision=highest)

def layer_norm(values, gain):
    average = lax.optimization_barrier(jnp.mean(values, axis=-1, keepdims=True))
    centred = values - average
    spread = lax.optimization_barrier(jnp.mean(centred * centred, axis=-1, keepdims=True))
    return centred * lax.rsqrt(spread + epsilon) * gain

def smooth(values):
    return jax.nn.gelu(values, approximate=True)

def unfold(grid):
    side = grid.shape[1]
    padded = jnp.pad(grid, ((0, 0), (1, 1), (1, 1), (0, 0)))
    pieces = [padded[:, row_off:row_off + side, col_off:col_off + side, :] for row_off in range(3) for col_off in range(3)]
    return jnp.concatenate(pieces, axis=-1)

def stem(features, w_reduce, w_spatial, w_expand, bn_gain, bn_shift, w_embed):
    images, side = (features.shape[0], features.shape[1])
    patch_count = images * side * side
    stem_in = features.reshape(patch_count, STEM_IN)
    first = low(smooth(low_back(product(stem_in, w_reduce))))
    columns = unfold(first.reshape(images, side, side, STEM_MID)).reshape(patch_count, 9 * STEM_MID)
    second = low(smooth(low_back(product(columns, w_spatial))))
    third = low_back(product(second, w_expand))
    bn_mean = lax.optimization_barrier(jnp.mean(third, axis=0))
    bn_var = lax.optimization_barrier(jnp.mean(third * third, axis=0)) - bn_mean * bn_mean
    normed = (third - bn_mean) * lax.rsqrt(bn_var + epsilon) * bn_gain + bn_shift
    joined = low(smooth(normed + stem_in))
    return low_back(product(joined, w_embed))

def relative(table, start, block, length):
    query_pos = (start + jnp.arange(block, dtype=jnp.int32)).astype(jnp.int32)
    key_pos = jnp.arange(length, dtype=jnp.int32)
    bucket = jnp.clip(key_pos[None, :] - query_pos[:, None], -RSPAN, RSPAN - 1) + RSPAN
    return jnp.take(table, bucket.astype(jnp.int32), axis=1)

def encoder_row(inputs, segment, layer_weights):
    w_qkv, w_out, w_up, w_down, gain_pre, gain_attn, gain_mid, gain_ffn, table, head_scale = layer_weights
    length = inputs.shape[0]
    normed0 = low(layer_norm(inputs, gain_pre))
    packed = low(low_back(product(normed0, w_qkv)))
    queries = packed[:, :D].reshape(length, HEADS, HDIM)
    keys = packed[:, D:2 * D].reshape(length, HEADS, HDIM)
    values = packed[:, 2 * D:].reshape(length, HEADS, HDIM)
    block = min(512, length)

    def attend(start):
        query_rows = lax.dynamic_slice_in_dim(queries, start, block, 0)
        segment_rows = lax.dynamic_slice_in_dim(segment, start, block, 0)
        scores = jnp.einsum('qhd,khd->hqk', query_rows, keys, precision=highest) * HDIM ** (-0.5)
        scores = low_back(scores + relative(table, start, block, length))
        allowed = (segment_rows[:, None] == segment[None, :])[None]
        probs = low(jax.nn.softmax(jnp.where(allowed, scores, -1e+30), axis=-1))
        return jnp.einsum('hqk,khd->qhd', probs, values, precision=highest)
    starts = jnp.arange(length // block, dtype=jnp.int32) * block
    attended = low_back(lax.map(jax.checkpoint(attend), starts).reshape(length, HEADS, HDIM))
    scaled = (attended * head_scale[None, :, None]).reshape(length, D)
    mixed_in = low(layer_norm(scaled, gain_attn))
    middle = inputs + low_back(product(mixed_in, w_out))
    normed2 = low(layer_norm(middle, gain_mid))
    activ = smooth(low_back(product(normed2, w_up)))
    narrowed = low(layer_norm(activ, gain_ffn))
    return middle + low_back(product(narrowed, w_down))

def forward(tokens, features, params, segments, positions):
    w_qkv, w_out, w_up, w_down, gain_pre, gain_attn, gain_mid, gain_ffn, rel_table, head_scale, w_reduce, w_spatial, w_expand, w_embed, bn_gain, bn_shift = params
    embedded = stem(features, w_reduce, w_spatial, w_expand, bn_gain, bn_shift, w_embed).reshape(ROWS, PATCHES, D)
    row_index = jnp.arange(ROWS, dtype=jnp.int32)[:, None]
    start_rows = tokens.reshape(ROWS, SEQ, D).at[row_index, positions].add(embedded)
    layer_weights = (w_qkv, w_out, w_up, w_down, gain_pre, gain_attn, gain_mid, gain_ffn, rel_table, head_scale)

    def one_row(pair):
        return encoder_row(pair[0], pair[1], layer_weights)
    result = lax.map(jax.checkpoint(one_row), (start_rows, segments))
    return result.reshape(TOKENS, D)

def reference(tokens, features, segments, positions, w_qkv, w_out, w_up, w_down, gain_pre, gain_attn, gain_mid, gain_ffn, rel_table, head_scale, w_reduce, w_spatial, w_expand, w_embed, bn_gain, bn_shift, d_out):
    params = tuple((item.astype(jnp.float32) for item in (w_qkv, w_out, w_up, w_down, gain_pre, gain_attn, gain_mid, gain_ffn, rel_table, head_scale, w_reduce, w_spatial, w_expand, w_embed, bn_gain, bn_shift)))

    def wrapped(token_vals, feature_vals, param_vals):
        return forward(token_vals, feature_vals, param_vals, segments, positions)
    result, pullback = jax.vjp(wrapped, tokens.astype(jnp.float32), features.astype(jnp.float32), params)
    grad_tokens, grad_features, grads = pullback(d_out.astype(jnp.float32))
    g_qkv, g_out, g_up, g_down, g_pre, g_attn, g_mid, g_ffn, g_table, g_head, g_reduce, g_spatial, g_expand, g_embed, g_bn_gain, g_bn_shift = grads
    return (result.astype(jnp.bfloat16), grad_tokens, grad_features, g_qkv, g_out, g_up, g_down, g_pre, g_attn, g_mid, g_ffn, g_table, g_head, g_reduce, g_spatial, g_expand, g_embed, g_bn_gain, g_bn_shift)
```

```python
import jax
import jax.numpy as jnp
from jax import lax
from jax.experimental import pallas as pl
from jax.experimental.pallas import tpu as pltpu
from jax.sharding import PartitionSpec as P

D = 768
HEADS = 12
HDIM = 64
RSPAN = 128


epsilon = 1e-05


def product(lhs_matrix, rhs_matrix):
    return jnp.dot(lhs_matrix, rhs_matrix, preferred_element_type=jnp.float32)


def product_tn(lhs_matrix, rhs_matrix):
    return lax.dot_general(
        lhs_matrix, rhs_matrix, (((0,), (0,)), ((), ())), preferred_element_type=jnp.float32
    )


def product_nt(lhs_matrix, rhs_matrix):
    return lax.dot_general(
        lhs_matrix, rhs_matrix, (((1,), (1,)), ((), ())), preferred_element_type=jnp.float32
    )


def layer_norm(values, gain):
    average = jnp.mean(values, axis=-1, keepdims=True)
    centred = values - average
    inv_std = lax.rsqrt(jnp.mean(centred * centred, axis=-1, keepdims=True) + epsilon)
    unit_rows = centred * inv_std
    return (unit_rows * gain, unit_rows, inv_std)


def layer_norm_back(cotangent, unit_rows, inv_std, gain):
    weighted = cotangent * gain
    inner = (
        weighted
        - jnp.mean(weighted, axis=-1, keepdims=True)
        - unit_rows * jnp.mean(weighted * unit_rows, axis=-1, keepdims=True)
    )
    return (inv_std * inner, jnp.sum(cotangent * unit_rows, axis=0))


def smooth(values):
    return jax.nn.gelu(values, approximate=True)


def smooth_back(values, cotangent):
    unused, pullback = jax.vjp(smooth, values)
    return pullback(cotangent)[0]


def unfold(grid):
    side = grid.shape[1]
    padded = jnp.pad(grid, ((0, 0), (1, 1), (1, 1), (0, 0)))
    pieces = [
        padded[:, row_off : row_off + side, col_off : col_off + side, :]
        for row_off in range(3)
        for col_off in range(3)
    ]
    return jnp.concatenate(pieces, axis=-1)


def fold(columns):
    channels = columns.shape[-1] // 9
    side = columns.shape[1]
    total = jnp.zeros((columns.shape[0], side + 2, side + 2, channels), jnp.float32)
    for row_off in range(3):
        for col_off in range(3):
            which = row_off * 3 + col_off
            piece = columns[..., which * channels : (which + 1) * channels]
            total = total + jnp.pad(
                piece, ((0, 0), (row_off, 2 - row_off), (col_off, 2 - col_off), (0, 0))
            )
    return total[:, 1:-1, 1:-1, :]


PAIRS = HEADS // 2
BLK = 128
NEG = -1e30


def dot_nn(a, b):
    return lax.dot_general(a, b, (((1,), (0,)), ((), ())), preferred_element_type=jnp.float32)


def dot_nt(a, b):
    return lax.dot_general(a, b, (((1,), (1,)), ((), ())), preferred_element_type=jnp.float32)


def split_heads(pair, scale):
    lane = lax.broadcasted_iota(jnp.int32, pair.shape, 1)
    vals = pair * jnp.asarray(scale, pair.dtype)
    zero = jnp.zeros_like(vals)
    return jnp.concatenate([jnp.where(lane < HDIM, vals, zero), jnp.where(lane < HDIM, zero, vals)], axis=0)


def join_heads(both):
    row = lax.broadcasted_iota(jnp.int32, (2 * HDIM, BLK), 0)
    return jnp.where(row < HDIM, both[:, :BLK], both[:, BLK:])


def bias_strips(table):
    rev = jnp.flip(table.astype(jnp.float32), axis=1)
    first, last = rev[:, 255:256], rev[:, 0:1]
    below = jnp.concatenate([jnp.broadcast_to(first, (HEADS, 129)), rev[:, 128:255]], axis=1)
    middle = jnp.concatenate([rev[:, 127:256], rev[:, 0:127]], axis=1)
    above = jnp.concatenate([last, rev[:, 0:127], jnp.broadcast_to(last, (HEADS, 128))], axis=1)
    low = jnp.broadcast_to(first, (HEADS, 256))
    high = jnp.broadcast_to(last, (HEADS, 256))
    return jnp.stack([low, below, middle, above, high], axis=1)


def table_from_strips(sums):
    low, below, middle, above, high = (sums[:, i] for i in range(5))
    total = jnp.concatenate([middle[:, 129:256], middle[:, 0:129]], axis=1)
    zero = jnp.zeros((HEADS, 127), jnp.float32)
    first = jnp.sum(low, axis=1, keepdims=True) + jnp.sum(below[:, :129], axis=1, keepdims=True)
    last = jnp.sum(high, axis=1, keepdims=True) + above[:, 0:1] + jnp.sum(above[:, 128:], axis=1, keepdims=True)
    total = total + jnp.concatenate([jnp.zeros((HEADS, 128), jnp.float32), below[:, 129:], first], axis=1)
    head = jnp.concatenate([above[:, 1:128], jnp.zeros((HEADS, 129), jnp.float32)], axis=1)
    total = total + head + jnp.concatenate([last, jnp.zeros((HEADS, 255), jnp.float32)], axis=1)
    return jnp.flip(total, axis=1)


def windows(segments):
    seg = segments.reshape(-1)
    starts = seg[::BLK]
    ends = seg[BLK - 1 :: BLK]
    low = jnp.sum((seg[None, :] < starts[:, None]).astype(jnp.int32), axis=1) // BLK
    high = (jnp.sum((seg[None, :] <= ends[:, None]).astype(jnp.int32), axis=1) + BLK - 1) // BLK
    return jnp.stack([low, high])


def attend_kernel(win, packed, segk, segq, strips, out, logsum, bias, vt, qm, acc, stat):
    i = pl.program_id(0)

    @pl.when(i == 0)
    def _():
        for hp in range(PAIRS):
            vt[pl.ds(hp * 128, 128), :] = packed[:, pl.ds(2 * D + hp * 128, 128)].T
            for d in range(5):
                for half in range(2):
                    row = strips[2 * hp + half, pl.ds(d, 1), :]
                    tile = jnp.broadcast_to(row, (BLK, 256))
                    if 0 < d < 4:
                        tile = pltpu.roll(tile, 0, 1, stride=1, stride_axis=0)
                    bias[hp, d, :, pl.ds(half * BLK, BLK)] = tile[:, :BLK]

    rows = pl.ds(pl.multiple_of(i * BLK, BLK), BLK)
    for hp in range(PAIRS):
        qm[hp] = split_heads(packed[rows, pl.ds(hp * 128, 128)], HDIM ** -0.5)
        acc[hp] = jnp.zeros((128, 256), jnp.float32)
        stat[hp, 0] = jnp.full((1, 256), NEG, jnp.float32)
        stat[hp, 1] = jnp.zeros((1, 256), jnp.float32)
    sq = segq[:, rows]
    sq2 = jnp.concatenate([sq, sq], axis=1)

    def body(kb, carry):
        keys = pl.ds(pl.multiple_of(kb * BLK, BLK), BLK)
        allowed = segk[keys, :] == sq2
        d = jnp.clip(kb - i, -2, 2) + 2
        for hp in range(PAIRS):
            s = dot_nt(packed[keys, pl.ds(D + hp * 128, 128)], qm[hp])
            s = jnp.where(allowed, s + bias[hp, d], NEG)
            old = stat[hp, 0]
            new = jnp.maximum(old, jnp.max(s, axis=0, keepdims=True))
            p = jnp.exp(s - new)
            alpha = jnp.exp(old - new)
            stat[hp, 0] = new
            stat[hp, 1] = stat[hp, 1] * alpha + jnp.sum(p, axis=0, keepdims=True)
            acc[hp] = acc[hp] * alpha + dot_nn(vt[pl.ds(hp * 128, 128), keys], p.astype(jnp.bfloat16))
        return carry

    lax.fori_loop(win[0, i], win[1, i], body, 0)
    for hp in range(PAIRS):
        total = stat[hp, 1]
        out[:, pl.ds(hp * 128, 128)] = join_heads(acc[hp] / total).T
        logsum[0, pl.ds(hp, 1), :] = stat[hp, 0] + jnp.log(total)


def attend(packed, segments, strips, win):
    length = packed.shape[0]
    blocks = length // BLK
    seg = segments.reshape(1, length)
    whole = lambda shape: pl.BlockSpec(shape, lambda i, w: (0,) * len(shape))
    return pl.pallas_call(
        attend_kernel,
        out_shape=(
            jax.ShapeDtypeStruct((length, D), jnp.float32),
            jax.ShapeDtypeStruct((blocks, PAIRS, 256), jnp.float32),
            jax.ShapeDtypeStruct((PAIRS, 5, BLK, 256), jnp.float32),
        ),
        grid_spec=pltpu.PrefetchScalarGridSpec(
            num_scalar_prefetch=1,
            grid=(blocks,),
            in_specs=[whole((length, 3 * D)), whole((length, 1)), whole((1, length)), whole((HEADS, 5, 256))],
            out_specs=(
                pl.BlockSpec((BLK, D), lambda i, w: (i, 0)),
                pl.BlockSpec((1, PAIRS, 256), lambda i, w: (i, 0, 0)),
                whole((PAIRS, 5, BLK, 256)),
            ),
            scratch_shapes=[
                pltpu.VMEM((D, length), jnp.bfloat16),
                pltpu.VMEM((PAIRS, 256, 128), jnp.bfloat16),
                pltpu.VMEM((PAIRS, 128, 256), jnp.float32),
                pltpu.VMEM((PAIRS, 2, 1, 256), jnp.float32),
            ],
        ),
        compiler_params=pltpu.CompilerParams(vmem_limit_bytes=48 * 2**20),
        cost_estimate=pl.CostEstimate(flops=2 * 10**10, bytes_accessed=10**7, transcendentals=6 * 10**6),
        name="attend",
    )(win, packed, seg.reshape(length, 1), seg, strips)


def unskew(tile):
    row = lax.broadcasted_iota(jnp.int32, tile.shape, 0)
    width = tile.shape[1]
    for bit in range(7):
        step = 1 << bit
        tile = jnp.where((row & step) != 0, pltpu.roll(tile, width - step, 1), tile)
    return tile


def attend_back_kernel(win, packed, grads, attended, segk, segq, bias, logsum, out, tab, kt, qm, om, dqt, dk, dv, gt):
    i = pl.program_id(0)
    last = pl.num_programs(0) - 1

    @pl.when(i == 0)
    def _():
        for hp in range(PAIRS):
            kt[pl.ds(hp * 128, 128), :] = packed[:, pl.ds(D + hp * 128, 128)].T
        dk[...] = jnp.zeros_like(dk)
        dv[...] = jnp.zeros_like(dv)
        gt[...] = jnp.zeros_like(gt)

    rows = pl.ds(pl.multiple_of(i * BLK, BLK), BLK)
    dots = []
    for hp in range(PAIRS):
        cols = pl.ds(hp * 128, 128)
        qm[hp] = split_heads(packed[rows, cols], HDIM ** -0.5)
        om[hp] = split_heads(grads[:, cols], 1.0)
        cross = (grads[:, cols].astype(jnp.float32) * attended[:, cols]).T
        dots.append(jnp.concatenate([
            jnp.sum(cross[:HDIM], axis=0, keepdims=True),
            jnp.sum(cross[HDIM:], axis=0, keepdims=True)], axis=1))
        dqt[hp] = jnp.zeros((128, 256), jnp.float32)
    sq = segq[:, rows]
    sq2 = jnp.concatenate([sq, sq], axis=1)

    def body(kb, carry):
        keys = pl.ds(pl.multiple_of(kb * BLK, BLK), BLK)
        allowed = segk[keys, :] == sq2
        d = jnp.clip(kb - i, -2, 2) + 2
        for hp in range(PAIRS):
            cols = pl.ds(hp * 128, 128)
            s = dot_nt(packed[keys, pl.ds(D + hp * 128, 128)], qm[hp]) + bias[hp, d]
            p = jnp.exp(jnp.where(allowed, s, NEG) - logsum[0, pl.ds(hp, 1), :])
            dp = dot_nt(packed[keys, pl.ds(2 * D + hp * 128, 128)], om[hp])
            ds = p * (dp - dots[hp])
            gt[hp, d] += ds
            low = ds.astype(jnp.bfloat16)
            dv[keys, cols] += dot_nn(p.astype(jnp.bfloat16), om[hp])
            dk[keys, cols] += dot_nn(low, qm[hp])
            dqt[hp] += dot_nn(kt[cols, keys], low)
        return carry

    lax.fori_loop(win[0, i], win[1, i], body, 0)
    for hp in range(PAIRS):
        out[rows, pl.ds(hp * 128, 128)] = (join_heads(dqt[hp]).T * (HDIM ** -0.5)).astype(jnp.bfloat16)

    @pl.when(i == last)
    def _():
        out[:, pl.ds(D, D)] = dk[...].astype(jnp.bfloat16)
        out[:, pl.ds(2 * D, D)] = dv[...].astype(jnp.bfloat16)
        for hp in range(PAIRS):
            for half in range(2):
                for d in range(5):
                    tile = gt[hp, d, :, pl.ds(half * BLK, BLK)]
                    tile = jnp.concatenate([tile, jnp.zeros_like(tile)], axis=1)
                    if 0 < d < 4:
                        tile = unskew(tile)
                    tab[2 * hp + half, pl.ds(d, 1), :] = jnp.sum(tile, axis=0, keepdims=True)


def attend_back(packed, grads, attended, segments, bias, logsum, win):
    length = packed.shape[0]
    blocks = length // BLK
    seg = segments.reshape(1, length)
    whole = lambda shape: pl.BlockSpec(shape, lambda i, w: (0,) * len(shape))
    return pl.pallas_call(
        attend_back_kernel,
        out_shape=(
            jax.ShapeDtypeStruct((length, 3 * D), jnp.bfloat16),
            jax.ShapeDtypeStruct((HEADS, 5, 256), jnp.float32),
        ),
        grid_spec=pltpu.PrefetchScalarGridSpec(
            num_scalar_prefetch=1,
            grid=(blocks,),
            in_specs=[
                whole((length, 3 * D)),
                pl.BlockSpec((BLK, D), lambda i, w: (i, 0)),
                pl.BlockSpec((BLK, D), lambda i, w: (i, 0)),
                whole((length, 1)),
                whole((1, length)),
                whole((PAIRS, 5, BLK, 256)),
                pl.BlockSpec((1, PAIRS, 256), lambda i, w: (i, 0, 0)),
            ],
            out_specs=(whole((length, 3 * D)), whole((HEADS, 5, 256))),
            scratch_shapes=[
                pltpu.VMEM((D, length), jnp.bfloat16),
                pltpu.VMEM((PAIRS, 256, 128), jnp.bfloat16),
                pltpu.VMEM((PAIRS, 256, 128), jnp.bfloat16),
                pltpu.VMEM((PAIRS, 128, 256), jnp.float32),
                pltpu.VMEM((length, D), jnp.float32),
                pltpu.VMEM((length, D), jnp.float32),
                pltpu.VMEM((PAIRS, 5, BLK, 256), jnp.float32),
            ],
        ),
        compiler_params=pltpu.CompilerParams(vmem_limit_bytes=56 * 2**20),
        cost_estimate=pl.CostEstimate(flops=5 * 10**10, bytes_accessed=2 * 10**7, transcendentals=6 * 10**6),
        name="attend_back",
    )(win, packed, grads, attended, seg.reshape(length, 1), seg, bias, logsum)


def local(
    tokens,
    features,
    segments,
    positions,
    w_qkv,
    w_out,
    w_up,
    w_down,
    gain_pre,
    gain_attn,
    gain_mid,
    gain_ffn,
    rel_table,
    head_scale,
    w_reduce,
    w_spatial,
    w_expand,
    w_embed,
    bn_gain,
    bn_shift,
    d_out,
):
    gathered = (
        lax.all_gather(w_qkv, ("wide", "narrow"), axis=0, tiled=True),
        lax.all_gather(w_out, ("wide", "narrow"), axis=0, tiled=True),
        lax.all_gather(w_up, ("wide", "narrow"), axis=0, tiled=True),
        lax.all_gather(w_down, ("wide", "narrow"), axis=0, tiled=True),
        lax.all_gather(gain_pre, ("wide", "narrow"), axis=0, tiled=True),
        lax.all_gather(gain_attn, ("wide", "narrow"), axis=0, tiled=True),
        lax.all_gather(gain_mid, ("wide", "narrow"), axis=0, tiled=True),
        lax.all_gather(gain_ffn, ("wide", "narrow"), axis=0, tiled=True),
        lax.all_gather(rel_table, ("wide", "narrow"), axis=1, tiled=True),
        lax.all_gather(w_reduce, ("wide", "narrow"), axis=0, tiled=True),
        lax.all_gather(w_spatial, ("wide", "narrow"), axis=0, tiled=True),
        lax.all_gather(w_expand, ("wide", "narrow"), axis=0, tiled=True),
        lax.all_gather(w_embed, ("wide", "narrow"), axis=0, tiled=True),
        lax.all_gather(bn_gain, ("wide", "narrow"), axis=0, tiled=True),
        lax.all_gather(bn_shift, ("wide", "narrow"), axis=0, tiled=True),
    )
    (
        full_qkv,
        full_out,
        full_up,
        full_down,
        full_pre,
        full_attn,
        full_mid,
        full_ffn,
        full_table,
        full_reduce,
        full_spatial,
        full_expand,
        full_embed,
        full_bn_gain,
        full_bn_shift,
    ) = gathered
    rows, length = (segments.shape[0], segments.shape[1])
    images, side = (features.shape[0], features.shape[1])
    patch_count = images * side * side
    whole = patch_count * lax.axis_size(("wide", "narrow"))
    stem_in = features.reshape(patch_count, features.shape[3])
    pre_first = product(stem_in, full_reduce)
    first = smooth(pre_first).astype(jnp.bfloat16)
    columns = unfold(first.reshape(images, side, side, first.shape[1])).reshape(
        patch_count, 9 * first.shape[1]
    )
    pre_second = product(columns, full_spatial)
    second = smooth(pre_second).astype(jnp.bfloat16)
    third = product(second, full_expand)
    bn_total, bn_squares = lax.psum(
        (jnp.sum(third, axis=0), jnp.sum(third * third, axis=0)), ("wide", "narrow")
    )
    bn_mean = bn_total / whole
    bn_inv = lax.rsqrt(bn_squares / whole - bn_mean * bn_mean + epsilon)
    bn_unit = (third - bn_mean) * bn_inv
    pre_joined = (
        bn_unit * full_bn_gain.astype(jnp.float32)
        + full_bn_shift.astype(jnp.float32)
        + stem_in.astype(jnp.float32)
    )
    joined = smooth(pre_joined).astype(jnp.bfloat16)
    embedded = product(joined, full_embed).reshape(images, side * side, -1)
    row_index = jnp.arange(rows, dtype=jnp.int32)[:, None]
    start_rows = (
        tokens.astype(jnp.float32).reshape(rows, length, -1).at[row_index, positions].add(embedded)
    )
    start = start_rows.reshape(rows * length, -1)
    normed0, unit0, inv0 = layer_norm(start, full_pre.astype(jnp.float32))
    normed0_low = normed0.astype(jnp.bfloat16)
    packed = product(normed0_low, full_qkv).astype(jnp.bfloat16)
    win = windows(segments)
    attended, logsums, bias = attend(packed, segments, bias_strips(full_table), win)
    scale_row = jnp.repeat(head_scale, HDIM)[None, :]
    scaled = attended * scale_row
    mixed_in, unit1, inv1 = layer_norm(scaled, full_attn.astype(jnp.float32))
    mixed_low = mixed_in.astype(jnp.bfloat16)
    middle = start + product(mixed_low, full_out)
    normed2, unit2, inv2 = layer_norm(middle, full_mid.astype(jnp.float32))
    normed2_low = normed2.astype(jnp.bfloat16)
    pre_up = product(normed2_low, full_up)
    activ = smooth(pre_up)
    narrowed, unit3, inv3 = layer_norm(activ, full_ffn.astype(jnp.float32))
    narrowed_low = narrowed.astype(jnp.bfloat16)
    result = middle + product(narrowed_low, full_down)
    mixed = result.astype(jnp.bfloat16)
    group_norm0, group_norm2, group_out = (
        lax.all_gather(normed0_low, "narrow", axis=0, tiled=True),
        lax.all_gather(normed2_low, "narrow", axis=0, tiled=True),
        lax.all_gather(d_out, "narrow", axis=0, tiled=True),
    )
    again = (
        lax.all_gather(w_qkv, ("wide", "narrow"), axis=0, tiled=True),
        lax.all_gather(w_out, ("wide", "narrow"), axis=0, tiled=True),
        lax.all_gather(w_up, ("wide", "narrow"), axis=0, tiled=True),
        lax.all_gather(w_down, ("wide", "narrow"), axis=0, tiled=True),
        lax.all_gather(gain_pre, ("wide", "narrow"), axis=0, tiled=True),
        lax.all_gather(gain_attn, ("wide", "narrow"), axis=0, tiled=True),
        lax.all_gather(gain_mid, ("wide", "narrow"), axis=0, tiled=True),
        lax.all_gather(gain_ffn, ("wide", "narrow"), axis=0, tiled=True),
        lax.all_gather(rel_table, ("wide", "narrow"), axis=1, tiled=True),
        lax.all_gather(w_reduce, ("wide", "narrow"), axis=0, tiled=True),
        lax.all_gather(w_spatial, ("wide", "narrow"), axis=0, tiled=True),
        lax.all_gather(w_expand, ("wide", "narrow"), axis=0, tiled=True),
        lax.all_gather(w_embed, ("wide", "narrow"), axis=0, tiled=True),
        lax.all_gather(bn_gain, ("wide", "narrow"), axis=0, tiled=True),
        lax.all_gather(bn_shift, ("wide", "narrow"), axis=0, tiled=True),
    )
    (
        back_qkv,
        back_out,
        back_up,
        back_down,
        back_pre,
        back_attn,
        back_mid,
        back_ffn,
        back_table,
        back_reduce,
        back_spatial,
        back_expand,
        back_embed,
        back_bn_gain,
        back_bn_shift,
    ) = again
    grad_result = d_out.astype(jnp.float32)
    grad_narrowed = product_nt(d_out, back_down)
    grad_activ, grad_gain_ffn = layer_norm_back(
        grad_narrowed, unit3, inv3, back_ffn.astype(jnp.float32)
    )
    grad_pre_up = smooth_back(pre_up, grad_activ).astype(jnp.bfloat16)
    ffn_grad_cols, ffn_act_cols = (
        lax.all_to_all(grad_pre_up, "narrow", split_axis=1, concat_axis=0, tiled=True),
        lax.all_to_all(narrowed_low, "narrow", split_axis=1, concat_axis=0, tiled=True),
    )
    grad_w_down = product_tn(ffn_act_cols, group_out)
    grad_w_up = product_tn(group_norm2, ffn_grad_cols)
    grad_normed2 = product_nt(grad_pre_up, back_up)
    grad_mid_in, grad_gain_mid = layer_norm_back(
        grad_normed2, unit2, inv2, back_mid.astype(jnp.float32)
    )
    grad_middle = grad_result + grad_mid_in
    grad_branch = grad_middle.astype(jnp.bfloat16)
    grad_w_out = product_tn(mixed_low, grad_branch)
    grad_mixed_in = product_nt(grad_branch, back_out)
    grad_scaled, grad_gain_attn = layer_norm_back(
        grad_mixed_in, unit1, inv1, back_attn.astype(jnp.float32)
    )
    grad_head_local = jnp.sum(jnp.sum(grad_scaled * attended, axis=0).reshape(HEADS, HDIM), axis=1)
    grad_attended = (grad_scaled * scale_row).astype(jnp.bfloat16)
    grad_packed, grad_strips = attend_back(packed, grad_attended, attended, segments, bias, logsums, win)
    grad_table = table_from_strips(grad_strips)
    qkv_cols = lax.all_to_all(grad_packed, "narrow", split_axis=1, concat_axis=0, tiled=True)
    grad_w_qkv = product_tn(group_norm0, qkv_cols)
    sum_qkv, sum_up, sum_down = (
        lax.psum_scatter(
            grad_w_qkv.astype(jnp.bfloat16), "wide", scatter_dimension=0, tiled=True
        ).astype(jnp.float32),
        lax.psum_scatter(
            grad_w_up.astype(jnp.bfloat16), "wide", scatter_dimension=0, tiled=True
        ).astype(jnp.float32),
        lax.psum_scatter(
            grad_w_down.astype(jnp.bfloat16), "wide", scatter_dimension=1, tiled=True
        ).astype(jnp.float32),
    )
    grad_normed0 = product_nt(grad_packed, back_qkv)
    grad_start_in, grad_gain_pre = layer_norm_back(
        grad_normed0, unit0, inv0, back_pre.astype(jnp.float32)
    )
    grad_tokens = grad_middle + grad_start_in
    grad_embedded = (
        grad_tokens.reshape(rows, length, -1)[row_index, positions]
        .reshape(patch_count, -1)
        .astype(jnp.bfloat16)
    )
    grad_w_embed = product_tn(joined, grad_embedded)
    grad_joined = product_nt(grad_embedded, back_embed)
    grad_pre_joined = smooth_back(pre_joined, grad_joined)
    grad_bn_shift = jnp.sum(grad_pre_joined, axis=0)
    grad_bn_gain = jnp.sum(grad_pre_joined * bn_unit, axis=0)
    grad_unit = grad_pre_joined * back_bn_gain.astype(jnp.float32)
    sum_unit, sum_cross, grad_head = lax.psum(
        (jnp.sum(grad_unit, axis=0), jnp.sum(grad_unit * bn_unit, axis=0), grad_head_local),
        ("wide", "narrow"),
    )
    grad_third = (bn_inv * (grad_unit - sum_unit / whole - bn_unit * (sum_cross / whole))).astype(
        jnp.bfloat16
    )
    grad_w_expand = product_tn(second, grad_third)
    grad_second = product_nt(grad_third, back_expand)
    grad_pre_second = smooth_back(pre_second, grad_second).astype(jnp.bfloat16)
    grad_w_spatial = product_tn(columns, grad_pre_second)
    grad_columns = product_nt(grad_pre_second, back_spatial)
    grad_first = fold(grad_columns.reshape(images, side, side, -1)).reshape(patch_count, -1)
    grad_pre_first = smooth_back(pre_first, grad_first).astype(jnp.bfloat16)
    grad_w_reduce = product_tn(stem_in, grad_pre_first)
    grad_features = (grad_pre_joined + product_nt(grad_pre_first, back_reduce)).reshape(
        features.shape
    )
    summed = (
        lax.psum_scatter(grad_w_out, ("wide", "narrow"), scatter_dimension=0, tiled=True),
        lax.psum_scatter(grad_gain_pre, ("wide", "narrow"), scatter_dimension=0, tiled=True),
        lax.psum_scatter(grad_gain_attn, ("wide", "narrow"), scatter_dimension=0, tiled=True),
        lax.psum_scatter(grad_gain_mid, ("wide", "narrow"), scatter_dimension=0, tiled=True),
        lax.psum_scatter(grad_gain_ffn, ("wide", "narrow"), scatter_dimension=0, tiled=True),
        lax.psum_scatter(grad_table, ("wide", "narrow"), scatter_dimension=1, tiled=True),
        lax.psum_scatter(grad_w_reduce, ("wide", "narrow"), scatter_dimension=0, tiled=True),
        lax.psum_scatter(grad_w_spatial, ("wide", "narrow"), scatter_dimension=0, tiled=True),
        lax.psum_scatter(grad_w_expand, ("wide", "narrow"), scatter_dimension=0, tiled=True),
        lax.psum_scatter(grad_w_embed, ("wide", "narrow"), scatter_dimension=0, tiled=True),
        lax.psum_scatter(grad_bn_gain, ("wide", "narrow"), scatter_dimension=0, tiled=True),
        lax.psum_scatter(grad_bn_shift, ("wide", "narrow"), scatter_dimension=0, tiled=True),
    )
    (
        sum_out,
        sum_pre,
        sum_attn,
        sum_mid,
        sum_ffn,
        sum_table,
        sum_reduce,
        sum_spatial,
        sum_expand,
        sum_embed,
        sum_bn_gain,
        sum_bn_shift,
    ) = summed
    return (
        mixed,
        grad_tokens,
        grad_features,
        sum_qkv,
        sum_out,
        sum_up,
        sum_down,
        sum_pre,
        sum_attn,
        sum_mid,
        sum_ffn,
        sum_table,
        grad_head,
        sum_reduce,
        sum_spatial,
        sum_expand,
        sum_embed,
        sum_bn_gain,
        sum_bn_shift,
    )


def solution(mesh):
    placed = (
        P(("wide", "narrow"), None),
        P(("wide", "narrow"), None, None, None),
        P(("wide", "narrow"), None),
        P(("wide", "narrow"), None),
        P(("wide", "narrow"), None),
        P(("wide", "narrow"), None),
        P(("wide", "narrow"), None),
        P(("wide", "narrow"), None),
        P(("wide", "narrow")),
        P(("wide", "narrow")),
        P(("wide", "narrow")),
        P(("wide", "narrow")),
        P(None, ("wide", "narrow")),
        P(),
        P(("wide", "narrow"), None),
        P(("wide", "narrow"), None),
        P(("wide", "narrow"), None),
        P(("wide", "narrow"), None),
        P(("wide", "narrow")),
        P(("wide", "narrow")),
        P(("wide", "narrow"), None),
    )
    return jax.shard_map(
        local,
        mesh=mesh,
        in_specs=placed,
        out_specs=(
            P(("wide", "narrow"), None),
            P(("wide", "narrow"), None),
            P(("wide", "narrow"), None, None, None),
            P("wide", "narrow"),
            P(("wide", "narrow"), None),
            P("wide", "narrow"),
            P("narrow", "wide"),
            P(("wide", "narrow")),
            P(("wide", "narrow")),
            P(("wide", "narrow")),
            P(("wide", "narrow")),
            P(None, ("wide", "narrow")),
            P(),
            P(("wide", "narrow"), None),
            P(("wide", "narrow"), None),
            P(("wide", "narrow"), None),
            P(("wide", "narrow"), None),
            P(("wide", "narrow")),
            P(("wide", "narrow")),
        ),
        check_vma=False,
    )
```

```python
import functools

import jax
import jax.numpy as jnp
from jax import lax
from jax.experimental import pallas as pl
from jax.experimental.pallas import tpu as pltpu
from jax.sharding import PartitionSpec as P

D = 768
HEADS = 12
HDIM = 64
RSPAN = 128


epsilon = 1e-05


def product(lhs_matrix, rhs_matrix):
    return jnp.dot(lhs_matrix, rhs_matrix, preferred_element_type=jnp.float32)


def product_tn(lhs_matrix, rhs_matrix):
    return lax.dot_general(
        lhs_matrix, rhs_matrix, (((0,), (0,)), ((), ())), preferred_element_type=jnp.float32
    )


def product_nt(lhs_matrix, rhs_matrix):
    return lax.dot_general(
        lhs_matrix, rhs_matrix, (((1,), (1,)), ((), ())), preferred_element_type=jnp.float32
    )


def layer_norm(values, gain):
    average = jnp.mean(values, axis=-1, keepdims=True)
    centred = values - average
    inv_std = lax.rsqrt(jnp.mean(centred * centred, axis=-1, keepdims=True) + epsilon)
    unit_rows = centred * inv_std
    return (unit_rows * gain, unit_rows, inv_std)


def layer_norm_back(cotangent, unit_rows, inv_std, gain):
    weighted = cotangent * gain
    inner = (
        weighted
        - jnp.mean(weighted, axis=-1, keepdims=True)
        - unit_rows * jnp.mean(weighted * unit_rows, axis=-1, keepdims=True)
    )
    return (inv_std * inner, jnp.sum(cotangent * unit_rows, axis=0))


def smooth(values):
    return jax.nn.gelu(values, approximate=True)


def smooth_back(values, cotangent):
    unused, pullback = jax.vjp(smooth, values)
    return pullback(cotangent)[0]


def unfold(grid):
    side = grid.shape[1]
    padded = jnp.pad(grid, ((0, 0), (1, 1), (1, 1), (0, 0)))
    pieces = [
        padded[:, row_off : row_off + side, col_off : col_off + side, :]
        for row_off in range(3)
        for col_off in range(3)
    ]
    return jnp.concatenate(pieces, axis=-1)


def fold(columns):
    channels = columns.shape[-1] // 9
    side = columns.shape[1]
    total = jnp.zeros((columns.shape[0], side + 2, side + 2, channels), jnp.float32)
    for row_off in range(3):
        for col_off in range(3):
            which = row_off * 3 + col_off
            piece = columns[..., which * channels : (which + 1) * channels]
            total = total + jnp.pad(
                piece, ((0, 0), (row_off, 2 - row_off), (col_off, 2 - col_off), (0, 0))
            )
    return total[:, 1:-1, 1:-1, :]


PAIRS = HEADS // 2
BLK = 128
NEG = -1e30


def dot_nn(a, b):
    return lax.dot_general(a, b, (((1,), (0,)), ((), ())), preferred_element_type=jnp.float32)


def dot_nt(a, b):
    return lax.dot_general(a, b, (((1,), (1,)), ((), ())), preferred_element_type=jnp.float32)


def split_heads(pair, scale):
    lane = lax.broadcasted_iota(jnp.int32, pair.shape, 1)
    vals = pair * jnp.asarray(scale, pair.dtype)
    zero = jnp.zeros_like(vals)
    return jnp.concatenate([jnp.where(lane < HDIM, vals, zero), jnp.where(lane < HDIM, zero, vals)], axis=0)


def join_heads(both):
    row = lax.broadcasted_iota(jnp.int32, (2 * HDIM, BLK), 0)
    return jnp.where(row < HDIM, both[:, :BLK], both[:, BLK:])


def bias_strips(table):
    rev = jnp.flip(table.astype(jnp.float32), axis=1)
    first, last = rev[:, 255:256], rev[:, 0:1]
    below = jnp.concatenate([jnp.broadcast_to(first, (HEADS, 129)), rev[:, 128:255]], axis=1)
    middle = jnp.concatenate([rev[:, 127:256], rev[:, 0:127]], axis=1)
    above = jnp.concatenate([last, rev[:, 0:127], jnp.broadcast_to(last, (HEADS, 128))], axis=1)
    low = jnp.broadcast_to(first, (HEADS, 256))
    high = jnp.broadcast_to(last, (HEADS, 256))
    return jnp.stack([low, below, middle, above, high], axis=1)


def table_from_strips(sums):
    low, below, middle, above, high = (sums[:, i] for i in range(5))
    total = jnp.concatenate([middle[:, 129:256], middle[:, 0:129]], axis=1)
    zero = jnp.zeros((HEADS, 127), jnp.float32)
    first = jnp.sum(low, axis=1, keepdims=True) + jnp.sum(below[:, :129], axis=1, keepdims=True)
    last = jnp.sum(high, axis=1, keepdims=True) + above[:, 0:1] + jnp.sum(above[:, 128:], axis=1, keepdims=True)
    total = total + jnp.concatenate([jnp.zeros((HEADS, 128), jnp.float32), below[:, 129:], first], axis=1)
    head = jnp.concatenate([above[:, 1:128], jnp.zeros((HEADS, 129), jnp.float32)], axis=1)
    total = total + head + jnp.concatenate([last, jnp.zeros((HEADS, 255), jnp.float32)], axis=1)
    return jnp.flip(total, axis=1)


def windows(segments):
    seg = segments.reshape(-1)
    starts = seg[::BLK]
    ends = seg[BLK - 1 :: BLK]
    low = jnp.sum((seg[None, :] < starts[:, None]).astype(jnp.int32), axis=1) // BLK
    high = (jnp.sum((seg[None, :] <= ends[:, None]).astype(jnp.int32), axis=1) + BLK - 1) // BLK
    return jnp.stack([low, high])


def attend_kernel(win, packed, segk, segq, strips, out, logsum, bias, vt, qm, acc, stat):
    i = pl.program_id(0)

    @pl.when(i == 0)
    def _():
        for hp in range(PAIRS):
            vt[pl.ds(hp * 128, 128), :] = packed[:, pl.ds(2 * D + hp * 128, 128)].T
            for d in range(5):
                for half in range(2):
                    row = strips[2 * hp + half, pl.ds(d, 1), :]
                    tile = jnp.broadcast_to(row, (BLK, 256))
                    if 0 < d < 4:
                        tile = pltpu.roll(tile, 0, 1, stride=1, stride_axis=0)
                    bias[hp, d, :, pl.ds(half * BLK, BLK)] = tile[:, :BLK]

    rows = pl.ds(pl.multiple_of(i * BLK, BLK), BLK)
    for hp in range(PAIRS):
        qm[hp] = split_heads(packed[rows, pl.ds(hp * 128, 128)], HDIM ** -0.5)
        acc[hp] = jnp.zeros((128, 256), jnp.float32)
        stat[hp, 0] = jnp.full((1, 256), NEG, jnp.float32)
        stat[hp, 1] = jnp.zeros((1, 256), jnp.float32)
    sq = segq[:, rows]
    sq2 = jnp.concatenate([sq, sq], axis=1)

    def body(kb, carry):
        keys = pl.ds(pl.multiple_of(kb * BLK, BLK), BLK)
        allowed = segk[keys, :] == sq2
        d = jnp.clip(kb - i, -2, 2) + 2
        for hp in range(PAIRS):
            s = dot_nt(packed[keys, pl.ds(D + hp * 128, 128)], qm[hp])
            s = jnp.where(allowed, s + bias[hp, d], NEG)
            old = stat[hp, 0]
            new = jnp.maximum(old, jnp.max(s, axis=0, keepdims=True))
            p = jnp.exp(s - new)
            alpha = jnp.exp(old - new)
            stat[hp, 0] = new
            stat[hp, 1] = stat[hp, 1] * alpha + jnp.sum(p, axis=0, keepdims=True)
            acc[hp] = acc[hp] * alpha + dot_nn(vt[pl.ds(hp * 128, 128), keys], p.astype(jnp.bfloat16))
        return carry

    lax.fori_loop(win[0, i], win[1, i], body, 0)
    for hp in range(PAIRS):
        total = stat[hp, 1]
        out[:, pl.ds(hp * 128, 128)] = join_heads(acc[hp] / total).T
        logsum[0, pl.ds(hp, 1), :] = stat[hp, 0] + jnp.log(total)


def attend(packed, segments, strips, win):
    length = packed.shape[0]
    blocks = length // BLK
    seg = segments.reshape(1, length)
    whole = lambda shape: pl.BlockSpec(shape, lambda i, w: (0,) * len(shape))
    return pl.pallas_call(
        attend_kernel,
        out_shape=(
            jax.ShapeDtypeStruct((length, D), jnp.float32),
            jax.ShapeDtypeStruct((blocks, PAIRS, 256), jnp.float32),
            jax.ShapeDtypeStruct((PAIRS, 5, BLK, 256), jnp.float32),
        ),
        grid_spec=pltpu.PrefetchScalarGridSpec(
            num_scalar_prefetch=1,
            grid=(blocks,),
            in_specs=[whole((length, 3 * D)), whole((length, 1)), whole((1, length)), whole((HEADS, 5, 256))],
            out_specs=(
                pl.BlockSpec((BLK, D), lambda i, w: (i, 0)),
                pl.BlockSpec((1, PAIRS, 256), lambda i, w: (i, 0, 0)),
                whole((PAIRS, 5, BLK, 256)),
            ),
            scratch_shapes=[
                pltpu.VMEM((D, length), jnp.bfloat16),
                pltpu.VMEM((PAIRS, 256, 128), jnp.bfloat16),
                pltpu.VMEM((PAIRS, 128, 256), jnp.float32),
                pltpu.VMEM((PAIRS, 2, 1, 256), jnp.float32),
            ],
        ),
        compiler_params=pltpu.CompilerParams(vmem_limit_bytes=48 * 2**20),
        cost_estimate=pl.CostEstimate(flops=2 * 10**10, bytes_accessed=10**7, transcendentals=6 * 10**6),
        name="attend",
    )(win, packed, seg.reshape(length, 1), seg, strips)


def unskew(tile):
    row = lax.broadcasted_iota(jnp.int32, tile.shape, 0)
    width = tile.shape[1]
    for bit in range(7):
        step = 1 << bit
        tile = jnp.where((row & step) != 0, pltpu.roll(tile, width - step, 1), tile)
    return tile


def attend_back_kernel(win, packed, grads, attended, segk, segq, bias, logsum, out, tab, kt, qm, om, dqt, dk, dv, gt):
    i = pl.program_id(0)
    last = pl.num_programs(0) - 1

    @pl.when(i == 0)
    def _():
        for hp in range(PAIRS):
            kt[pl.ds(hp * 128, 128), :] = packed[:, pl.ds(D + hp * 128, 128)].T
        dk[...] = jnp.zeros_like(dk)
        dv[...] = jnp.zeros_like(dv)
        gt[...] = jnp.zeros_like(gt)

    rows = pl.ds(pl.multiple_of(i * BLK, BLK), BLK)
    dots = []
    for hp in range(PAIRS):
        cols = pl.ds(hp * 128, 128)
        qm[hp] = split_heads(packed[rows, cols], HDIM ** -0.5)
        om[hp] = split_heads(grads[:, cols], 1.0)
        cross = (grads[:, cols].astype(jnp.float32) * attended[:, cols]).T
        dots.append(jnp.concatenate([
            jnp.sum(cross[:HDIM], axis=0, keepdims=True),
            jnp.sum(cross[HDIM:], axis=0, keepdims=True)], axis=1))
        dqt[hp] = jnp.zeros((128, 256), jnp.float32)
    sq = segq[:, rows]
    sq2 = jnp.concatenate([sq, sq], axis=1)

    def body(kb, carry):
        keys = pl.ds(pl.multiple_of(kb * BLK, BLK), BLK)
        allowed = segk[keys, :] == sq2
        d = jnp.clip(kb - i, -2, 2) + 2
        for hp in range(PAIRS):
            cols = pl.ds(hp * 128, 128)
            s = dot_nt(packed[keys, pl.ds(D + hp * 128, 128)], qm[hp]) + bias[hp, d]
            p = jnp.exp(jnp.where(allowed, s, NEG) - logsum[0, pl.ds(hp, 1), :])
            dp = dot_nt(packed[keys, pl.ds(2 * D + hp * 128, 128)], om[hp])
            ds = p * (dp - dots[hp])
            gt[hp, d] += ds
            low = ds.astype(jnp.bfloat16)
            dv[keys, cols] += dot_nn(p.astype(jnp.bfloat16), om[hp])
            dk[keys, cols] += dot_nn(low, qm[hp])
            dqt[hp] += dot_nn(kt[cols, keys], low)
        return carry

    lax.fori_loop(win[0, i], win[1, i], body, 0)
    for hp in range(PAIRS):
        out[rows, pl.ds(hp * 128, 128)] = (join_heads(dqt[hp]).T * (HDIM ** -0.5)).astype(jnp.bfloat16)

    @pl.when(i == last)
    def _():
        out[:, pl.ds(D, D)] = dk[...].astype(jnp.bfloat16)
        out[:, pl.ds(2 * D, D)] = dv[...].astype(jnp.bfloat16)
        for hp in range(PAIRS):
            for half in range(2):
                for d in range(5):
                    tile = gt[hp, d, :, pl.ds(half * BLK, BLK)]
                    tile = jnp.concatenate([tile, jnp.zeros_like(tile)], axis=1)
                    if 0 < d < 4:
                        tile = unskew(tile)
                    tab[2 * hp + half, pl.ds(d, 1), :] = jnp.sum(tile, axis=0, keepdims=True)


def attend_back(packed, grads, attended, segments, bias, logsum, win):
    length = packed.shape[0]
    blocks = length // BLK
    seg = segments.reshape(1, length)
    whole = lambda shape: pl.BlockSpec(shape, lambda i, w: (0,) * len(shape))
    return pl.pallas_call(
        attend_back_kernel,
        out_shape=(
            jax.ShapeDtypeStruct((length, 3 * D), jnp.bfloat16),
            jax.ShapeDtypeStruct((HEADS, 5, 256), jnp.float32),
        ),
        grid_spec=pltpu.PrefetchScalarGridSpec(
            num_scalar_prefetch=1,
            grid=(blocks,),
            in_specs=[
                whole((length, 3 * D)),
                pl.BlockSpec((BLK, D), lambda i, w: (i, 0)),
                pl.BlockSpec((BLK, D), lambda i, w: (i, 0)),
                whole((length, 1)),
                whole((1, length)),
                whole((PAIRS, 5, BLK, 256)),
                pl.BlockSpec((1, PAIRS, 256), lambda i, w: (i, 0, 0)),
            ],
            out_specs=(whole((length, 3 * D)), whole((HEADS, 5, 256))),
            scratch_shapes=[
                pltpu.VMEM((D, length), jnp.bfloat16),
                pltpu.VMEM((PAIRS, 256, 128), jnp.bfloat16),
                pltpu.VMEM((PAIRS, 256, 128), jnp.bfloat16),
                pltpu.VMEM((PAIRS, 128, 256), jnp.float32),
                pltpu.VMEM((length, D), jnp.float32),
                pltpu.VMEM((length, D), jnp.float32),
                pltpu.VMEM((PAIRS, 5, BLK, 256), jnp.float32),
            ],
        ),
        compiler_params=pltpu.CompilerParams(vmem_limit_bytes=56 * 2**20),
        cost_estimate=pl.CostEstimate(flops=5 * 10**10, bytes_accessed=2 * 10**7, transcendentals=6 * 10**6),
        name="attend_back",
    )(win, packed, grads, attended, seg.reshape(length, 1), seg, bias, logsum)


MESH = pl.DeviceIdType.MESH


class Place:
    def __init__(self, lines, rows):
        self.lines, self.rows = lines, rows
        wide, narrow = lax.axis_index("wide"), lax.axis_index("narrow")
        self.line, self.side = wide // 2, wide % 2
        self.row, self.core = narrow // 2, narrow % 2

    def device(self, line=None, side=None, row=None, core=None):
        line = self.line if line is None else line
        side = self.side if side is None else side
        row = self.row if row is None else row
        core = self.core if core is None else core
        return (line * 2 + side, row * 2 + core)

    def line_peer(self, k):
        return lax.rem(self.line + k, self.lines)

    def line_source(self, k):
        return lax.rem(self.line + self.lines - k, self.lines)

    def row_peer(self, k):
        return lax.rem(self.row + k, self.rows)

    def row_source(self, k):
        return lax.rem(self.row + self.rows - k, self.rows)

    def greet(self):
        barrier = pltpu.get_barrier_semaphore()
        targets = [self.device(line=self.line_peer(k)) for k in range(1, self.lines)]
        targets += [self.device(row=self.row_peer(k)) for k in range(1, self.rows)]
        targets += [self.device(side=1 - self.side), self.device(core=1 - self.core)]
        for target in targets:
            pl.semaphore_signal(barrier, inc=1, device_id=target, device_id_type=MESH)
        pl.semaphore_wait(barrier, len(targets))


class Sends:
    def __init__(self, send_sems, recv_sems):
        self.send_sems, self.recv_sems, self.used = send_sems, recv_sems, 0
        self.started = []

    def start(self, src, dst, device):
        copy = pltpu.make_async_remote_copy(
            src_ref=src, dst_ref=dst, send_sem=self.send_sems.at[self.used], recv_sem=self.recv_sems.at[self.used],
            device_id=device, device_id_type=MESH)
        copy.start()
        self.used += 1
        self.started.append(copy)
        return copy

    def finish(self):
        for copy in self.started:
            copy.wait_send()


def gather_copies(lines, rows):
    return (lines - 1) + 1 + (rows - 1) + (rows - 1) + 1 + 1 + rows + rows


class Gather:
    def __init__(self, place, sends, shard, out, local_sem):
        self.p, self.s, self.shard, self.out = place, sends, shard, out
        self.local_sem = local_sem
        cols = out.shape[-1]
        cut = cols // 256 * 128
        self.low, self.high = pl.ds(0, cut), pl.ds(cut, cols - cut)
        self.cores = []

    def begin(self):
        p = self.p
        mine = self.out.at[p.line, p.side, p.row, p.core]
        self.local = pltpu.make_async_copy(self.shard, mine, self.local_sem)
        self.local.start()
        self.stage = [self.s.start(self.shard, mine, p.device(line=p.line_peer(k))) for k in range(1, p.lines)]

    def across(self, src):
        self.cores.append(self.s.start(src, src, self.p.device(core=1 - self.p.core)))

    def second(self):
        p, out = self.p, self.out
        self.local.wait()
        for copy in self.stage:
            copy.wait_recv()
        low = out.at[:, p.side, p.row, p.core, :, self.low]
        high = out.at[:, p.side, p.row, p.core, :, self.high]
        self.stage = [self.s.start(low, low, p.device(side=1 - p.side))]
        self.stage += [self.s.start(high, high, p.device(row=p.row_peer(k))) for k in range(1, p.rows)]
        self.across(out.at[:, p.side, p.row, p.core])

    def third(self):
        p, out = self.p, self.out
        for copy in self.stage:
            copy.wait_recv()
        low = out.at[:, :, p.row, p.core, :, self.low]
        high = out.at[:, p.side, :, p.core, :, self.high]
        self.stage = [self.s.start(high, high, p.device(side=1 - p.side))]
        self.stage += [self.s.start(low, low, p.device(row=p.row_peer(k))) for k in range(1, p.rows)]
        self.across(out.at[:, 1 - p.side, p.row, p.core, :, self.low])
        for k in range(1, p.rows):
            self.across(out.at[:, p.side, p.row_source(k), p.core, :, self.high])

    def fourth(self):
        p, out = self.p, self.out
        for copy in self.stage:
            copy.wait_recv()
        for k in range(1, p.rows):
            self.across(out.at[:, :, p.row_source(k), p.core, :, self.low])
        self.across(out.at[:, 1 - p.side, :, p.core, :, self.high])

    def last(self):
        for copy in self.cores:
            copy.wait_recv()


def gather_kernel(count, lines, rows, *refs):
    shards, outs = refs[:count], refs[count : 2 * count]
    send_sems, recv_sems, local_sems = refs[2 * count :]
    place = Place(lines, rows)
    place.greet()
    sends = Sends(send_sems, recv_sems)
    parts = [Gather(place, sends, shards[i], outs[i], local_sems.at[i]) for i in range(count)]
    for part in parts:
        part.begin()
    for i in range(count + 3):
        for lag, step in ((0, "second"), (1, "third"), (2, "fourth"), (3, "last")):
            if 0 <= i - lag < count:
                getattr(parts[i - lag], step)()
    sends.finish()


def gather_all(shards, collective_id):
    wide, narrow = lax.axis_size("wide"), lax.axis_size("narrow")
    lines, rows = wide // 2, narrow // 2
    count = len(shards)
    copies = count * gather_copies(lines, rows)
    outs = pl.pallas_call(
        functools.partial(gather_kernel, count, lines, rows),
        out_shape=[jax.ShapeDtypeStruct((lines, 2, rows, 2) + s.shape, s.dtype) for s in shards],
        in_specs=[pl.BlockSpec(memory_space=pl.ANY)] * count,
        out_specs=[pl.BlockSpec(memory_space=pl.ANY)] * count,
        scratch_shapes=[pltpu.SemaphoreType.DMA((copies,)), pltpu.SemaphoreType.DMA((copies,)), pltpu.SemaphoreType.DMA((count,))],
        compiler_params=pltpu.CompilerParams(collective_id=collective_id, has_side_effects=True),
        cost_estimate=pl.CostEstimate(flops=0, bytes_accessed=4 * 10**7, transcendentals=0),
        name="gather_weights",
    )(*shards)
    return outs


def scatter_copies(lines, rows):
    return 1 + (rows - 1) + 1 + 1 + (rows - 1) + (lines - 1)


def add_loop(lead, fn):
    total = 1
    for size in lead:
        total *= size

    def body(i, carry):
        index = []
        for size in reversed(lead):
            index.append(lax.rem(i, size))
            i = i // size
        fn(tuple(reversed(index)))
        return carry

    lax.fori_loop(0, total, body, 0)


def plus(*terms):
    total = terms[0].astype(jnp.float32)
    for term in terms[1:]:
        total = total + term.astype(jnp.float32)
    return total


class Scatter:
    def __init__(self, place, sends, grad, out, buffers, local_sem):
        self.p, self.s, self.grad, self.out, self.local_sem = place, sends, grad, out, local_sem
        self.own, self.other, self.low1, self.high1, self.low2, self.high2, self.line0, self.lines_in = buffers
        cols = grad.shape[-1]
        cut = cols // 256 * 128
        self.low, self.high = pl.ds(0, cut), pl.ds(cut, cols - cut)

    def begin(self):
        p = self.p
        self.local = pltpu.make_async_copy(self.grad.at[:, :, :, p.core], self.own, self.local_sem)
        self.local.start()
        self.stage = [self.s.start(self.grad.at[:, :, :, 1 - p.core], self.other, p.device(core=1 - p.core))]

    def second(self):
        p, own = self.p, self.own
        self.local.wait()
        for copy in self.stage:
            copy.wait_recv()

        def add(i):
            own[i] = plus(own[i], self.other[i]).astype(own.dtype)

        add_loop(own.shape[:3], add)
        self.stage = [self.s.start(own.at[:, 1 - p.side, :, :, self.high], self.high1, p.device(side=1 - p.side))]
        for k in range(1, p.rows):
            to = p.row_peer(k)
            self.stage.append(self.s.start(own.at[:, :, to, :, self.low], self.low1.at[k - 1], p.device(row=to)))

    def third(self):
        p, own = self.p, self.own
        for copy in self.stage:
            copy.wait_recv()

        def add_low(i):
            l, x = i
            terms = [own[l, x, p.row, :, self.low]] + [self.low1[k, l, x] for k in range(p.rows - 1)]
            own[l, x, p.row, :, self.low] = plus(*terms).astype(own.dtype)

        def add_high(i):
            l, y = i
            own[l, p.side, y, :, self.high] = plus(own[l, p.side, y, :, self.high], self.high1[l, y]).astype(own.dtype)

        add_loop((p.lines, 2), add_low)
        add_loop((p.lines, p.rows), add_high)
        self.stage = [self.s.start(own.at[:, 1 - p.side, p.row, :, self.low], self.low2, p.device(side=1 - p.side))]
        for k in range(1, p.rows):
            to = p.row_peer(k)
            self.stage.append(self.s.start(own.at[:, p.side, to, :, self.high], self.high2.at[k - 1], p.device(row=to)))

    def fourth(self):
        p, own = self.p, self.own
        for copy in self.stage:
            copy.wait_recv()

        def add(i):
            (l,) = i
            self.line0[l, :, self.low] = plus(own[l, p.side, p.row, :, self.low], self.low2[l]).astype(own.dtype)
            terms = [own[l, p.side, p.row, :, self.high]] + [self.high2[k, l] for k in range(p.rows - 1)]
            self.line0[l, :, self.high] = plus(*terms).astype(own.dtype)

        add_loop((p.lines,), add)
        self.stage = []
        for k in range(1, p.lines):
            to = p.line_peer(k)
            self.stage.append(self.s.start(self.line0.at[to], self.lines_in.at[k - 1], p.device(line=to)))

    def last(self):
        p = self.p
        for copy in self.stage:
            copy.wait_recv()
        self.out[...] = plus(self.line0[p.line], *[self.lines_in[k] for k in range(p.lines - 1)])


def scatter_buffers(lines, rows, r, c, dtype):
    low = c // 256 * 128
    high = c - low
    return [
        pltpu.VMEM((lines, 2, rows, r, c), dtype),
        pltpu.VMEM((lines, 2, rows, r, c), dtype),
        pltpu.VMEM((max(rows - 1, 1), lines, 2, r, low), dtype),
        pltpu.VMEM((lines, rows, r, high), dtype),
        pltpu.VMEM((lines, r, low), dtype),
        pltpu.VMEM((max(rows - 1, 1), lines, r, high), dtype),
        pltpu.VMEM((lines, r, c), dtype),
        pltpu.VMEM((max(lines - 1, 1), r, c), dtype),
    ]


def scatter_kernel(count, lines, rows, *refs):
    grads, outs = refs[:count], refs[count : 2 * count]
    buffers = refs[2 * count : 2 * count + 8 * count]
    send_sems, recv_sems, local_sems = refs[10 * count :]
    place = Place(lines, rows)
    place.greet()
    sends = Sends(send_sems, recv_sems)
    parts = [Scatter(place, sends, grads[i], outs[i], buffers[8 * i : 8 * i + 8], local_sems.at[i]) for i in range(count)]
    for part in parts:
        part.begin()
    for i in range(count + 3):
        for lag, step in ((0, "second"), (1, "third"), (2, "fourth"), (3, "last")):
            if 0 <= i - lag < count:
                getattr(parts[i - lag], step)()
    sends.finish()


def scatter_all(grads, collective_id):
    wide, narrow = lax.axis_size("wide"), lax.axis_size("narrow")
    lines, rows = wide // 2, narrow // 2
    count = len(grads)
    copies = count * scatter_copies(lines, rows)
    buffers = []
    for g in grads:
        buffers += scatter_buffers(lines, rows, g.shape[-2], g.shape[-1], g.dtype)
    return pl.pallas_call(
        functools.partial(scatter_kernel, count, lines, rows),
        out_shape=[jax.ShapeDtypeStruct(g.shape[-2:], jnp.float32) for g in grads],
        in_specs=[pl.BlockSpec(memory_space=pl.ANY)] * count,
        out_specs=[pl.BlockSpec(memory_space=pltpu.VMEM)] * count,
        scratch_shapes=buffers + [pltpu.SemaphoreType.DMA((copies,)), pltpu.SemaphoreType.DMA((copies,)), pltpu.SemaphoreType.DMA((count,))],
        compiler_params=pltpu.CompilerParams(collective_id=collective_id, has_side_effects=True, vmem_limit_bytes=60 * 2**20),
        cost_estimate=pl.CostEstimate(flops=0, bytes_accessed=4 * 10**7, transcendentals=0),
        name="scatter_grads",
    )(*grads)


def total_kernel(lines, rows, x_ref, o_ref, core_in, plane, line_in, send_sems, recv_sems):
    p = Place(lines, rows)
    barrier = pltpu.get_barrier_semaphore()
    plane_peers = [(k // rows, k % rows) for k in range(1, 2 * rows)]
    targets = [p.device(core=1 - p.core)]
    targets += [p.device(side=lax.rem(p.side + a, 2), row=p.row_peer(b)) for a, b in plane_peers]
    targets += [p.device(line=p.line_peer(k)) for k in range(1, lines)]
    for target in targets:
        pl.semaphore_signal(barrier, inc=1, device_id=target, device_id_type=MESH)
    pl.semaphore_wait(barrier, len(targets))
    sends = Sends(send_sems, recv_sems)
    sends.start(x_ref, core_in, targets[0]).wait_recv()
    here = p.side * rows + p.row
    plane[here] = x_ref[...] + core_in[...]
    stage = [sends.start(plane.at[here], plane.at[here], t) for t in targets[1 : 2 * rows]]
    for copy in stage:
        copy.wait_recv()
    total = plane[0]
    for k in range(1, 2 * rows):
        total = total + plane[k]
    line_in[p.line] = total
    stage = [sends.start(line_in.at[p.line], line_in.at[p.line], t) for t in targets[2 * rows :]]
    for copy in stage:
        copy.wait_recv()
    total = line_in[0]
    for k in range(1, lines):
        total = total + line_in[k]
    o_ref[...] = total
    sends.finish()


def total_sum(x, collective_id):
    wide, narrow = lax.axis_size("wide"), lax.axis_size("narrow")
    lines, rows = wide // 2, narrow // 2
    copies = 1 + 2 * rows - 1 + lines - 1
    return pl.pallas_call(
        functools.partial(total_kernel, lines, rows),
        out_shape=jax.ShapeDtypeStruct(x.shape, x.dtype),
        in_specs=[pl.BlockSpec(memory_space=pltpu.VMEM)],
        out_specs=pl.BlockSpec(memory_space=pltpu.VMEM),
        scratch_shapes=[
            pltpu.VMEM(x.shape, x.dtype),
            pltpu.VMEM((2 * rows,) + x.shape, x.dtype),
            pltpu.VMEM((lines,) + x.shape, x.dtype),
            pltpu.SemaphoreType.DMA((copies,)),
            pltpu.SemaphoreType.DMA((copies,)),
        ],
        compiler_params=pltpu.CompilerParams(collective_id=collective_id, has_side_effects=True),
        cost_estimate=pl.CostEstimate(flops=0, bytes_accessed=10**6, transcendentals=0),
        name="total_sum",
    )(x)


def local(
    tokens,
    features,
    segments,
    positions,
    w_qkv,
    w_out,
    w_up,
    w_down,
    gain_pre,
    gain_attn,
    gain_mid,
    gain_ffn,
    rel_table,
    head_scale,
    w_reduce,
    w_spatial,
    w_expand,
    w_embed,
    bn_gain,
    bn_shift,
    d_out,
):
    both = ("wide", "narrow")
    devices = lax.axis_size(both)
    me = lax.axis_index("wide") * lax.axis_size("narrow") + lax.axis_index("narrow")
    vectors = (gain_pre, gain_attn, gain_mid, gain_ffn, bn_gain, bn_shift, rel_table.reshape(-1))
    held = jnp.concatenate(vectors)
    held = jnp.pad(held, (0, 16 * 256 - held.shape[0])).reshape(16, 256)
    gathered = gather_all([held, w_reduce, w_spatial, w_expand, w_embed, w_qkv, w_out, w_up, w_down], 1)
    full_held = gathered[0].reshape(devices, -1)
    full_reduce, full_spatial, full_expand, full_embed, full_qkv, full_out, full_up, full_down = (
        item.reshape(-1, item.shape[-1]) for item in gathered[1:]
    )
    full_vectors, at = [], 0
    for item in vectors:
        full_vectors.append(full_held[:, at : at + item.shape[0]])
        at += item.shape[0]
    full_pre, full_attn, full_mid, full_ffn, full_bn_gain, full_bn_shift = (
        item.reshape(-1) for item in full_vectors[:6]
    )
    full_table = full_vectors[6].reshape(devices, HEADS, -1).transpose(1, 0, 2).reshape(HEADS, -1)
    rows, length = (segments.shape[0], segments.shape[1])
    images, side = (features.shape[0], features.shape[1])
    patch_count = images * side * side
    whole = patch_count * lax.axis_size(("wide", "narrow"))
    stem_in = features.reshape(patch_count, features.shape[3])
    pre_first = product(stem_in, full_reduce)
    first = smooth(pre_first).astype(jnp.bfloat16)
    columns = unfold(first.reshape(images, side, side, first.shape[1])).reshape(
        patch_count, 9 * first.shape[1]
    )
    pre_second = product(columns, full_spatial)
    second = smooth(pre_second).astype(jnp.bfloat16)
    third = product(second, full_expand)
    sums = jnp.concatenate([jnp.sum(third, axis=0), jnp.sum(third * third, axis=0)])
    bn_total, bn_squares = jnp.split(total_sum(sums.reshape(16, -1), 3).reshape(-1), 2)
    bn_mean = bn_total / whole
    bn_inv = lax.rsqrt(bn_squares / whole - bn_mean * bn_mean + epsilon)
    bn_unit = (third - bn_mean) * bn_inv
    pre_joined = (
        bn_unit * full_bn_gain.astype(jnp.float32)
        + full_bn_shift.astype(jnp.float32)
        + stem_in.astype(jnp.float32)
    )
    joined = smooth(pre_joined).astype(jnp.bfloat16)
    embedded = product(joined, full_embed).reshape(images, side * side, -1)
    row_index = jnp.arange(rows, dtype=jnp.int32)[:, None]
    start_rows = (
        tokens.astype(jnp.float32).reshape(rows, length, -1).at[row_index, positions].add(embedded)
    )
    start = start_rows.reshape(rows * length, -1)
    normed0, unit0, inv0 = layer_norm(start, full_pre.astype(jnp.float32))
    normed0_low = normed0.astype(jnp.bfloat16)
    packed = product(normed0_low, full_qkv).astype(jnp.bfloat16)
    win = windows(segments)
    attended, logsums, bias = attend(packed, segments, bias_strips(full_table), win)
    scale_row = jnp.repeat(head_scale, HDIM)[None, :]
    scaled = attended * scale_row
    mixed_in, unit1, inv1 = layer_norm(scaled, full_attn.astype(jnp.float32))
    mixed_low = mixed_in.astype(jnp.bfloat16)
    middle = start + product(mixed_low, full_out)
    normed2, unit2, inv2 = layer_norm(middle, full_mid.astype(jnp.float32))
    normed2_low = normed2.astype(jnp.bfloat16)
    pre_up = product(normed2_low, full_up)
    activ = smooth(pre_up)
    narrowed, unit3, inv3 = layer_norm(activ, full_ffn.astype(jnp.float32))
    narrowed_low = narrowed.astype(jnp.bfloat16)
    result = middle + product(narrowed_low, full_down)
    mixed = result.astype(jnp.bfloat16)
    grad_result = d_out.astype(jnp.float32)
    grad_narrowed = product_nt(d_out, full_down)
    grad_activ, grad_gain_ffn = layer_norm_back(
        grad_narrowed, unit3, inv3, full_ffn.astype(jnp.float32)
    )
    grad_pre_up = smooth_back(pre_up, grad_activ).astype(jnp.bfloat16)
    grad_w_down = product_tn(d_out, narrowed_low)
    grad_w_up = product_tn(normed2_low, grad_pre_up)
    grad_normed2 = product_nt(grad_pre_up, full_up)
    grad_mid_in, grad_gain_mid = layer_norm_back(
        grad_normed2, unit2, inv2, full_mid.astype(jnp.float32)
    )
    grad_middle = grad_result + grad_mid_in
    grad_branch = grad_middle.astype(jnp.bfloat16)
    grad_w_out = product_tn(mixed_low, grad_branch)
    grad_mixed_in = product_nt(grad_branch, full_out)
    grad_scaled, grad_gain_attn = layer_norm_back(
        grad_mixed_in, unit1, inv1, full_attn.astype(jnp.float32)
    )
    grad_head_local = jnp.sum(jnp.sum(grad_scaled * attended, axis=0).reshape(HEADS, HDIM), axis=1)
    grad_attended = (grad_scaled * scale_row).astype(jnp.bfloat16)
    grad_packed, grad_strips = attend_back(packed, grad_attended, attended, segments, bias, logsums, win)
    grad_table = table_from_strips(grad_strips)
    grad_w_qkv = product_tn(normed0_low, grad_packed)
    grad_normed0 = product_nt(grad_packed, full_qkv)
    grad_start_in, grad_gain_pre = layer_norm_back(
        grad_normed0, unit0, inv0, full_pre.astype(jnp.float32)
    )
    grad_tokens = grad_middle + grad_start_in
    grad_embedded = (
        grad_tokens.reshape(rows, length, -1)[row_index, positions]
        .reshape(patch_count, -1)
        .astype(jnp.bfloat16)
    )
    grad_w_embed = product_tn(joined, grad_embedded)
    grad_joined = product_nt(grad_embedded, full_embed)
    grad_pre_joined = smooth_back(pre_joined, grad_joined)
    grad_bn_shift = jnp.sum(grad_pre_joined, axis=0)
    grad_bn_gain = jnp.sum(grad_pre_joined * bn_unit, axis=0)
    smalls = (
        grad_gain_pre,
        grad_gain_attn,
        grad_gain_mid,
        grad_gain_ffn,
        grad_bn_gain,
        grad_bn_shift,
        grad_table.reshape(-1),
        grad_head_local,
    )
    small = jnp.concatenate(smalls)
    small = jnp.pad(small, (0, -small.shape[0] % 1024)).reshape(-1, 128)
    small = total_sum(small, 4).reshape(-1)
    totals, at = [], 0
    for item in smalls:
        totals.append(small[at : at + item.shape[0]])
        at += item.shape[0]
    sum_pre, sum_attn, sum_mid, sum_ffn, sum_bn_gain, sum_bn_shift = (
        lax.dynamic_slice_in_dim(item, me * (item.shape[0] // devices), item.shape[0] // devices)
        for item in totals[:6]
    )
    breadth = 2 * RSPAN // devices
    sum_table = lax.dynamic_slice_in_dim(totals[6].reshape(HEADS, -1), me * breadth, breadth, 1)
    grad_head = totals[7]
    bn_gain_row = full_bn_gain.astype(jnp.float32)
    grad_unit = grad_pre_joined * bn_gain_row
    sum_unit, sum_cross = totals[5] * bn_gain_row, totals[4] * bn_gain_row
    grad_third = (bn_inv * (grad_unit - sum_unit / whole - bn_unit * (sum_cross / whole))).astype(
        jnp.bfloat16
    )
    grad_w_expand = product_tn(second, grad_third)
    grad_second = product_nt(grad_third, full_expand)
    grad_pre_second = smooth_back(pre_second, grad_second).astype(jnp.bfloat16)
    grad_w_spatial = product_tn(columns, grad_pre_second)
    grad_columns = product_nt(grad_pre_second, full_spatial)
    grad_first = fold(grad_columns.reshape(images, side, side, -1)).reshape(patch_count, -1)
    grad_pre_first = smooth_back(pre_first, grad_first).astype(jnp.bfloat16)
    grad_w_reduce = product_tn(stem_in, grad_pre_first)
    grad_features = (grad_pre_joined + product_nt(grad_pre_first, full_reduce)).reshape(
        features.shape
    )
    lines, planes = lax.axis_size("wide") // 2, lax.axis_size("narrow") // 2

    def by_rows(grad):
        return grad.astype(jnp.bfloat16).reshape(lines, 2, planes, 2, -1, grad.shape[1])

    def by_blocks(grad):
        low = grad.astype(jnp.bfloat16).reshape(lines, 2, -1, planes, 2, grad.shape[1] // (2 * planes))
        return low.transpose(0, 1, 3, 4, 2, 5)

    def by_windows(grad):
        low = grad.astype(jnp.bfloat16).reshape(lines, 2, -1, planes, grad.shape[1] // planes)
        width = grad.shape[1] // (2 * planes)
        window = -(-width // 128) * 128
        span = 2 * width
        pieces = [low[..., :window], low[..., span - window :]]
        return jnp.stack(pieces, axis=4).transpose(0, 1, 3, 4, 2, 5)

    grads = [
        by_blocks(grad_w_down),
        by_blocks(grad_w_up),
        by_rows(grad_w_out),
        by_windows(grad_w_qkv),
        by_rows(grad_w_embed),
        by_rows(grad_w_expand),
        by_rows(grad_w_spatial),
        by_rows(grad_w_reduce),
    ]
    sum_down, sum_up, sum_out, sum_qkv, sum_embed, sum_expand, sum_spatial, sum_reduce = scatter_all(grads, 2)
    sum_down = sum_down.T
    width = 3 * D // (2 * planes)
    sum_qkv = jnp.where(
        lax.axis_index("narrow") % 2 == 0, sum_qkv[:, :width], sum_qkv[:, sum_qkv.shape[1] - width :]
    )
    return (
        mixed,
        grad_tokens,
        grad_features,
        sum_qkv,
        sum_out,
        sum_up,
        sum_down,
        sum_pre,
        sum_attn,
        sum_mid,
        sum_ffn,
        sum_table,
        grad_head,
        sum_reduce,
        sum_spatial,
        sum_expand,
        sum_embed,
        sum_bn_gain,
        sum_bn_shift,
    )


def solution(mesh):
    placed = (
        P(("wide", "narrow"), None),
        P(("wide", "narrow"), None, None, None),
        P(("wide", "narrow"), None),
        P(("wide", "narrow"), None),
        P(("wide", "narrow"), None),
        P(("wide", "narrow"), None),
        P(("wide", "narrow"), None),
        P(("wide", "narrow"), None),
        P(("wide", "narrow")),
        P(("wide", "narrow")),
        P(("wide", "narrow")),
        P(("wide", "narrow")),
        P(None, ("wide", "narrow")),
        P(),
        P(("wide", "narrow"), None),
        P(("wide", "narrow"), None),
        P(("wide", "narrow"), None),
        P(("wide", "narrow"), None),
        P(("wide", "narrow")),
        P(("wide", "narrow")),
        P(("wide", "narrow"), None),
    )
    return jax.shard_map(
        local,
        mesh=mesh,
        in_specs=placed,
        out_specs=(
            P(("wide", "narrow"), None),
            P(("wide", "narrow"), None),
            P(("wide", "narrow"), None, None, None),
            P("wide", "narrow"),
            P(("wide", "narrow"), None),
            P("wide", "narrow"),
            P("narrow", "wide"),
            P(("wide", "narrow")),
            P(("wide", "narrow")),
            P(("wide", "narrow")),
            P(("wide", "narrow")),
            P(None, ("wide", "narrow")),
            P(),
            P(("wide", "narrow"), None),
            P(("wide", "narrow"), None),
            P(("wide", "narrow"), None),
            P(("wide", "narrow"), None),
            P(("wide", "narrow")),
            P(("wide", "narrow")),
        ),
        check_vma=False,
    )
```

```python
import functools

import jax
import jax.numpy as jnp
from jax import lax
from jax.experimental import pallas as pl
from jax.experimental.pallas import tpu as pltpu
from jax.sharding import PartitionSpec as P

D = 768
HEADS = 12
HDIM = 64
RSPAN = 128


epsilon = 1e-05


def product(lhs_matrix, rhs_matrix):
    return jnp.dot(lhs_matrix, rhs_matrix, preferred_element_type=jnp.float32)


def product_tn(lhs_matrix, rhs_matrix):
    return lax.dot_general(
        lhs_matrix, rhs_matrix, (((0,), (0,)), ((), ())), preferred_element_type=jnp.float32
    )


def product_nt(lhs_matrix, rhs_matrix):
    return lax.dot_general(
        lhs_matrix, rhs_matrix, (((1,), (1,)), ((), ())), preferred_element_type=jnp.float32
    )


def layer_norm(values, gain):
    average = jnp.mean(values, axis=-1, keepdims=True)
    centred = values - average
    inv_std = lax.rsqrt(jnp.mean(centred * centred, axis=-1, keepdims=True) + epsilon)
    unit_rows = centred * inv_std
    return (unit_rows * gain, unit_rows, inv_std)


def layer_norm_back(cotangent, unit_rows, inv_std, gain):
    weighted = cotangent * gain
    inner = (
        weighted
        - jnp.mean(weighted, axis=-1, keepdims=True)
        - unit_rows * jnp.mean(weighted * unit_rows, axis=-1, keepdims=True)
    )
    return (inv_std * inner, jnp.sum(cotangent * unit_rows, axis=0))


def smooth(values):
    return jax.nn.gelu(values, approximate=True)


def smooth_back(values, cotangent):
    unused, pullback = jax.vjp(smooth, values)
    return pullback(cotangent)[0]


def unfold(grid):
    side = grid.shape[1]
    padded = jnp.pad(grid, ((0, 0), (1, 1), (1, 1), (0, 0)))
    pieces = [
        padded[:, row_off : row_off + side, col_off : col_off + side, :]
        for row_off in range(3)
        for col_off in range(3)
    ]
    return jnp.concatenate(pieces, axis=-1)


def fold(columns):
    channels = columns.shape[-1] // 9
    side = columns.shape[1]
    total = jnp.zeros((columns.shape[0], side + 2, side + 2, channels), jnp.float32)
    for row_off in range(3):
        for col_off in range(3):
            which = row_off * 3 + col_off
            piece = columns[..., which * channels : (which + 1) * channels]
            total = total + jnp.pad(
                piece, ((0, 0), (row_off, 2 - row_off), (col_off, 2 - col_off), (0, 0))
            )
    return total[:, 1:-1, 1:-1, :]


PAIRS = HEADS // 2
BLK = 128
NEG = -1e30


def dot_nn(a, b):
    return lax.dot_general(a, b, (((1,), (0,)), ((), ())), preferred_element_type=jnp.float32)


def dot_nt(a, b):
    return lax.dot_general(a, b, (((1,), (1,)), ((), ())), preferred_element_type=jnp.float32)


def split_heads(pair, scale):
    lane = lax.broadcasted_iota(jnp.int32, pair.shape, 1)
    vals = pair * jnp.asarray(scale, pair.dtype)
    zero = jnp.zeros_like(vals)
    return jnp.concatenate([jnp.where(lane < HDIM, vals, zero), jnp.where(lane < HDIM, zero, vals)], axis=0)


def join_heads(both):
    row = lax.broadcasted_iota(jnp.int32, (2 * HDIM, BLK), 0)
    return jnp.where(row < HDIM, both[:, :BLK], both[:, BLK:])


def bias_strips(table):
    rev = jnp.flip(table.astype(jnp.float32), axis=1)
    first, last = rev[:, 255:256], rev[:, 0:1]
    below = jnp.concatenate([jnp.broadcast_to(first, (HEADS, 129)), rev[:, 128:255]], axis=1)
    middle = jnp.concatenate([rev[:, 127:256], rev[:, 0:127]], axis=1)
    above = jnp.concatenate([last, rev[:, 0:127], jnp.broadcast_to(last, (HEADS, 128))], axis=1)
    low = jnp.broadcast_to(first, (HEADS, 256))
    high = jnp.broadcast_to(last, (HEADS, 256))
    return jnp.stack([low, below, middle, above, high], axis=1)


def table_from_strips(sums):
    low, below, middle, above, high = (sums[:, i] for i in range(5))
    total = jnp.concatenate([middle[:, 129:256], middle[:, 0:129]], axis=1)
    zero = jnp.zeros((HEADS, 127), jnp.float32)
    first = jnp.sum(low, axis=1, keepdims=True) + jnp.sum(below[:, :129], axis=1, keepdims=True)
    last = jnp.sum(high, axis=1, keepdims=True) + above[:, 0:1] + jnp.sum(above[:, 128:], axis=1, keepdims=True)
    total = total + jnp.concatenate([jnp.zeros((HEADS, 128), jnp.float32), below[:, 129:], first], axis=1)
    head = jnp.concatenate([above[:, 1:128], jnp.zeros((HEADS, 129), jnp.float32)], axis=1)
    total = total + head + jnp.concatenate([last, jnp.zeros((HEADS, 255), jnp.float32)], axis=1)
    return jnp.flip(total, axis=1)


def windows(segments):
    seg = segments.reshape(-1)
    starts = seg[::BLK]
    ends = seg[BLK - 1 :: BLK]
    low = jnp.sum((seg[None, :] < starts[:, None]).astype(jnp.int32), axis=1) // BLK
    high = (jnp.sum((seg[None, :] <= ends[:, None]).astype(jnp.int32), axis=1) + BLK - 1) // BLK
    return jnp.stack([low, high])


def attend_kernel(win, packed, segk, segq, strips, out, logsum, bias, vt, qm, acc, stat):
    i = pl.program_id(0)

    @pl.when(i == 0)
    def _():
        for hp in range(PAIRS):
            vt[pl.ds(hp * 128, 128), :] = packed[:, pl.ds(2 * D + hp * 128, 128)].T
            for d in range(5):
                for half in range(2):
                    row = strips[2 * hp + half, pl.ds(d, 1), :]
                    tile = jnp.broadcast_to(row, (BLK, 256))
                    if 0 < d < 4:
                        tile = pltpu.roll(tile, 0, 1, stride=1, stride_axis=0)
                    bias[hp, d, :, pl.ds(half * BLK, BLK)] = tile[:, :BLK]

    rows = pl.ds(pl.multiple_of(i * BLK, BLK), BLK)
    for hp in range(PAIRS):
        qm[hp] = split_heads(packed[rows, pl.ds(hp * 128, 128)], HDIM ** -0.5)
        acc[hp] = jnp.zeros((128, 256), jnp.float32)
        stat[hp, 0] = jnp.full((1, 256), NEG, jnp.float32)
        stat[hp, 1] = jnp.zeros((1, 256), jnp.float32)
    sq = segq[:, rows]
    sq2 = jnp.concatenate([sq, sq], axis=1)

    def body(kb, carry):
        keys = pl.ds(pl.multiple_of(kb * BLK, BLK), BLK)
        allowed = segk[keys, :] == sq2
        d = jnp.clip(kb - i, -2, 2) + 2
        for hp in range(PAIRS):
            s = dot_nt(packed[keys, pl.ds(D + hp * 128, 128)], qm[hp])
            s = jnp.where(allowed, s + bias[hp, d], NEG)
            old = stat[hp, 0]
            new = jnp.maximum(old, jnp.max(s, axis=0, keepdims=True))
            p = jnp.exp(s - new)
            alpha = jnp.exp(old - new)
            stat[hp, 0] = new
            stat[hp, 1] = stat[hp, 1] * alpha + jnp.sum(p, axis=0, keepdims=True)
            acc[hp] = acc[hp] * alpha + dot_nn(vt[pl.ds(hp * 128, 128), keys], p.astype(jnp.bfloat16))
        return carry

    lax.fori_loop(win[0, i], win[1, i], body, 0)
    for hp in range(PAIRS):
        total = stat[hp, 1]
        out[:, pl.ds(hp * 128, 128)] = join_heads(acc[hp] / total).T
        logsum[0, pl.ds(hp, 1), :] = stat[hp, 0] + jnp.log(total)


def attend(packed, segments, strips, win):
    length = packed.shape[0]
    blocks = length // BLK
    seg = segments.reshape(1, length)
    whole = lambda shape: pl.BlockSpec(shape, lambda i, w: (0,) * len(shape))
    return pl.pallas_call(
        attend_kernel,
        out_shape=(
            jax.ShapeDtypeStruct((length, D), jnp.float32),
            jax.ShapeDtypeStruct((blocks, PAIRS, 256), jnp.float32),
            jax.ShapeDtypeStruct((PAIRS, 5, BLK, 256), jnp.float32),
        ),
        grid_spec=pltpu.PrefetchScalarGridSpec(
            num_scalar_prefetch=1,
            grid=(blocks,),
            in_specs=[whole((length, 3 * D)), whole((length, 1)), whole((1, length)), whole((HEADS, 5, 256))],
            out_specs=(
                pl.BlockSpec((BLK, D), lambda i, w: (i, 0)),
                pl.BlockSpec((1, PAIRS, 256), lambda i, w: (i, 0, 0)),
                whole((PAIRS, 5, BLK, 256)),
            ),
            scratch_shapes=[
                pltpu.VMEM((D, length), jnp.bfloat16),
                pltpu.VMEM((PAIRS, 256, 128), jnp.bfloat16),
                pltpu.VMEM((PAIRS, 128, 256), jnp.float32),
                pltpu.VMEM((PAIRS, 2, 1, 256), jnp.float32),
            ],
        ),
        compiler_params=pltpu.CompilerParams(vmem_limit_bytes=48 * 2**20),
        cost_estimate=pl.CostEstimate(flops=2 * 10**10, bytes_accessed=10**7, transcendentals=6 * 10**6),
        name="attend",
    )(win, packed, seg.reshape(length, 1), seg, strips)


def unskew(tile):
    row = lax.broadcasted_iota(jnp.int32, tile.shape, 0)
    width = tile.shape[1]
    for bit in range(7):
        step = 1 << bit
        tile = jnp.where((row & step) != 0, pltpu.roll(tile, width - step, 1), tile)
    return tile


def attend_back_kernel(win, packed, grads, attended, segk, segq, bias, logsum, out, tab, kt, qm, om, dqt, dk, dv, gt):
    i = pl.program_id(0)
    last = pl.num_programs(0) - 1

    @pl.when(i == 0)
    def _():
        for hp in range(PAIRS):
            kt[pl.ds(hp * 128, 128), :] = packed[:, pl.ds(D + hp * 128, 128)].T
        dk[...] = jnp.zeros_like(dk)
        dv[...] = jnp.zeros_like(dv)
        gt[...] = jnp.zeros_like(gt)

    rows = pl.ds(pl.multiple_of(i * BLK, BLK), BLK)
    dots = []
    for hp in range(PAIRS):
        cols = pl.ds(hp * 128, 128)
        qm[hp] = split_heads(packed[rows, cols], HDIM ** -0.5)
        om[hp] = split_heads(grads[:, cols], 1.0)
        cross = (grads[:, cols].astype(jnp.float32) * attended[:, cols]).T
        dots.append(jnp.concatenate([
            jnp.sum(cross[:HDIM], axis=0, keepdims=True),
            jnp.sum(cross[HDIM:], axis=0, keepdims=True)], axis=1))
        dqt[hp] = jnp.zeros((128, 256), jnp.float32)
    sq = segq[:, rows]
    sq2 = jnp.concatenate([sq, sq], axis=1)

    def body(kb, carry):
        keys = pl.ds(pl.multiple_of(kb * BLK, BLK), BLK)
        allowed = segk[keys, :] == sq2
        d = jnp.clip(kb - i, -2, 2) + 2
        for hp in range(PAIRS):
            cols = pl.ds(hp * 128, 128)
            s = dot_nt(packed[keys, pl.ds(D + hp * 128, 128)], qm[hp]) + bias[hp, d]
            p = jnp.exp(jnp.where(allowed, s, NEG) - logsum[0, pl.ds(hp, 1), :])
            dp = dot_nt(packed[keys, pl.ds(2 * D + hp * 128, 128)], om[hp])
            ds = p * (dp - dots[hp])
            gt[hp, d] += ds
            low = ds.astype(jnp.bfloat16)
            dv[keys, cols] += dot_nn(p.astype(jnp.bfloat16), om[hp])
            dk[keys, cols] += dot_nn(low, qm[hp])
            dqt[hp] += dot_nn(kt[cols, keys], low)
        return carry

    lax.fori_loop(win[0, i], win[1, i], body, 0)
    for hp in range(PAIRS):
        out[rows, pl.ds(hp * 128, 128)] = (join_heads(dqt[hp]).T * (HDIM ** -0.5)).astype(jnp.bfloat16)

    @pl.when(i == last)
    def _():
        out[:, pl.ds(D, D)] = dk[...].astype(jnp.bfloat16)
        out[:, pl.ds(2 * D, D)] = dv[...].astype(jnp.bfloat16)
        for hp in range(PAIRS):
            for half in range(2):
                for d in range(5):
                    tile = gt[hp, d, :, pl.ds(half * BLK, BLK)]
                    tile = jnp.concatenate([tile, jnp.zeros_like(tile)], axis=1)
                    if 0 < d < 4:
                        tile = unskew(tile)
                    tab[2 * hp + half, pl.ds(d, 1), :] = jnp.sum(tile, axis=0, keepdims=True)


def attend_back(packed, grads, attended, segments, bias, logsum, win):
    length = packed.shape[0]
    blocks = length // BLK
    seg = segments.reshape(1, length)
    whole = lambda shape: pl.BlockSpec(shape, lambda i, w: (0,) * len(shape))
    return pl.pallas_call(
        attend_back_kernel,
        out_shape=(
            jax.ShapeDtypeStruct((length, 3 * D), jnp.bfloat16),
            jax.ShapeDtypeStruct((HEADS, 5, 256), jnp.float32),
        ),
        grid_spec=pltpu.PrefetchScalarGridSpec(
            num_scalar_prefetch=1,
            grid=(blocks,),
            in_specs=[
                whole((length, 3 * D)),
                pl.BlockSpec((BLK, D), lambda i, w: (i, 0)),
                pl.BlockSpec((BLK, D), lambda i, w: (i, 0)),
                whole((length, 1)),
                whole((1, length)),
                whole((PAIRS, 5, BLK, 256)),
                pl.BlockSpec((1, PAIRS, 256), lambda i, w: (i, 0, 0)),
            ],
            out_specs=(whole((length, 3 * D)), whole((HEADS, 5, 256))),
            scratch_shapes=[
                pltpu.VMEM((D, length), jnp.bfloat16),
                pltpu.VMEM((PAIRS, 256, 128), jnp.bfloat16),
                pltpu.VMEM((PAIRS, 256, 128), jnp.bfloat16),
                pltpu.VMEM((PAIRS, 128, 256), jnp.float32),
                pltpu.VMEM((length, D), jnp.float32),
                pltpu.VMEM((length, D), jnp.float32),
                pltpu.VMEM((PAIRS, 5, BLK, 256), jnp.float32),
            ],
        ),
        compiler_params=pltpu.CompilerParams(vmem_limit_bytes=56 * 2**20),
        cost_estimate=pl.CostEstimate(flops=5 * 10**10, bytes_accessed=2 * 10**7, transcendentals=6 * 10**6),
        name="attend_back",
    )(win, packed, grads, attended, seg.reshape(length, 1), seg, bias, logsum)


MESH = pl.DeviceIdType.MESH


class Place:
    def __init__(self, lines, rows):
        self.lines, self.rows = lines, rows
        wide, narrow = lax.axis_index("wide"), lax.axis_index("narrow")
        self.line, self.side = wide // 2, wide % 2
        self.row, self.core = narrow // 2, narrow % 2

    def device(self, line=None, side=None, row=None, core=None):
        line = self.line if line is None else line
        side = self.side if side is None else side
        row = self.row if row is None else row
        core = self.core if core is None else core
        return (line * 2 + side, row * 2 + core)

    def line_peer(self, k):
        return lax.rem(self.line + k, self.lines)

    def line_source(self, k):
        return lax.rem(self.line + self.lines - k, self.lines)

    def row_peer(self, k):
        return lax.rem(self.row + k, self.rows)

    def row_source(self, k):
        return lax.rem(self.row + self.rows - k, self.rows)

    def greet(self):
        barrier = pltpu.get_barrier_semaphore()
        targets = [self.device(line=self.line_peer(k)) for k in range(1, self.lines)]
        targets += [self.device(row=self.row_peer(k)) for k in range(1, self.rows)]
        targets += [self.device(side=1 - self.side), self.device(core=1 - self.core)]
        for target in targets:
            pl.semaphore_signal(barrier, inc=1, device_id=target, device_id_type=MESH)
        pl.semaphore_wait(barrier, len(targets))


class Sends:
    def __init__(self, send_sems, recv_sems):
        self.send_sems, self.recv_sems, self.used = send_sems, recv_sems, 0
        self.started = []

    def start(self, src, dst, device):
        copy = pltpu.make_async_remote_copy(
            src_ref=src, dst_ref=dst, send_sem=self.send_sems.at[self.used], recv_sem=self.recv_sems.at[self.used],
            device_id=device, device_id_type=MESH)
        copy.start()
        self.used += 1
        self.started.append(copy)
        return copy

    def finish(self):
        for copy in self.started:
            copy.wait_send()


def gather_copies(lines, rows):
    return (lines - 1) + 1 + (rows - 1) + (rows - 1) + 1 + 1 + rows + rows


class Gather:
    def __init__(self, place, sends, shard, out, local_sem):
        self.p, self.s, self.shard, self.out = place, sends, shard, out
        self.local_sem = local_sem
        cols = out.shape[-1]
        cut = cols // 256 * 128
        self.low, self.high = pl.ds(0, cut), pl.ds(cut, cols - cut)
        self.cores = []

    def begin(self):
        p = self.p
        mine = self.out.at[p.line, p.side, p.row, p.core]
        self.local = pltpu.make_async_copy(self.shard, mine, self.local_sem)
        self.local.start()
        self.stage = [self.s.start(self.shard, mine, p.device(line=p.line_peer(k))) for k in range(1, p.lines)]

    def across(self, src):
        self.cores.append(self.s.start(src, src, self.p.device(core=1 - self.p.core)))

    def second(self):
        p, out = self.p, self.out
        self.local.wait()
        for copy in self.stage:
            copy.wait_recv()
        low = out.at[:, p.side, p.row, p.core, :, self.low]
        high = out.at[:, p.side, p.row, p.core, :, self.high]
        self.stage = [self.s.start(low, low, p.device(side=1 - p.side))]
        self.stage += [self.s.start(high, high, p.device(row=p.row_peer(k))) for k in range(1, p.rows)]
        self.across(out.at[:, p.side, p.row, p.core])

    def third(self):
        p, out = self.p, self.out
        for copy in self.stage:
            copy.wait_recv()
        low = out.at[:, :, p.row, p.core, :, self.low]
        high = out.at[:, p.side, :, p.core, :, self.high]
        self.stage = [self.s.start(high, high, p.device(side=1 - p.side))]
        self.stage += [self.s.start(low, low, p.device(row=p.row_peer(k))) for k in range(1, p.rows)]
        self.across(out.at[:, 1 - p.side, p.row, p.core, :, self.low])
        for k in range(1, p.rows):
            self.across(out.at[:, p.side, p.row_source(k), p.core, :, self.high])

    def fourth(self):
        p, out = self.p, self.out
        for copy in self.stage:
            copy.wait_recv()
        for k in range(1, p.rows):
            self.across(out.at[:, :, p.row_source(k), p.core, :, self.low])
        self.across(out.at[:, 1 - p.side, :, p.core, :, self.high])

    def last(self):
        for copy in self.cores:
            copy.wait_recv()


def gather_kernel(count, lines, rows, *refs):
    shards, outs = refs[:count], refs[count : 2 * count]
    send_sems, recv_sems, local_sems = refs[2 * count :]
    place = Place(lines, rows)
    place.greet()
    sends = Sends(send_sems, recv_sems)
    parts = [Gather(place, sends, shards[i], outs[i], local_sems.at[i]) for i in range(count)]
    for part in parts:
        part.begin()
    for i in range(count + 3):
        for lag, step in ((0, "second"), (1, "third"), (2, "fourth"), (3, "last")):
            if 0 <= i - lag < count:
                getattr(parts[i - lag], step)()
    sends.finish()


def gather_all(shards, collective_id):
    wide, narrow = lax.axis_size("wide"), lax.axis_size("narrow")
    lines, rows = wide // 2, narrow // 2
    count = len(shards)
    copies = count * gather_copies(lines, rows)
    outs = pl.pallas_call(
        functools.partial(gather_kernel, count, lines, rows),
        out_shape=[jax.ShapeDtypeStruct((lines, 2, rows, 2) + s.shape, s.dtype) for s in shards],
        in_specs=[pl.BlockSpec(memory_space=pl.ANY)] * count,
        out_specs=[pl.BlockSpec(memory_space=pl.ANY)] * count,
        scratch_shapes=[pltpu.SemaphoreType.DMA((copies,)), pltpu.SemaphoreType.DMA((copies,)), pltpu.SemaphoreType.DMA((count,))],
        compiler_params=pltpu.CompilerParams(collective_id=collective_id, has_side_effects=True),
        cost_estimate=pl.CostEstimate(flops=0, bytes_accessed=4 * 10**7, transcendentals=0),
        name="gather_weights",
    )(*shards)
    return outs


def scatter_copies(lines, rows):
    return 1 + (rows - 1) + 1 + 1 + (rows - 1) + (lines - 1)


def add_loop(lead, fn):
    total = 1
    for size in lead:
        total *= size

    def body(i, carry):
        index = []
        for size in reversed(lead):
            index.append(lax.rem(i, size))
            i = i // size
        fn(tuple(reversed(index)))
        return carry

    lax.fori_loop(0, total, body, 0)


def plus(*terms):
    total = terms[0].astype(jnp.float32)
    for term in terms[1:]:
        total = total + term.astype(jnp.float32)
    return total


class Scatter:
    def __init__(self, place, sends, full, out, buffers):
        self.p, self.s, self.full, self.out = place, sends, full, out
        self.other, self.low1, self.high1, self.low2, self.high2, self.line0, self.lines_in = buffers
        cols = full.shape[-1]
        cut = cols // 256 * 128
        self.low, self.high = pl.ds(0, cut), pl.ds(cut, cols - cut)

    def begin(self):
        core = self.p.core
        self.stage = [self.s.start(self.full.at[:, :, :, 1 - core], self.other, self.p.device(core=1 - core))]

    def second(self):
        p, full, dtype = self.p, self.full, self.full.dtype
        for copy in self.stage:
            copy.wait_recv()

        def add(i):
            l, x, y = i
            full[l, x, y, p.core] = plus(full[l, x, y, p.core], self.other[l, x, y]).astype(dtype)

        add_loop(self.other.shape[:3], add)
        self.stage = [self.s.start(full.at[:, 1 - p.side, :, p.core, :, self.high], self.high1, p.device(side=1 - p.side))]
        for k in range(1, p.rows):
            to = p.row_peer(k)
            self.stage.append(self.s.start(full.at[:, :, to, p.core, :, self.low], self.low1.at[k - 1], p.device(row=to)))

    def third(self):
        p, full, dtype = self.p, self.full, self.full.dtype
        for copy in self.stage:
            copy.wait_recv()

        def add_low(i):
            l, x = i
            terms = [full[l, x, p.row, p.core, :, self.low]] + [self.low1[k, l, x] for k in range(p.rows - 1)]
            full[l, x, p.row, p.core, :, self.low] = plus(*terms).astype(dtype)

        def add_high(i):
            l, y = i
            full[l, p.side, y, p.core, :, self.high] = plus(full[l, p.side, y, p.core, :, self.high], self.high1[l, y]).astype(dtype)

        add_loop((p.lines, 2), add_low)
        add_loop((p.lines, p.rows), add_high)
        self.stage = [self.s.start(full.at[:, 1 - p.side, p.row, p.core, :, self.low], self.low2, p.device(side=1 - p.side))]
        for k in range(1, p.rows):
            to = p.row_peer(k)
            self.stage.append(self.s.start(full.at[:, p.side, to, p.core, :, self.high], self.high2.at[k - 1], p.device(row=to)))

    def fourth(self):
        p, full, dtype = self.p, self.full, self.full.dtype
        for copy in self.stage:
            copy.wait_recv()

        def add(i):
            (l,) = i
            self.line0[l, :, self.low] = plus(full[l, p.side, p.row, p.core, :, self.low], self.low2[l]).astype(dtype)
            terms = [full[l, p.side, p.row, p.core, :, self.high]] + [self.high2[k, l] for k in range(p.rows - 1)]
            self.line0[l, :, self.high] = plus(*terms).astype(dtype)

        add_loop((p.lines,), add)
        self.stage = []
        for k in range(1, p.lines):
            to = p.line_peer(k)
            self.stage.append(self.s.start(self.line0.at[to], self.lines_in.at[k - 1], p.device(line=to)))

    def last(self):
        p = self.p
        for copy in self.stage:
            copy.wait_recv()
        self.out[...] = plus(self.line0[p.line], *[self.lines_in[k] for k in range(p.lines - 1)])


def scatter_buffers(lines, rows, r, c, dtype):
    low = c // 256 * 128
    high = c - low
    return [
        pltpu.VMEM((lines, 2, rows, r, c), dtype),
        pltpu.VMEM((max(rows - 1, 1), lines, 2, r, low), dtype),
        pltpu.VMEM((lines, rows, r, high), dtype),
        pltpu.VMEM((lines, r, low), dtype),
        pltpu.VMEM((max(rows - 1, 1), lines, r, high), dtype),
        pltpu.VMEM((lines, r, c), dtype),
        pltpu.VMEM((max(lines - 1, 1), r, c), dtype),
    ]


NBUF = 7


def tile_loop(width, fn):
    full = width // 256

    def body(j, carry):
        fn(pl.ds(pl.multiple_of(j * 256, 256), 256))
        return carry

    lax.fori_loop(0, full, body, 0)
    if width % 256:
        fn(pl.ds(full * 256, width % 256))


def finish_kernel(lines, rows, products, given, *refs):
    refs = list(refs)

    def take(n):
        out = refs[:n]
        del refs[:n]
        return out

    number = len(products)
    lefts, rights, ready = take(number), take(number), take(given)
    count = number + given
    outs = take(count)
    fulls, buffers = take(count), take(count * NBUF)
    xbuf, gbuf, xsem, gsem, ready_sem, send_sems, recv_sems = refs
    place = Place(lines, rows)
    place.greet()
    sends = Sends(send_sems, recv_sems)
    parts = [Scatter(place, sends, fulls[i], outs[i], buffers[NBUF * i : NBUF * (i + 1)]) for i in range(count)]
    ready_copies = [pltpu.make_async_copy(ready[i], fulls[number + i], ready_sem.at[i]) for i in range(given)]
    for copy in ready_copies:
        copy.start()

    core = place.core
    tasks = []
    for a, (kind, width) in enumerate(products):
        if kind == "rows":
            tasks.append((a, 0, None, None))
        else:
            for c in (1 - core, core):
                for y in range(rows):
                    pitch = rights[a].shape[1] // rows
                    start = y * pitch + c * (pitch - width)
                    tasks.append((a, start, y, c))

    def fetch_right(t):
        a, start, y, c = tasks[t]
        width = products[a][1]
        start = pl.multiple_of(jnp.int32(start), 128)
        return pltpu.make_async_copy(rights[a].at[:, pl.ds(start, width)], gbuf.at[t % 2, :, pl.ds(0, width)], gsem.at[t % 2])

    def fetch_left(a):
        return pltpu.make_async_copy(lefts[a], xbuf.at[a % 2], xsem.at[a % 2])

    fetch_left(0).start()
    fetch_right(0).start()

    def multiply(t):
        a, start, y, c = tasks[t]
        kind, width = products[a]
        if t + 1 < len(tasks):
            fetch_right(t + 1).start()
            if tasks[t + 1][0] != a:
                fetch_left(a + 1).start()
        if t == 0 or tasks[t - 1][0] != a:
            fetch_left(a).wait()
        fetch_right(t).wait()
        full = fulls[a]

        def tile(cols):
            block = dot_nn(xbuf[a % 2], gbuf[t % 2, :, cols])
            n = block.shape[1]
            if kind == "rows":
                full[:, :, :, :, :, cols] = block.reshape(lines, 2, rows, 2, -1, n).astype(full.dtype)
            else:
                full[:, :, y, c, :, cols] = block.reshape(lines, 2, -1, n).astype(full.dtype)

        tile_loop(width, tile)

    order = [number + i for i in range(given)] + list(range(number))
    pending = []

    def advance():
        for item in list(pending):
            getattr(parts[item[0]], item[1].pop(0))()
            if not item[1]:
                pending.remove(item)

    for i in range(given):
        ready_copies[i].wait()
        parts[number + i].begin()
        pending.append((number + i, ["second", "third", "fourth", "last"]))
    for t, (a, start, y, c) in enumerate(tasks):
        multiply(t)
        sent = products[a][0] == "rows" or (c is not core and y == rows - 1)
        if sent:
            parts[a].begin()
        done = t + 1 == len(tasks) or tasks[t + 1][0] != a
        if done or sent:
            advance()
        if done:
            pending.append((a, ["second", "third", "fourth", "last"]))
    while pending:
        advance()
    sends.finish()


def finish(products, given, collective_id):
    wide, narrow = lax.axis_size("wide"), lax.axis_size("narrow")
    lines, rows = wide // 2, narrow // 2
    shapes, plan = [], []
    for left, right, kind in products:
        m, n = left.shape[0], right.shape[1]
        if kind == "rows":
            width = n
            shapes.append((lines, 2, rows, 2, m // (4 * lines * rows), n))
        else:
            width = -(-(n // (2 * rows)) // 128) * 128
            shapes.append((lines, 2, rows, 2, m // (2 * lines), width))
        plan.append((kind, width))
    shapes += [g.shape for g in given]
    count = len(shapes)
    copies = count * scatter_copies(lines, rows)
    dtype = jnp.bfloat16
    scratch = [pltpu.VMEM(s, dtype) for s in shapes]
    for s in shapes:
        scratch += scatter_buffers(lines, rows, s[-2], s[-1], dtype)
    m, t = products[0][0].shape
    widest = max(width for _, width in plan)
    scratch += [
        pltpu.VMEM((2, m, t), dtype),
        pltpu.VMEM((2, t, widest), dtype),
        pltpu.SemaphoreType.DMA((2,)),
        pltpu.SemaphoreType.DMA((2,)),
        pltpu.SemaphoreType.DMA((max(len(given), 1),)),
        pltpu.SemaphoreType.DMA((copies,)),
        pltpu.SemaphoreType.DMA((copies,)),
    ]
    ins = [p[0] for p in products] + [p[1] for p in products] + list(given)
    return pl.pallas_call(
        functools.partial(finish_kernel, lines, rows, plan, len(given)),
        out_shape=[jax.ShapeDtypeStruct(s[-2:], jnp.float32) for s in shapes],
        in_specs=[pl.BlockSpec(memory_space=pl.ANY)] * len(ins),
        out_specs=[pl.BlockSpec(memory_space=pltpu.VMEM)] * count,
        scratch_shapes=scratch,
        compiler_params=pltpu.CompilerParams(collective_id=collective_id, has_side_effects=True, vmem_limit_bytes=60 * 2**20),
        cost_estimate=pl.CostEstimate(flops=14 * 10**9, bytes_accessed=6 * 10**7, transcendentals=0),
        name="finish",
    )(*ins)


def total_kernel(lines, rows, x_ref, o_ref, core_in, plane, line_in, send_sems, recv_sems):
    p = Place(lines, rows)
    barrier = pltpu.get_barrier_semaphore()
    plane_peers = [(k // rows, k % rows) for k in range(1, 2 * rows)]
    targets = [p.device(core=1 - p.core)]
    targets += [p.device(side=lax.rem(p.side + a, 2), row=p.row_peer(b)) for a, b in plane_peers]
    targets += [p.device(line=p.line_peer(k)) for k in range(1, lines)]
    for target in targets:
        pl.semaphore_signal(barrier, inc=1, device_id=target, device_id_type=MESH)
    pl.semaphore_wait(barrier, len(targets))
    sends = Sends(send_sems, recv_sems)
    sends.start(x_ref, core_in, targets[0]).wait_recv()
    here = p.side * rows + p.row
    plane[here] = x_ref[...] + core_in[...]
    stage = [sends.start(plane.at[here], plane.at[here], t) for t in targets[1 : 2 * rows]]
    for copy in stage:
        copy.wait_recv()
    total = plane[0]
    for k in range(1, 2 * rows):
        total = total + plane[k]
    line_in[p.line] = total
    stage = [sends.start(line_in.at[p.line], line_in.at[p.line], t) for t in targets[2 * rows :]]
    for copy in stage:
        copy.wait_recv()
    total = line_in[0]
    for k in range(1, lines):
        total = total + line_in[k]
    o_ref[...] = total
    sends.finish()


def total_sum(x, collective_id):
    wide, narrow = lax.axis_size("wide"), lax.axis_size("narrow")
    lines, rows = wide // 2, narrow // 2
    copies = 1 + 2 * rows - 1 + lines - 1
    return pl.pallas_call(
        functools.partial(total_kernel, lines, rows),
        out_shape=jax.ShapeDtypeStruct(x.shape, x.dtype),
        in_specs=[pl.BlockSpec(memory_space=pltpu.VMEM)],
        out_specs=pl.BlockSpec(memory_space=pltpu.VMEM),
        scratch_shapes=[
            pltpu.VMEM(x.shape, x.dtype),
            pltpu.VMEM((2 * rows,) + x.shape, x.dtype),
            pltpu.VMEM((lines,) + x.shape, x.dtype),
            pltpu.SemaphoreType.DMA((copies,)),
            pltpu.SemaphoreType.DMA((copies,)),
        ],
        compiler_params=pltpu.CompilerParams(collective_id=collective_id, has_side_effects=True),
        cost_estimate=pl.CostEstimate(flops=0, bytes_accessed=10**6, transcendentals=0),
        name="total_sum",
    )(x)


def local(
    tokens,
    features,
    segments,
    positions,
    w_qkv,
    w_out,
    w_up,
    w_down,
    gain_pre,
    gain_attn,
    gain_mid,
    gain_ffn,
    rel_table,
    head_scale,
    w_reduce,
    w_spatial,
    w_expand,
    w_embed,
    bn_gain,
    bn_shift,
    d_out,
):
    both = ("wide", "narrow")
    devices = lax.axis_size(both)
    me = lax.axis_index("wide") * lax.axis_size("narrow") + lax.axis_index("narrow")
    vectors = (gain_pre, gain_attn, gain_mid, gain_ffn, bn_gain, bn_shift, rel_table.reshape(-1))
    held = jnp.concatenate(vectors)
    held = jnp.pad(held, (0, 16 * 256 - held.shape[0])).reshape(16, 256)
    gathered = gather_all([held, w_reduce, w_spatial, w_expand, w_embed, w_qkv, w_out, w_up, w_down], 1)
    full_held = gathered[0].reshape(devices, -1)
    full_reduce, full_spatial, full_expand, full_embed, full_qkv, full_out, full_up, full_down = (
        item.reshape(-1, item.shape[-1]) for item in gathered[1:]
    )
    full_vectors, at = [], 0
    for item in vectors:
        full_vectors.append(full_held[:, at : at + item.shape[0]])
        at += item.shape[0]
    full_pre, full_attn, full_mid, full_ffn, full_bn_gain, full_bn_shift = (
        item.reshape(-1) for item in full_vectors[:6]
    )
    full_table = full_vectors[6].reshape(devices, HEADS, -1).transpose(1, 0, 2).reshape(HEADS, -1)
    rows, length = (segments.shape[0], segments.shape[1])
    images, side = (features.shape[0], features.shape[1])
    patch_count = images * side * side
    whole = patch_count * lax.axis_size(("wide", "narrow"))
    stem_in = features.reshape(patch_count, features.shape[3])
    pre_first = product(stem_in, full_reduce)
    first = smooth(pre_first).astype(jnp.bfloat16)
    columns = unfold(first.reshape(images, side, side, first.shape[1])).reshape(
        patch_count, 9 * first.shape[1]
    )
    pre_second = product(columns, full_spatial)
    second = smooth(pre_second).astype(jnp.bfloat16)
    third = product(second, full_expand)
    sums = jnp.concatenate([jnp.sum(third, axis=0), jnp.sum(third * third, axis=0)])
    bn_total, bn_squares = jnp.split(total_sum(sums.reshape(16, -1), 3).reshape(-1), 2)
    bn_mean = bn_total / whole
    bn_inv = lax.rsqrt(bn_squares / whole - bn_mean * bn_mean + epsilon)
    bn_unit = (third - bn_mean) * bn_inv
    pre_joined = (
        bn_unit * full_bn_gain.astype(jnp.float32)
        + full_bn_shift.astype(jnp.float32)
        + stem_in.astype(jnp.float32)
    )
    joined = smooth(pre_joined).astype(jnp.bfloat16)
    embedded = product(joined, full_embed)
    first_at = positions[0, 0]
    base = tokens.astype(jnp.float32)
    covered = lax.dynamic_slice_in_dim(base, first_at, patch_count, 0) + embedded
    start = lax.dynamic_update_slice_in_dim(base, covered, first_at, 0)
    normed0, unit0, inv0 = layer_norm(start, full_pre.astype(jnp.float32))
    normed0_low = normed0.astype(jnp.bfloat16)
    packed = product(normed0_low, full_qkv).astype(jnp.bfloat16)
    win = windows(segments)
    attended, logsums, bias = attend(packed, segments, bias_strips(full_table), win)
    scale_row = jnp.repeat(head_scale, HDIM)[None, :]
    scaled = attended * scale_row
    mixed_in, unit1, inv1 = layer_norm(scaled, full_attn.astype(jnp.float32))
    mixed_low = mixed_in.astype(jnp.bfloat16)
    middle = start + product(mixed_low, full_out)
    normed2, unit2, inv2 = layer_norm(middle, full_mid.astype(jnp.float32))
    normed2_low = normed2.astype(jnp.bfloat16)
    pre_up = product(normed2_low, full_up)
    activ = smooth(pre_up)
    narrowed, unit3, inv3 = layer_norm(activ, full_ffn.astype(jnp.float32))
    narrowed_low = narrowed.astype(jnp.bfloat16)
    result = middle + product(narrowed_low, full_down)
    mixed = result.astype(jnp.bfloat16)
    grad_result = d_out.astype(jnp.float32)
    grad_narrowed = product_nt(d_out, full_down)
    grad_activ, grad_gain_ffn = layer_norm_back(
        grad_narrowed, unit3, inv3, full_ffn.astype(jnp.float32)
    )
    grad_pre_up = smooth_back(pre_up, grad_activ).astype(jnp.bfloat16)
    grad_normed2 = product_nt(grad_pre_up, full_up)
    grad_mid_in, grad_gain_mid = layer_norm_back(
        grad_normed2, unit2, inv2, full_mid.astype(jnp.float32)
    )
    grad_middle = grad_result + grad_mid_in
    grad_branch = grad_middle.astype(jnp.bfloat16)
    grad_mixed_in = product_nt(grad_branch, full_out)
    grad_scaled, grad_gain_attn = layer_norm_back(
        grad_mixed_in, unit1, inv1, full_attn.astype(jnp.float32)
    )
    grad_head_local = jnp.sum(jnp.sum(grad_scaled * attended, axis=0).reshape(HEADS, HDIM), axis=1)
    grad_attended = (grad_scaled * scale_row).astype(jnp.bfloat16)
    grad_packed, grad_strips = attend_back(packed, grad_attended, attended, segments, bias, logsums, win)
    grad_table = table_from_strips(grad_strips)
    grad_normed0 = product_nt(grad_packed, full_qkv)
    grad_start_in, grad_gain_pre = layer_norm_back(
        grad_normed0, unit0, inv0, full_pre.astype(jnp.float32)
    )
    grad_tokens = grad_middle + grad_start_in
    grad_embedded = lax.dynamic_slice_in_dim(grad_tokens, first_at, patch_count, 0).astype(jnp.bfloat16)
    grad_w_embed = product_tn(joined, grad_embedded)
    grad_joined = product_nt(grad_embedded, full_embed)
    grad_pre_joined = smooth_back(pre_joined, grad_joined)
    grad_bn_shift = jnp.sum(grad_pre_joined, axis=0)
    grad_bn_gain = jnp.sum(grad_pre_joined * bn_unit, axis=0)
    smalls = (
        grad_gain_pre,
        grad_gain_attn,
        grad_gain_mid,
        grad_gain_ffn,
        grad_bn_gain,
        grad_bn_shift,
        grad_table.reshape(-1),
        grad_head_local,
    )
    small = jnp.concatenate(smalls)
    small = jnp.pad(small, (0, -small.shape[0] % 1024)).reshape(-1, 128)
    small = total_sum(small, 4).reshape(-1)
    totals, at = [], 0
    for item in smalls:
        totals.append(small[at : at + item.shape[0]])
        at += item.shape[0]
    sum_pre, sum_attn, sum_mid, sum_ffn, sum_bn_gain, sum_bn_shift = (
        lax.dynamic_slice_in_dim(item, me * (item.shape[0] // devices), item.shape[0] // devices)
        for item in totals[:6]
    )
    breadth = 2 * RSPAN // devices
    sum_table = lax.dynamic_slice_in_dim(totals[6].reshape(HEADS, -1), me * breadth, breadth, 1)
    grad_head = totals[7]
    bn_gain_row = full_bn_gain.astype(jnp.float32)
    grad_unit = grad_pre_joined * bn_gain_row
    sum_unit, sum_cross = totals[5] * bn_gain_row, totals[4] * bn_gain_row
    grad_third = (bn_inv * (grad_unit - sum_unit / whole - bn_unit * (sum_cross / whole))).astype(
        jnp.bfloat16
    )
    grad_w_expand = product_tn(second, grad_third)
    grad_second = product_nt(grad_third, full_expand)
    grad_pre_second = smooth_back(pre_second, grad_second).astype(jnp.bfloat16)
    grad_w_spatial = product_tn(columns, grad_pre_second)
    grad_columns = product_nt(grad_pre_second, full_spatial)
    grad_first = fold(grad_columns.reshape(images, side, side, -1)).reshape(patch_count, -1)
    grad_pre_first = smooth_back(pre_first, grad_first).astype(jnp.bfloat16)
    grad_w_reduce = product_tn(stem_in, grad_pre_first)
    grad_features = (grad_pre_joined + product_nt(grad_pre_first, full_reduce)).reshape(
        features.shape
    )
    lines, planes = lax.axis_size("wide") // 2, lax.axis_size("narrow") // 2

    def by_rows(grad):
        return grad.astype(jnp.bfloat16).reshape(lines, 2, planes, 2, -1, grad.shape[1])

    sum_down, sum_up, sum_qkv, sum_out, sum_embed, sum_expand, sum_spatial, sum_reduce = finish(
        [
            (d_out.T, narrowed_low, "blocks"),
            (normed2_low.T, grad_pre_up, "blocks"),
            (normed0_low.T, grad_packed, "blocks"),
            (mixed_low.T, grad_branch, "rows"),
        ],
        [by_rows(grad_w_embed), by_rows(grad_w_expand), by_rows(grad_w_spatial), by_rows(grad_w_reduce)],
        2,
    )
    sum_down = sum_down.T
    width = 3 * D // (2 * planes)
    sum_qkv = jnp.where(
        lax.axis_index("narrow") % 2 == 0, sum_qkv[:, :width], sum_qkv[:, sum_qkv.shape[1] - width :]
    )
    return (
        mixed,
        grad_tokens,
        grad_features,
        sum_qkv,
        sum_out,
        sum_up,
        sum_down,
        sum_pre,
        sum_attn,
        sum_mid,
        sum_ffn,
        sum_table,
        grad_head,
        sum_reduce,
        sum_spatial,
        sum_expand,
        sum_embed,
        sum_bn_gain,
        sum_bn_shift,
    )


def solution(mesh):
    placed = (
        P(("wide", "narrow"), None),
        P(("wide", "narrow"), None, None, None),
        P(("wide", "narrow"), None),
        P(("wide", "narrow"), None),
        P(("wide", "narrow"), None),
        P(("wide", "narrow"), None),
        P(("wide", "narrow"), None),
        P(("wide", "narrow"), None),
        P(("wide", "narrow")),
        P(("wide", "narrow")),
        P(("wide", "narrow")),
        P(("wide", "narrow")),
        P(None, ("wide", "narrow")),
        P(),
        P(("wide", "narrow"), None),
        P(("wide", "narrow"), None),
        P(("wide", "narrow"), None),
        P(("wide", "narrow"), None),
        P(("wide", "narrow")),
        P(("wide", "narrow")),
        P(("wide", "narrow"), None),
    )
    return jax.shard_map(
        local,
        mesh=mesh,
        in_specs=placed,
        out_specs=(
            P(("wide", "narrow"), None),
            P(("wide", "narrow"), None),
            P(("wide", "narrow"), None, None, None),
            P("wide", "narrow"),
            P(("wide", "narrow"), None),
            P("wide", "narrow"),
            P("narrow", "wide"),
            P(("wide", "narrow")),
            P(("wide", "narrow")),
            P(("wide", "narrow")),
            P(("wide", "narrow")),
            P(None, ("wide", "narrow")),
            P(),
            P(("wide", "narrow"), None),
            P(("wide", "narrow"), None),
            P(("wide", "narrow"), None),
            P(("wide", "narrow"), None),
            P(("wide", "narrow")),
            P(("wide", "narrow")),
        ),
        check_vma=False,
    )
```

```python
import functools

import jax
import jax.numpy as jnp
from jax import lax
from jax.experimental import pallas as pl
from jax.experimental.pallas import tpu as pltpu
from jax.sharding import PartitionSpec as P

D = 768
HEADS = 12
HDIM = 64
RSPAN = 128


epsilon = 1e-05


def product(lhs_matrix, rhs_matrix):
    return jnp.dot(lhs_matrix, rhs_matrix, preferred_element_type=jnp.float32)


def product_tn(lhs_matrix, rhs_matrix):
    return lax.dot_general(
        lhs_matrix, rhs_matrix, (((0,), (0,)), ((), ())), preferred_element_type=jnp.float32
    )


def product_nt(lhs_matrix, rhs_matrix):
    return lax.dot_general(
        lhs_matrix, rhs_matrix, (((1,), (1,)), ((), ())), preferred_element_type=jnp.float32
    )


def layer_norm(values, gain):
    average = jnp.mean(values, axis=-1, keepdims=True)
    centred = values - average
    inv_std = lax.rsqrt(jnp.mean(centred * centred, axis=-1, keepdims=True) + epsilon)
    unit_rows = centred * inv_std
    return (unit_rows * gain, unit_rows, inv_std)


def layer_norm_back(cotangent, unit_rows, inv_std, gain):
    weighted = cotangent * gain
    inner = (
        weighted
        - jnp.mean(weighted, axis=-1, keepdims=True)
        - unit_rows * jnp.mean(weighted * unit_rows, axis=-1, keepdims=True)
    )
    return (inv_std * inner, jnp.sum(cotangent * unit_rows, axis=0))


def smooth(values):
    return jax.nn.gelu(values, approximate=True)


def smooth_back(values, cotangent):
    unused, pullback = jax.vjp(smooth, values)
    return pullback(cotangent)[0]


def unfold(grid):
    side = grid.shape[1]
    padded = jnp.pad(grid, ((0, 0), (1, 1), (1, 1), (0, 0)))
    pieces = [
        padded[:, row_off : row_off + side, col_off : col_off + side, :]
        for row_off in range(3)
        for col_off in range(3)
    ]
    return jnp.concatenate(pieces, axis=-1)


def fold(columns):
    channels = columns.shape[-1] // 9
    side = columns.shape[1]
    total = jnp.zeros((columns.shape[0], side + 2, side + 2, channels), jnp.float32)
    for row_off in range(3):
        for col_off in range(3):
            which = row_off * 3 + col_off
            piece = columns[..., which * channels : (which + 1) * channels]
            total = total + jnp.pad(
                piece, ((0, 0), (row_off, 2 - row_off), (col_off, 2 - col_off), (0, 0))
            )
    return total[:, 1:-1, 1:-1, :]


PAIRS = HEADS // 2
BLK = 128
NEG = -1e30


def dot_nn(a, b):
    return lax.dot_general(a, b, (((1,), (0,)), ((), ())), preferred_element_type=jnp.float32)


def dot_nt(a, b):
    return lax.dot_general(a, b, (((1,), (1,)), ((), ())), preferred_element_type=jnp.float32)


def split_heads(pair, scale):
    lane = lax.broadcasted_iota(jnp.int32, pair.shape, 1)
    vals = pair * jnp.asarray(scale, pair.dtype)
    zero = jnp.zeros_like(vals)
    return jnp.concatenate([jnp.where(lane < HDIM, vals, zero), jnp.where(lane < HDIM, zero, vals)], axis=0)


def join_heads(both):
    row = lax.broadcasted_iota(jnp.int32, (2 * HDIM, BLK), 0)
    return jnp.where(row < HDIM, both[:, :BLK], both[:, BLK:])


def bias_strips(table):
    rev = jnp.flip(table.astype(jnp.float32), axis=1)
    first, last = rev[:, 255:256], rev[:, 0:1]
    below = jnp.concatenate([jnp.broadcast_to(first, (HEADS, 129)), rev[:, 128:255]], axis=1)
    middle = jnp.concatenate([rev[:, 127:256], rev[:, 0:127]], axis=1)
    above = jnp.concatenate([last, rev[:, 0:127], jnp.broadcast_to(last, (HEADS, 128))], axis=1)
    low = jnp.broadcast_to(first, (HEADS, 256))
    high = jnp.broadcast_to(last, (HEADS, 256))
    return jnp.stack([low, below, middle, above, high], axis=1)


def table_from_strips(sums):
    low, below, middle, above, high = (sums[:, i] for i in range(5))
    total = jnp.concatenate([middle[:, 129:256], middle[:, 0:129]], axis=1)
    zero = jnp.zeros((HEADS, 127), jnp.float32)
    first = jnp.sum(low, axis=1, keepdims=True) + jnp.sum(below[:, :129], axis=1, keepdims=True)
    last = jnp.sum(high, axis=1, keepdims=True) + above[:, 0:1] + jnp.sum(above[:, 128:], axis=1, keepdims=True)
    total = total + jnp.concatenate([jnp.zeros((HEADS, 128), jnp.float32), below[:, 129:], first], axis=1)
    head = jnp.concatenate([above[:, 1:128], jnp.zeros((HEADS, 129), jnp.float32)], axis=1)
    total = total + head + jnp.concatenate([last, jnp.zeros((HEADS, 255), jnp.float32)], axis=1)
    return jnp.flip(total, axis=1)


def windows(segments):
    seg = segments.reshape(-1)
    starts = seg[::BLK]
    ends = seg[BLK - 1 :: BLK]
    low = jnp.sum((seg[None, :] < starts[:, None]).astype(jnp.int32), axis=1) // BLK
    high = (jnp.sum((seg[None, :] <= ends[:, None]).astype(jnp.int32), axis=1) + BLK - 1) // BLK
    return jnp.stack([low, high])


def attend_kernel(win, packed, segk, segq, strips, out, logsum, bias, vt, qm, acc, stat):
    i = pl.program_id(0)

    @pl.when(i == 0)
    def _():
        for hp in range(PAIRS):
            vt[pl.ds(hp * 128, 128), :] = packed[:, pl.ds(2 * D + hp * 128, 128)].T
            for d in range(5):
                for half in range(2):
                    row = strips[2 * hp + half, pl.ds(d, 1), :]
                    tile = jnp.broadcast_to(row, (BLK, 256))
                    if 0 < d < 4:
                        tile = pltpu.roll(tile, 0, 1, stride=1, stride_axis=0)
                    bias[hp, d, :, pl.ds(half * BLK, BLK)] = tile[:, :BLK]

    rows = pl.ds(pl.multiple_of(i * BLK, BLK), BLK)
    for hp in range(PAIRS):
        qm[hp] = split_heads(packed[rows, pl.ds(hp * 128, 128)], HDIM ** -0.5)
        acc[hp] = jnp.zeros((128, 256), jnp.float32)
        stat[hp, 0] = jnp.full((1, 256), NEG, jnp.float32)
        stat[hp, 1] = jnp.zeros((1, 256), jnp.float32)
    sq = segq[:, rows]
    sq2 = jnp.concatenate([sq, sq], axis=1)

    def body(kb, carry):
        keys = pl.ds(pl.multiple_of(kb * BLK, BLK), BLK)
        allowed = segk[keys, :] == sq2
        d = jnp.clip(kb - i, -2, 2) + 2
        for hp in range(PAIRS):
            s = dot_nt(packed[keys, pl.ds(D + hp * 128, 128)], qm[hp])
            s = jnp.where(allowed, s + bias[hp, d], NEG)
            old = stat[hp, 0]
            new = jnp.maximum(old, jnp.max(s, axis=0, keepdims=True))
            p = jnp.exp(s - new)
            alpha = jnp.exp(old - new)
            stat[hp, 0] = new
            stat[hp, 1] = stat[hp, 1] * alpha + jnp.sum(p, axis=0, keepdims=True)
            acc[hp] = acc[hp] * alpha + dot_nn(vt[pl.ds(hp * 128, 128), keys], p.astype(jnp.bfloat16))
        return carry

    lax.fori_loop(win[0, i], win[1, i], body, 0)
    for hp in range(PAIRS):
        total = stat[hp, 1]
        out[:, pl.ds(hp * 128, 128)] = join_heads(acc[hp] / total).T
        logsum[0, pl.ds(hp, 1), :] = stat[hp, 0] + jnp.log(total)


def attend(packed, segments, strips, win):
    length = packed.shape[0]
    blocks = length // BLK
    seg = segments.reshape(1, length)
    whole = lambda shape: pl.BlockSpec(shape, lambda i, w: (0,) * len(shape))
    return pl.pallas_call(
        attend_kernel,
        out_shape=(
            jax.ShapeDtypeStruct((length, D), jnp.float32),
            jax.ShapeDtypeStruct((blocks, PAIRS, 256), jnp.float32),
            jax.ShapeDtypeStruct((PAIRS, 5, BLK, 256), jnp.float32),
        ),
        grid_spec=pltpu.PrefetchScalarGridSpec(
            num_scalar_prefetch=1,
            grid=(blocks,),
            in_specs=[whole((length, 3 * D)), whole((length, 1)), whole((1, length)), whole((HEADS, 5, 256))],
            out_specs=(
                pl.BlockSpec((BLK, D), lambda i, w: (i, 0)),
                pl.BlockSpec((1, PAIRS, 256), lambda i, w: (i, 0, 0)),
                whole((PAIRS, 5, BLK, 256)),
            ),
            scratch_shapes=[
                pltpu.VMEM((D, length), jnp.bfloat16),
                pltpu.VMEM((PAIRS, 256, 128), jnp.bfloat16),
                pltpu.VMEM((PAIRS, 128, 256), jnp.float32),
                pltpu.VMEM((PAIRS, 2, 1, 256), jnp.float32),
            ],
        ),
        compiler_params=pltpu.CompilerParams(vmem_limit_bytes=48 * 2**20),
        cost_estimate=pl.CostEstimate(flops=2 * 10**10, bytes_accessed=10**7, transcendentals=6 * 10**6),
        name="attend",
    )(win, packed, seg.reshape(length, 1), seg, strips)


def unskew(tile):
    row = lax.broadcasted_iota(jnp.int32, tile.shape, 0)
    width = tile.shape[1]
    for bit in range(7):
        step = 1 << bit
        tile = jnp.where((row & step) != 0, pltpu.roll(tile, width - step, 1), tile)
    return tile


def attend_back_kernel(win, packed, grads, attended, segk, segq, bias, logsum, out, tab, kt, qm, om, dqt, dk, dv, gt):
    i = pl.program_id(0)
    last = pl.num_programs(0) - 1

    @pl.when(i == 0)
    def _():
        for hp in range(PAIRS):
            kt[pl.ds(hp * 128, 128), :] = packed[:, pl.ds(D + hp * 128, 128)].T
        dk[...] = jnp.zeros_like(dk)
        dv[...] = jnp.zeros_like(dv)
        gt[...] = jnp.zeros_like(gt)

    rows = pl.ds(pl.multiple_of(i * BLK, BLK), BLK)
    dots = []
    for hp in range(PAIRS):
        cols = pl.ds(hp * 128, 128)
        qm[hp] = split_heads(packed[rows, cols], HDIM ** -0.5)
        om[hp] = split_heads(grads[:, cols], 1.0)
        cross = (grads[:, cols].astype(jnp.float32) * attended[:, cols]).T
        dots.append(jnp.concatenate([
            jnp.sum(cross[:HDIM], axis=0, keepdims=True),
            jnp.sum(cross[HDIM:], axis=0, keepdims=True)], axis=1))
        dqt[hp] = jnp.zeros((128, 256), jnp.float32)
    sq = segq[:, rows]
    sq2 = jnp.concatenate([sq, sq], axis=1)

    def body(kb, carry):
        keys = pl.ds(pl.multiple_of(kb * BLK, BLK), BLK)
        allowed = segk[keys, :] == sq2
        d = jnp.clip(kb - i, -2, 2) + 2
        for hp in range(PAIRS):
            cols = pl.ds(hp * 128, 128)
            s = dot_nt(packed[keys, pl.ds(D + hp * 128, 128)], qm[hp]) + bias[hp, d]
            p = jnp.exp(jnp.where(allowed, s, NEG) - logsum[0, pl.ds(hp, 1), :])
            dp = dot_nt(packed[keys, pl.ds(2 * D + hp * 128, 128)], om[hp])
            ds = p * (dp - dots[hp])
            gt[hp, d] += ds
            low = ds.astype(jnp.bfloat16)
            dv[keys, cols] += dot_nn(p.astype(jnp.bfloat16), om[hp])
            dk[keys, cols] += dot_nn(low, qm[hp])
            dqt[hp] += dot_nn(kt[cols, keys], low)
        return carry

    lax.fori_loop(win[0, i], win[1, i], body, 0)
    for hp in range(PAIRS):
        out[rows, pl.ds(hp * 128, 128)] = (join_heads(dqt[hp]).T * (HDIM ** -0.5)).astype(jnp.bfloat16)

    @pl.when(i == last)
    def _():
        out[:, pl.ds(D, D)] = dk[...].astype(jnp.bfloat16)
        out[:, pl.ds(2 * D, D)] = dv[...].astype(jnp.bfloat16)
        for hp in range(PAIRS):
            for half in range(2):
                for d in range(5):
                    tile = gt[hp, d, :, pl.ds(half * BLK, BLK)]
                    tile = jnp.concatenate([tile, jnp.zeros_like(tile)], axis=1)
                    if 0 < d < 4:
                        tile = unskew(tile)
                    tab[2 * hp + half, pl.ds(d, 1), :] = jnp.sum(tile, axis=0, keepdims=True)


def attend_back(packed, grads, attended, segments, bias, logsum, win):
    length = packed.shape[0]
    blocks = length // BLK
    seg = segments.reshape(1, length)
    whole = lambda shape: pl.BlockSpec(shape, lambda i, w: (0,) * len(shape))
    return pl.pallas_call(
        attend_back_kernel,
        out_shape=(
            jax.ShapeDtypeStruct((length, 3 * D), jnp.bfloat16),
            jax.ShapeDtypeStruct((HEADS, 5, 256), jnp.float32),
        ),
        grid_spec=pltpu.PrefetchScalarGridSpec(
            num_scalar_prefetch=1,
            grid=(blocks,),
            in_specs=[
                whole((length, 3 * D)),
                pl.BlockSpec((BLK, D), lambda i, w: (i, 0)),
                pl.BlockSpec((BLK, D), lambda i, w: (i, 0)),
                whole((length, 1)),
                whole((1, length)),
                whole((PAIRS, 5, BLK, 256)),
                pl.BlockSpec((1, PAIRS, 256), lambda i, w: (i, 0, 0)),
            ],
            out_specs=(whole((length, 3 * D)), whole((HEADS, 5, 256))),
            scratch_shapes=[
                pltpu.VMEM((D, length), jnp.bfloat16),
                pltpu.VMEM((PAIRS, 256, 128), jnp.bfloat16),
                pltpu.VMEM((PAIRS, 256, 128), jnp.bfloat16),
                pltpu.VMEM((PAIRS, 128, 256), jnp.float32),
                pltpu.VMEM((length, D), jnp.float32),
                pltpu.VMEM((length, D), jnp.float32),
                pltpu.VMEM((PAIRS, 5, BLK, 256), jnp.float32),
            ],
        ),
        compiler_params=pltpu.CompilerParams(vmem_limit_bytes=56 * 2**20),
        cost_estimate=pl.CostEstimate(flops=5 * 10**10, bytes_accessed=2 * 10**7, transcendentals=6 * 10**6),
        name="attend_back",
    )(win, packed, grads, attended, seg.reshape(length, 1), seg, bias, logsum)


MESH = pl.DeviceIdType.MESH


class Place:
    def __init__(self, lines, rows):
        self.lines, self.rows = lines, rows
        wide, narrow = lax.axis_index("wide"), lax.axis_index("narrow")
        self.line, self.side = wide // 2, wide % 2
        self.row, self.core = narrow // 2, narrow % 2

    def device(self, line=None, side=None, row=None, core=None):
        line = self.line if line is None else line
        side = self.side if side is None else side
        row = self.row if row is None else row
        core = self.core if core is None else core
        return (line * 2 + side, row * 2 + core)

    def line_peer(self, k):
        return lax.rem(self.line + k, self.lines)

    def line_source(self, k):
        return lax.rem(self.line + self.lines - k, self.lines)

    def row_peer(self, k):
        return lax.rem(self.row + k, self.rows)

    def row_source(self, k):
        return lax.rem(self.row + self.rows - k, self.rows)

    def plane_peers(self):
        steps = [(k // self.rows, k % self.rows) for k in range(1, 2 * self.rows)]
        return [self.device(side=lax.rem(self.side + a, 2), row=self.row_peer(b)) for a, b in steps]

    def greet(self):
        barrier = pltpu.get_barrier_semaphore()
        targets = [self.device(line=self.line_peer(k)) for k in range(1, self.lines)]
        targets += self.plane_peers() + [self.device(core=1 - self.core)]
        for target in targets:
            pl.semaphore_signal(barrier, inc=1, device_id=target, device_id_type=MESH)
        pl.semaphore_wait(barrier, len(targets))


class Sends:
    def __init__(self, send_sems, recv_sems):
        self.send_sems, self.recv_sems, self.used = send_sems, recv_sems, 0
        self.started = []

    def start(self, src, dst, device):
        copy = pltpu.make_async_remote_copy(
            src_ref=src, dst_ref=dst, send_sem=self.send_sems.at[self.used], recv_sem=self.recv_sems.at[self.used],
            device_id=device, device_id_type=MESH)
        copy.start()
        self.used += 1
        self.started.append(copy)
        return copy

    def finish(self):
        for copy in self.started:
            copy.wait_send()


def gather_copies(lines, rows):
    return (lines - 1) + 1 + (rows - 1) + (rows - 1) + 1 + 1 + rows + rows


class Gather:
    def __init__(self, place, sends, shard, out, local_sem, at, width):
        self.p, self.s, self.shard, self.out = place, sends, shard, out
        self.local_sem = local_sem
        cut = width // 256 * 128
        self.every, self.low, self.high = pl.ds(at, width), pl.ds(at, cut), pl.ds(at + cut, width - cut)
        self.cores = []

    def begin(self):
        p = self.p
        mine = self.out.at[p.line, p.side, p.row, p.core, :, self.every]
        shard = self.shard.at[:, self.every]
        self.local = pltpu.make_async_copy(shard, mine, self.local_sem)
        self.local.start()
        self.stage = [self.s.start(shard, mine, p.device(line=p.line_peer(k))) for k in range(1, p.lines)]

    def across(self, src):
        self.cores.append(self.s.start(src, src, self.p.device(core=1 - self.p.core)))

    def second(self):
        p, out = self.p, self.out
        self.local.wait()
        for copy in self.stage:
            copy.wait_recv()
        low = out.at[:, p.side, p.row, p.core, :, self.low]
        high = out.at[:, p.side, p.row, p.core, :, self.high]
        self.stage = [self.s.start(low, low, p.device(side=1 - p.side))]
        self.stage += [self.s.start(high, high, p.device(row=p.row_peer(k))) for k in range(1, p.rows)]
        self.across(out.at[:, p.side, p.row, p.core, :, self.every])

    def third(self):
        p, out = self.p, self.out
        for copy in self.stage:
            copy.wait_recv()
        low = out.at[:, :, p.row, p.core, :, self.low]
        high = out.at[:, p.side, :, p.core, :, self.high]
        self.stage = [self.s.start(high, high, p.device(side=1 - p.side))]
        self.stage += [self.s.start(low, low, p.device(row=p.row_peer(k))) for k in range(1, p.rows)]
        self.across(out.at[:, 1 - p.side, p.row, p.core, :, self.low])
        for k in range(1, p.rows):
            self.across(out.at[:, p.side, p.row_source(k), p.core, :, self.high])

    def fourth(self):
        p, out = self.p, self.out
        for copy in self.stage:
            copy.wait_recv()
        for k in range(1, p.rows):
            self.across(out.at[:, :, p.row_source(k), p.core, :, self.low])
        self.across(out.at[:, 1 - p.side, :, p.core, :, self.high])

    def last(self):
        for copy in self.cores:
            copy.wait_recv()


class Total:
    def __init__(self, place, sends, x, core_in, plane, line_in):
        self.p, self.s, self.x, self.core_in, self.plane, self.line_in = place, sends, x, core_in, plane, line_in

    def begin(self):
        p = self.p
        self.stage = [self.s.start(self.x, self.core_in, p.device(core=1 - p.core))]

    def second(self):
        p = self.p
        for copy in self.stage:
            copy.wait_recv()
        here = p.side * p.rows + p.row
        self.plane[here] = self.x[...] + self.core_in[...]
        self.stage = [self.s.start(self.plane.at[here], self.plane.at[here], t) for t in p.plane_peers()]

    def third(self):
        p = self.p
        for copy in self.stage:
            copy.wait_recv()
        total = self.plane[0]
        for k in range(1, 2 * p.rows):
            total = total + self.plane[k]
        self.line_in[p.line] = total
        mine = self.line_in.at[p.line]
        self.stage = [self.s.start(mine, mine, p.device(line=p.line_peer(k))) for k in range(1, p.lines)]

    def last(self):
        for copy in self.stage:
            copy.wait_recv()
        total = self.line_in[0]
        for k in range(1, self.p.lines):
            total = total + self.line_in[k]
        return total


def total_buffers(lines, rows, shape, dtype):
    return [
        pltpu.VMEM(shape, dtype),
        pltpu.VMEM(shape, dtype),
        pltpu.VMEM((2 * rows,) + shape, dtype),
        pltpu.VMEM((lines,) + shape, dtype),
    ]


def total_copies(lines, rows):
    return 2 * rows + lines - 1


def gelu(v):
    return 0.5 * v * (1.0 + jnp.tanh(0.7978845608028654 * (v + 0.044715 * (v * v * v))))


def spread(vector, me, total):
    n = vector.shape[1]
    lane = lax.broadcasted_iota(jnp.int32, (n, total), 1)
    row = lax.broadcasted_iota(jnp.int32, (n, total), 0)
    hot = jnp.where(lane == me * n + row, 1.0, 0.0).astype(jnp.bfloat16)
    return dot_nn(vector, hot)


def matrix(ref):
    block = ref[...].astype(jnp.float32)
    return block.reshape(-1, block.shape[-1]).astype(jnp.bfloat16)


def shifted(values, row_off, col_off, side):
    count = values.shape[0]
    step = row_off * side + col_off
    moved = pltpu.roll(values, (-step) % count, 0) if step % count else values
    patch = lax.broadcasted_iota(jnp.int32, (count, 1), 0)
    row, col = patch // side + row_off, lax.rem(patch, side) + col_off
    inside = (row >= 0) & (row < side) & (col >= 0) & (col < side)
    return jnp.where(inside, moved, 0.0)


FRONT_VECTORS = 7


def front_kernel(lines, rows, side, whole, pieces, number, *refs):
    refs = list(refs)

    def take(n):
        out = refs[:n]
        del refs[:n]
        return out

    (at,) = take(1)
    vectors = take(FRONT_VECTORS)
    (stem, tokens) = take(2)
    shards = take(number)
    outs = take(number)
    (gains, pre_first, columns, pre_second, second, unit, inv, joined, start, normed, packed) = take(11)
    mats = take(5)
    (placing,) = take(1)
    held_bufs, sum_bufs = take(4), take(4)
    send_sems, recv_sems, local_sems = take(3)
    place = Place(lines, rows)
    place.greet()
    sends = Sends(send_sems, recv_sems)

    me = (place.line * 2 + place.side) * (2 * rows) + place.row * 2 + place.core
    held = held_bufs[0]
    held[...] = jnp.zeros_like(held)
    devices = 4 * lines * rows

    parts = []
    for i, (which, col, width) in enumerate(pieces):
        parts.append(Gather(place, sends, shards[which], outs[which], local_sems.at[i], col, width))
    parts[0].begin()
    parts[1].begin()
    for v, (ref, row) in enumerate(zip(vectors[:6], (2, 3, 4, 5, 0, 1))):
        n = ref.shape[1]
        line = spread(ref[...], me, n * devices).astype(jnp.bfloat16)
        for k in range(0, n * devices, 1024):
            span = min(1024, n * devices - k)
            held[pl.ds(row + k // 1024, 1), pl.ds(0, span)] = line[:, k : k + span]
    table = spread(vectors[6][...], me, vectors[6].shape[1] * devices).astype(jnp.bfloat16)
    for h in range(HEADS):
        held[pl.ds(8 + h // 4, 1), pl.ds(h % 4 * 256, 256)] = table[h : h + 1, :]
    vector_total = Total(place, sends, *held_bufs)
    vector_total.begin()
    for part in parts[2:]:
        part.begin()

    steps = []
    for i in range(len(parts) + 3):
        for lag, name in ((0, "second"), (1, "third"), (2, "fourth"), (3, "last")):
            if 0 <= i - lag < len(parts):
                steps.append((i - lag, name))

    def pump(n=None, until=None):
        while steps and (n is None or n > 0):
            i, name = steps.pop(0)
            getattr(parts[i], name)()
            n = None if n is None else n - 1
            if until is not None and (i, name) == (until, "last"):
                break

    pump(2)
    vector_total.second()
    pump(2)
    vector_total.third()
    pump(until=0)
    count = side * side
    w_reduce, w_spatial, w_expand, w_embed, w_qkv = mats
    w_reduce[...] = matrix(outs[0])
    pre = dot_nn(stem[...], w_reduce[...])
    pre_first[...] = pre
    first = gelu(pre).astype(jnp.bfloat16).astype(jnp.float32)
    channels = first.shape[1]
    for r in range(3):
        for c in range(3):
            k = r * 3 + c
            columns[:, pl.ds(k * channels, channels)] = shifted(first, r - 1, c - 1, side).astype(jnp.bfloat16)
    pump(until=1)
    w_spatial[...] = matrix(outs[1])
    pre = dot_nn(columns[...], w_spatial[...])
    pre_second[...] = pre
    second[...] = gelu(pre).astype(jnp.bfloat16)
    pump(until=2)
    w_expand[...] = matrix(outs[2])
    sums = sum_bufs[0]
    sums[...] = jnp.zeros_like(sums)

    def expand(cols):
        third = dot_nn(second[...], w_expand[:, cols])
        unit[:, cols] = third
        sums[pl.ds(0, 1), cols] = jnp.sum(third, axis=0, keepdims=True)
        sums[pl.ds(1, 1), cols] = jnp.sum(third * third, axis=0, keepdims=True)

    tile_loop(unit.shape[1], expand)
    norm_total = Total(place, sends, *sum_bufs)
    norm_total.begin()
    pump(2)
    norm_total.second()
    gains[...] = vector_total.last().astype(jnp.float32)
    pump(until=3)
    norm_total.third()
    w_embed[...] = matrix(outs[3])
    pump(1)
    totals = norm_total.last()
    mean = totals[0:1] / whole
    inv_std = lax.rsqrt(totals[1:2] / whole - mean * mean + epsilon)
    inv[...] = jnp.broadcast_to(inv_std, inv.shape)

    third_rows = count // 3

    def join(i, carry):
        at_rows = pl.ds(pl.multiple_of(i * third_rows, third_rows), third_rows)
        value = (unit[at_rows, :] - mean) * inv_std
        unit[at_rows, :] = value
        pre_joined = value * gains[0:1, :] + gains[1:2, :] + stem[at_rows, :].astype(jnp.float32)
        joined[at_rows, :] = gelu(pre_joined).astype(jnp.bfloat16)
        return carry

    lax.fori_loop(0, 3, join, 0)
    length, width = start.shape
    token = lax.broadcasted_iota(jnp.int32, (length, count), 0)
    patch = lax.broadcasted_iota(jnp.int32, (length, count), 1)
    placing[...] = jnp.where(token - patch == at[0], 1.0, 0.0).astype(jnp.bfloat16)

    def embed(cols):
        value = dot_nn(joined[...], w_embed[:, cols])
        high = value.astype(jnp.bfloat16)
        low = (value - high.astype(jnp.float32)).astype(jnp.bfloat16)
        moved = dot_nn(placing[...], high) + dot_nn(placing[...], low)
        start[:, cols] = tokens[:, cols].astype(jnp.float32) + moved

    tile_loop(width, embed)
    gain = gains[2:3, :width]

    def norm(i, carry):
        at_rows = pl.ds(pl.multiple_of(i * 128, 128), 128)
        value = start[at_rows, :]
        centred = value - jnp.mean(value, axis=-1, keepdims=True)
        scale = lax.rsqrt(jnp.mean(centred * centred, axis=-1, keepdims=True) + epsilon)
        normed[at_rows, :] = (centred * scale * gain).astype(jnp.bfloat16)
        return carry

    lax.fori_loop(0, length // 128, norm, 0)
    pump(until=4)
    w_qkv[...] = matrix(outs[4])

    def project(cols):
        packed[:, cols] = dot_nn(normed[...], w_qkv[:, cols]).astype(jnp.bfloat16)

    tile_loop(packed.shape[1], project)
    pump()
    sends.finish()


def front(first_at, vectors, stem, tokens, shards, side, collective_id):
    wide, narrow = lax.axis_size("wide"), lax.axis_size("narrow")
    lines, rows = wide // 2, narrow // 2
    devices = wide * narrow
    number = len(shards)
    pieces = []
    for i, s in enumerate(shards):
        cuts = 2 if i >= 6 else 1
        for k in range(cuts):
            pieces.append((i, k * s.shape[1] // cuts, s.shape[1] // cuts))
    copies = len(pieces) * gather_copies(lines, rows) + 2 * total_copies(lines, rows)
    count, length = side * side, tokens.shape[0]
    mid = shards[0].shape[1]
    wide_in = stem.shape[1]
    f32, bf16 = jnp.float32, jnp.bfloat16
    gathered = [jax.ShapeDtypeStruct((lines, 2, rows, 2) + s.shape, s.dtype) for s in shards]
    kept = [
        ((16, 1024), f32),
        ((count, mid), f32),
        ((count, 9 * mid), bf16),
        ((count, mid), f32),
        ((count, mid), bf16),
        ((count, wide_in), f32),
        ((8, wide_in), f32),
        ((count, wide_in), bf16),
        ((length, D), f32),
        ((length, D), bf16),
        ((length, 3 * D), bf16),
    ]
    vmem = pl.BlockSpec(memory_space=pltpu.VMEM)
    anywhere = pl.BlockSpec(memory_space=pl.ANY)
    scratch = [pltpu.VMEM((s.shape[0] * devices, s.shape[1]), bf16) for s in shards[:5]]
    scratch += [pltpu.VMEM((length, count), bf16)]
    scratch += total_buffers(lines, rows, (16, 1024), bf16)
    scratch += total_buffers(lines, rows, (8, 1024), f32)
    scratch += [pltpu.SemaphoreType.DMA((copies,)), pltpu.SemaphoreType.DMA((copies,)), pltpu.SemaphoreType.DMA((len(pieces),))]
    results = pl.pallas_call(
        functools.partial(front_kernel, lines, rows, side, float(count * devices), pieces, number),
        out_shape=gathered + [jax.ShapeDtypeStruct(s, d) for s, d in kept],
        in_specs=[pl.BlockSpec(memory_space=pltpu.SMEM)] + [vmem] * (FRONT_VECTORS + 2) + [anywhere] * number,
        out_specs=[vmem] * 5 + [anywhere] * (number - 5) + [vmem] * len(kept),
        scratch_shapes=scratch,
        compiler_params=pltpu.CompilerParams(collective_id=collective_id, has_side_effects=True, vmem_limit_bytes=60 * 2**20),
        cost_estimate=pl.CostEstimate(flops=6 * 10**9, bytes_accessed=7 * 10**7, transcendentals=10**6),
        name="front",
    )(first_at, *vectors, stem, tokens, *shards)
    return results[:number], results[number:]


def scatter_copies(lines, rows):
    return 1 + (rows - 1) + 1 + 1 + (rows - 1) + (lines - 1)


def add_loop(lead, fn):
    total = 1
    for size in lead:
        total *= size

    def body(i, carry):
        index = []
        for size in reversed(lead):
            index.append(lax.rem(i, size))
            i = i // size
        fn(tuple(reversed(index)))
        return carry

    lax.fori_loop(0, total, body, 0)


def plus(*terms):
    total = terms[0].astype(jnp.float32)
    for term in terms[1:]:
        total = total + term.astype(jnp.float32)
    return total


class Scatter:
    def __init__(self, place, sends, full, out, buffers):
        self.p, self.s, self.full, self.out = place, sends, full, out
        self.other, self.low1, self.high1, self.low2, self.high2, self.line0, self.lines_in = buffers
        cols = full.shape[-1]
        cut = cols // 256 * 128
        self.low, self.high = pl.ds(0, cut), pl.ds(cut, cols - cut)

    def begin(self):
        core = self.p.core
        self.stage = [self.s.start(self.full.at[:, :, :, 1 - core], self.other, self.p.device(core=1 - core))]

    def second(self):
        p, full, dtype = self.p, self.full, self.full.dtype
        for copy in self.stage:
            copy.wait_recv()

        def add(i):
            l, x, y = i
            full[l, x, y, p.core] = plus(full[l, x, y, p.core], self.other[l, x, y]).astype(dtype)

        add_loop(self.other.shape[:3], add)
        self.stage = [self.s.start(full.at[:, 1 - p.side, :, p.core, :, self.high], self.high1, p.device(side=1 - p.side))]
        for k in range(1, p.rows):
            to = p.row_peer(k)
            self.stage.append(self.s.start(full.at[:, :, to, p.core, :, self.low], self.low1.at[k - 1], p.device(row=to)))

    def third(self):
        p, full, dtype = self.p, self.full, self.full.dtype
        for copy in self.stage:
            copy.wait_recv()

        def add_low(i):
            l, x = i
            terms = [full[l, x, p.row, p.core, :, self.low]] + [self.low1[k, l, x] for k in range(p.rows - 1)]
            full[l, x, p.row, p.core, :, self.low] = plus(*terms).astype(dtype)

        def add_high(i):
            l, y = i
            full[l, p.side, y, p.core, :, self.high] = plus(full[l, p.side, y, p.core, :, self.high], self.high1[l, y]).astype(dtype)

        add_loop((p.lines, 2), add_low)
        add_loop((p.lines, p.rows), add_high)
        self.stage = [self.s.start(full.at[:, 1 - p.side, p.row, p.core, :, self.low], self.low2, p.device(side=1 - p.side))]
        for k in range(1, p.rows):
            to = p.row_peer(k)
            self.stage.append(self.s.start(full.at[:, p.side, to, p.core, :, self.high], self.high2.at[k - 1], p.device(row=to)))

    def fourth(self):
        p, full, dtype = self.p, self.full, self.full.dtype
        for copy in self.stage:
            copy.wait_recv()

        def add(i):
            (l,) = i
            self.line0[l, :, self.low] = plus(full[l, p.side, p.row, p.core, :, self.low], self.low2[l]).astype(dtype)
            terms = [full[l, p.side, p.row, p.core, :, self.high]] + [self.high2[k, l] for k in range(p.rows - 1)]
            self.line0[l, :, self.high] = plus(*terms).astype(dtype)

        add_loop((p.lines,), add)
        self.stage = []
        for k in range(1, p.lines):
            to = p.line_peer(k)
            self.stage.append(self.s.start(self.line0.at[to], self.lines_in.at[k - 1], p.device(line=to)))

    def last(self):
        p = self.p
        for copy in self.stage:
            copy.wait_recv()
        self.out[...] = plus(self.line0[p.line], *[self.lines_in[k] for k in range(p.lines - 1)])


def scatter_buffers(lines, rows, r, c, dtype):
    low = c // 256 * 128
    high = c - low
    return [
        pltpu.VMEM((lines, 2, rows, r, c), dtype),
        pltpu.VMEM((max(rows - 1, 1), lines, 2, r, low), dtype),
        pltpu.VMEM((lines, rows, r, high), dtype),
        pltpu.VMEM((lines, r, low), dtype),
        pltpu.VMEM((max(rows - 1, 1), lines, r, high), dtype),
        pltpu.VMEM((lines, r, c), dtype),
        pltpu.VMEM((max(lines - 1, 1), r, c), dtype),
    ]


NBUF = 7


def tile_loop(width, fn):
    full = width // 256

    def body(j, carry):
        fn(pl.ds(pl.multiple_of(j * 256, 256), 256))
        return carry

    lax.fori_loop(0, full, body, 0)
    if width % 256:
        fn(pl.ds(full * 256, width % 256))


def finish_kernel(lines, rows, products, given, *refs):
    refs = list(refs)

    def take(n):
        out = refs[:n]
        del refs[:n]
        return out

    number = len(products)
    lefts, rights, ready = take(number), take(number), take(given)
    count = number + given
    outs = take(count)
    fulls, buffers = take(count), take(count * NBUF)
    xbuf, gbuf, xsem, gsem, ready_sem, send_sems, recv_sems = refs
    place = Place(lines, rows)
    place.greet()
    sends = Sends(send_sems, recv_sems)
    parts = [Scatter(place, sends, fulls[i], outs[i], buffers[NBUF * i : NBUF * (i + 1)]) for i in range(count)]
    ready_copies = [pltpu.make_async_copy(ready[i], fulls[number + i], ready_sem.at[i]) for i in range(given)]
    for copy in ready_copies:
        copy.start()

    core = place.core
    tasks = []
    for a, (kind, width) in enumerate(products):
        if kind == "rows":
            tasks.append((a, 0, None, None))
        else:
            for c in (1 - core, core):
                for y in range(rows):
                    pitch = rights[a].shape[1] // rows
                    start = y * pitch + c * (pitch - width)
                    tasks.append((a, start, y, c))

    def fetch_right(t):
        a, start, y, c = tasks[t]
        width = products[a][1]
        start = pl.multiple_of(jnp.int32(start), 128)
        return pltpu.make_async_copy(rights[a].at[:, pl.ds(start, width)], gbuf.at[t % 2, :, pl.ds(0, width)], gsem.at[t % 2])

    def fetch_left(a):
        return pltpu.make_async_copy(lefts[a], xbuf.at[a % 2], xsem.at[a % 2])

    fetch_left(0).start()
    fetch_right(0).start()

    def multiply(t):
        a, start, y, c = tasks[t]
        kind, width = products[a]
        if t + 1 < len(tasks):
            fetch_right(t + 1).start()
            if tasks[t + 1][0] != a:
                fetch_left(a + 1).start()
        if t == 0 or tasks[t - 1][0] != a:
            fetch_left(a).wait()
        fetch_right(t).wait()
        full = fulls[a]

        def tile(cols):
            block = dot_nn(xbuf[a % 2], gbuf[t % 2, :, cols])
            n = block.shape[1]
            if kind == "rows":
                full[:, :, :, :, :, cols] = block.reshape(lines, 2, rows, 2, -1, n).astype(full.dtype)
            else:
                full[:, :, y, c, :, cols] = block.reshape(lines, 2, -1, n).astype(full.dtype)

        tile_loop(width, tile)

    order = [number + i for i in range(given)] + list(range(number))
    pending = []

    def advance():
        for item in list(pending):
            getattr(parts[item[0]], item[1].pop(0))()
            if not item[1]:
                pending.remove(item)

    for i in range(given):
        ready_copies[i].wait()
        parts[number + i].begin()
        pending.append((number + i, ["second", "third", "fourth", "last"]))
    for t, (a, start, y, c) in enumerate(tasks):
        multiply(t)
        sent = products[a][0] == "rows" or (c is not core and y == rows - 1)
        if sent:
            parts[a].begin()
        done = t + 1 == len(tasks) or tasks[t + 1][0] != a
        if done or sent:
            advance()
        if done:
            pending.append((a, ["second", "third", "fourth", "last"]))
    while pending:
        advance()
    sends.finish()


def finish(products, given, collective_id):
    wide, narrow = lax.axis_size("wide"), lax.axis_size("narrow")
    lines, rows = wide // 2, narrow // 2
    shapes, plan = [], []
    for left, right, kind in products:
        m, n = left.shape[0], right.shape[1]
        if kind == "rows":
            width = n
            shapes.append((lines, 2, rows, 2, m // (4 * lines * rows), n))
        else:
            width = -(-(n // (2 * rows)) // 128) * 128
            shapes.append((lines, 2, rows, 2, m // (2 * lines), width))
        plan.append((kind, width))
    shapes += [g.shape for g in given]
    count = len(shapes)
    copies = count * scatter_copies(lines, rows)
    dtype = jnp.bfloat16
    scratch = [pltpu.VMEM(s, dtype) for s in shapes]
    for s in shapes:
        scratch += scatter_buffers(lines, rows, s[-2], s[-1], dtype)
    m, t = products[0][0].shape
    widest = max(width for _, width in plan)
    scratch += [
        pltpu.VMEM((2, m, t), dtype),
        pltpu.VMEM((2, t, widest), dtype),
        pltpu.SemaphoreType.DMA((2,)),
        pltpu.SemaphoreType.DMA((2,)),
        pltpu.SemaphoreType.DMA((max(len(given), 1),)),
        pltpu.SemaphoreType.DMA((copies,)),
        pltpu.SemaphoreType.DMA((copies,)),
    ]
    ins = [p[0] for p in products] + [p[1] for p in products] + list(given)
    return pl.pallas_call(
        functools.partial(finish_kernel, lines, rows, plan, len(given)),
        out_shape=[jax.ShapeDtypeStruct(s[-2:], jnp.float32) for s in shapes],
        in_specs=[pl.BlockSpec(memory_space=pl.ANY)] * len(ins),
        out_specs=[pl.BlockSpec(memory_space=pltpu.VMEM)] * count,
        scratch_shapes=scratch,
        compiler_params=pltpu.CompilerParams(collective_id=collective_id, has_side_effects=True, vmem_limit_bytes=60 * 2**20),
        cost_estimate=pl.CostEstimate(flops=14 * 10**9, bytes_accessed=6 * 10**7, transcendentals=0),
        name="finish",
    )(*ins)


def total_kernel(lines, rows, x_ref, o_ref, core_in, plane, line_in, send_sems, recv_sems):
    p = Place(lines, rows)
    barrier = pltpu.get_barrier_semaphore()
    plane_peers = [(k // rows, k % rows) for k in range(1, 2 * rows)]
    targets = [p.device(core=1 - p.core)]
    targets += [p.device(side=lax.rem(p.side + a, 2), row=p.row_peer(b)) for a, b in plane_peers]
    targets += [p.device(line=p.line_peer(k)) for k in range(1, lines)]
    for target in targets:
        pl.semaphore_signal(barrier, inc=1, device_id=target, device_id_type=MESH)
    pl.semaphore_wait(barrier, len(targets))
    sends = Sends(send_sems, recv_sems)
    sends.start(x_ref, core_in, targets[0]).wait_recv()
    here = p.side * rows + p.row
    plane[here] = x_ref[...] + core_in[...]
    stage = [sends.start(plane.at[here], plane.at[here], t) for t in targets[1 : 2 * rows]]
    for copy in stage:
        copy.wait_recv()
    total = plane[0]
    for k in range(1, 2 * rows):
        total = total + plane[k]
    line_in[p.line] = total
    stage = [sends.start(line_in.at[p.line], line_in.at[p.line], t) for t in targets[2 * rows :]]
    for copy in stage:
        copy.wait_recv()
    total = line_in[0]
    for k in range(1, lines):
        total = total + line_in[k]
    o_ref[...] = total
    sends.finish()


def total_sum(x, collective_id):
    wide, narrow = lax.axis_size("wide"), lax.axis_size("narrow")
    lines, rows = wide // 2, narrow // 2
    copies = 1 + 2 * rows - 1 + lines - 1
    return pl.pallas_call(
        functools.partial(total_kernel, lines, rows),
        out_shape=jax.ShapeDtypeStruct(x.shape, x.dtype),
        in_specs=[pl.BlockSpec(memory_space=pltpu.VMEM)],
        out_specs=pl.BlockSpec(memory_space=pltpu.VMEM),
        scratch_shapes=[
            pltpu.VMEM(x.shape, x.dtype),
            pltpu.VMEM((2 * rows,) + x.shape, x.dtype),
            pltpu.VMEM((lines,) + x.shape, x.dtype),
            pltpu.SemaphoreType.DMA((copies,)),
            pltpu.SemaphoreType.DMA((copies,)),
        ],
        compiler_params=pltpu.CompilerParams(collective_id=collective_id, has_side_effects=True),
        cost_estimate=pl.CostEstimate(flops=0, bytes_accessed=10**6, transcendentals=0),
        name="total_sum",
    )(x)


def local(
    tokens,
    features,
    segments,
    positions,
    w_qkv,
    w_out,
    w_up,
    w_down,
    gain_pre,
    gain_attn,
    gain_mid,
    gain_ffn,
    rel_table,
    head_scale,
    w_reduce,
    w_spatial,
    w_expand,
    w_embed,
    bn_gain,
    bn_shift,
    d_out,
):
    both = ("wide", "narrow")
    devices = lax.axis_size(both)
    me = lax.axis_index("wide") * lax.axis_size("narrow") + lax.axis_index("narrow")
    rows, length = (segments.shape[0], segments.shape[1])
    images, side = (features.shape[0], features.shape[1])
    patch_count = images * side * side
    whole = patch_count * devices
    first_at = positions[0, 0]
    stem_in = features.reshape(patch_count, features.shape[3])
    vectors = [item.reshape(1, -1) for item in (gain_pre, gain_attn, gain_mid, gain_ffn, bn_gain, bn_shift)]
    gathered, kept = front(
        positions[0, :1],
        vectors + [rel_table],
        stem_in,
        tokens,
        [w_reduce, w_spatial, w_expand, w_embed, w_qkv, w_out, w_up, w_down],
        side,
        1,
    )
    full_reduce, full_spatial, full_expand, full_embed, full_qkv, full_out, full_up, full_down = (
        item.reshape(-1, item.shape[-1]) for item in gathered
    )
    gains, pre_first, columns, pre_second, second, bn_unit, bn_inv, joined, start, normed0_low, packed = kept
    full_bn_gain, full_bn_shift = gains[0], gains[1]
    full_pre, full_attn, full_mid = gains[2, :D], gains[3, :D], gains[4, :D]
    full_ffn = gains[5:8].reshape(-1)
    full_table = gains[8:11].reshape(HEADS, 2 * RSPAN)
    bn_inv = bn_inv[0]
    pre_joined = bn_unit * full_bn_gain + full_bn_shift + stem_in.astype(jnp.float32)
    unused, unit0, inv0 = layer_norm(start, full_pre)
    win = windows(segments)
    attended, logsums, bias = attend(packed, segments, bias_strips(full_table), win)
    scale_row = jnp.repeat(head_scale, HDIM)[None, :]
    scaled = attended * scale_row
    mixed_in, unit1, inv1 = layer_norm(scaled, full_attn.astype(jnp.float32))
    mixed_low = mixed_in.astype(jnp.bfloat16)
    middle = start + product(mixed_low, full_out)
    normed2, unit2, inv2 = layer_norm(middle, full_mid.astype(jnp.float32))
    normed2_low = normed2.astype(jnp.bfloat16)
    pre_up = product(normed2_low, full_up)
    activ = smooth(pre_up)
    narrowed, unit3, inv3 = layer_norm(activ, full_ffn.astype(jnp.float32))
    narrowed_low = narrowed.astype(jnp.bfloat16)
    result = middle + product(narrowed_low, full_down)
    mixed = result.astype(jnp.bfloat16)
    grad_result = d_out.astype(jnp.float32)
    grad_narrowed = product_nt(d_out, full_down)
    grad_activ, grad_gain_ffn = layer_norm_back(
        grad_narrowed, unit3, inv3, full_ffn.astype(jnp.float32)
    )
    grad_pre_up = smooth_back(pre_up, grad_activ).astype(jnp.bfloat16)
    grad_normed2 = product_nt(grad_pre_up, full_up)
    grad_mid_in, grad_gain_mid = layer_norm_back(
        grad_normed2, unit2, inv2, full_mid.astype(jnp.float32)
    )
    grad_middle = grad_result + grad_mid_in
    grad_branch = grad_middle.astype(jnp.bfloat16)
    grad_mixed_in = product_nt(grad_branch, full_out)
    grad_scaled, grad_gain_attn = layer_norm_back(
        grad_mixed_in, unit1, inv1, full_attn.astype(jnp.float32)
    )
    grad_head_local = jnp.sum(jnp.sum(grad_scaled * attended, axis=0).reshape(HEADS, HDIM), axis=1)
    grad_attended = (grad_scaled * scale_row).astype(jnp.bfloat16)
    grad_packed, grad_strips = attend_back(packed, grad_attended, attended, segments, bias, logsums, win)
    grad_table = table_from_strips(grad_strips)
    grad_normed0 = product_nt(grad_packed, full_qkv)
    grad_start_in, grad_gain_pre = layer_norm_back(
        grad_normed0, unit0, inv0, full_pre.astype(jnp.float32)
    )
    grad_tokens = grad_middle + grad_start_in
    grad_embedded = lax.dynamic_slice_in_dim(grad_tokens, first_at, patch_count, 0).astype(jnp.bfloat16)
    grad_w_embed = product_tn(joined, grad_embedded)
    grad_joined = product_nt(grad_embedded, full_embed)
    grad_pre_joined = smooth_back(pre_joined, grad_joined)
    grad_bn_shift = jnp.sum(grad_pre_joined, axis=0)
    grad_bn_gain = jnp.sum(grad_pre_joined * bn_unit, axis=0)
    smalls = (
        grad_gain_pre,
        grad_gain_attn,
        grad_gain_mid,
        grad_gain_ffn,
        grad_bn_gain,
        grad_bn_shift,
        grad_table.reshape(-1),
        grad_head_local,
    )
    small = jnp.concatenate(smalls)
    small = jnp.pad(small, (0, -small.shape[0] % 1024)).reshape(-1, 128)
    small = total_sum(small, 4).reshape(-1)
    totals, at = [], 0
    for item in smalls:
        totals.append(small[at : at + item.shape[0]])
        at += item.shape[0]
    sum_pre, sum_attn, sum_mid, sum_ffn, sum_bn_gain, sum_bn_shift = (
        lax.dynamic_slice_in_dim(item, me * (item.shape[0] // devices), item.shape[0] // devices)
        for item in totals[:6]
    )
    breadth = 2 * RSPAN // devices
    sum_table = lax.dynamic_slice_in_dim(totals[6].reshape(HEADS, -1), me * breadth, breadth, 1)
    grad_head = totals[7]
    bn_gain_row = full_bn_gain.astype(jnp.float32)
    grad_unit = grad_pre_joined * bn_gain_row
    sum_unit, sum_cross = totals[5] * bn_gain_row, totals[4] * bn_gain_row
    grad_third = (bn_inv * (grad_unit - sum_unit / whole - bn_unit * (sum_cross / whole))).astype(
        jnp.bfloat16
    )
    grad_w_expand = product_tn(second, grad_third)
    grad_second = product_nt(grad_third, full_expand)
    grad_pre_second = smooth_back(pre_second, grad_second).astype(jnp.bfloat16)
    grad_w_spatial = product_tn(columns, grad_pre_second)
    grad_columns = product_nt(grad_pre_second, full_spatial)
    grad_first = fold(grad_columns.reshape(images, side, side, -1)).reshape(patch_count, -1)
    grad_pre_first = smooth_back(pre_first, grad_first).astype(jnp.bfloat16)
    grad_w_reduce = product_tn(stem_in, grad_pre_first)
    grad_features = (grad_pre_joined + product_nt(grad_pre_first, full_reduce)).reshape(
        features.shape
    )
    lines, planes = lax.axis_size("wide") // 2, lax.axis_size("narrow") // 2

    def by_rows(grad):
        return grad.astype(jnp.bfloat16).reshape(lines, 2, planes, 2, -1, grad.shape[1])

    sum_down, sum_up, sum_qkv, sum_out, sum_embed, sum_expand, sum_spatial, sum_reduce = finish(
        [
            (d_out.T, narrowed_low, "blocks"),
            (normed2_low.T, grad_pre_up, "blocks"),
            (normed0_low.T, grad_packed, "blocks"),
            (mixed_low.T, grad_branch, "rows"),
        ],
        [by_rows(grad_w_embed), by_rows(grad_w_expand), by_rows(grad_w_spatial), by_rows(grad_w_reduce)],
        2,
    )
    sum_down = sum_down.T
    width = 3 * D // (2 * planes)
    sum_qkv = jnp.where(
        lax.axis_index("narrow") % 2 == 0, sum_qkv[:, :width], sum_qkv[:, sum_qkv.shape[1] - width :]
    )
    return (
        mixed,
        grad_tokens,
        grad_features,
        sum_qkv,
        sum_out,
        sum_up,
        sum_down,
        sum_pre,
        sum_attn,
        sum_mid,
        sum_ffn,
        sum_table,
        grad_head,
        sum_reduce,
        sum_spatial,
        sum_expand,
        sum_embed,
        sum_bn_gain,
        sum_bn_shift,
    )


def solution(mesh):
    placed = (
        P(("wide", "narrow"), None),
        P(("wide", "narrow"), None, None, None),
        P(("wide", "narrow"), None),
        P(("wide", "narrow"), None),
        P(("wide", "narrow"), None),
        P(("wide", "narrow"), None),
        P(("wide", "narrow"), None),
        P(("wide", "narrow"), None),
        P(("wide", "narrow")),
        P(("wide", "narrow")),
        P(("wide", "narrow")),
        P(("wide", "narrow")),
        P(None, ("wide", "narrow")),
        P(),
        P(("wide", "narrow"), None),
        P(("wide", "narrow"), None),
        P(("wide", "narrow"), None),
        P(("wide", "narrow"), None),
        P(("wide", "narrow")),
        P(("wide", "narrow")),
        P(("wide", "narrow"), None),
    )
    return jax.shard_map(
        local,
        mesh=mesh,
        in_specs=placed,
        out_specs=(
            P(("wide", "narrow"), None),
            P(("wide", "narrow"), None),
            P(("wide", "narrow"), None, None, None),
            P("wide", "narrow"),
            P(("wide", "narrow"), None),
            P("wide", "narrow"),
            P("narrow", "wide"),
            P(("wide", "narrow")),
            P(("wide", "narrow")),
            P(("wide", "narrow")),
            P(("wide", "narrow")),
            P(None, ("wide", "narrow")),
            P(),
            P(("wide", "narrow"), None),
            P(("wide", "narrow"), None),
            P(("wide", "narrow"), None),
            P(("wide", "narrow"), None),
            P(("wide", "narrow")),
            P(("wide", "narrow")),
        ),
        check_vma=False,
    )
```

```python
import functools

import jax
import jax.numpy as jnp
from jax import lax
from jax.experimental import pallas as pl
from jax.experimental.pallas import tpu as pltpu
from jax.sharding import PartitionSpec as P

D = 768
HEADS = 12
HDIM = 64
RSPAN = 128


epsilon = 1e-05


def product(lhs_matrix, rhs_matrix):
    return jnp.dot(lhs_matrix, rhs_matrix, preferred_element_type=jnp.float32)


def product_tn(lhs_matrix, rhs_matrix):
    return lax.dot_general(
        lhs_matrix, rhs_matrix, (((0,), (0,)), ((), ())), preferred_element_type=jnp.float32
    )


def product_nt(lhs_matrix, rhs_matrix):
    return lax.dot_general(
        lhs_matrix, rhs_matrix, (((1,), (1,)), ((), ())), preferred_element_type=jnp.float32
    )


def layer_norm(values, gain):
    average = jnp.mean(values, axis=-1, keepdims=True)
    centred = values - average
    inv_std = lax.rsqrt(jnp.mean(centred * centred, axis=-1, keepdims=True) + epsilon)
    unit_rows = centred * inv_std
    return (unit_rows * gain, unit_rows, inv_std)


def layer_norm_back(cotangent, unit_rows, inv_std, gain):
    weighted = cotangent * gain
    inner = (
        weighted
        - jnp.mean(weighted, axis=-1, keepdims=True)
        - unit_rows * jnp.mean(weighted * unit_rows, axis=-1, keepdims=True)
    )
    return (inv_std * inner, jnp.sum(cotangent * unit_rows, axis=0))


def smooth(values):
    return jax.nn.gelu(values, approximate=True)


def smooth_back(values, cotangent):
    unused, pullback = jax.vjp(smooth, values)
    return pullback(cotangent)[0]


def unfold(grid):
    side = grid.shape[1]
    padded = jnp.pad(grid, ((0, 0), (1, 1), (1, 1), (0, 0)))
    pieces = [
        padded[:, row_off : row_off + side, col_off : col_off + side, :]
        for row_off in range(3)
        for col_off in range(3)
    ]
    return jnp.concatenate(pieces, axis=-1)


def fold(columns):
    channels = columns.shape[-1] // 9
    side = columns.shape[1]
    total = jnp.zeros((columns.shape[0], side + 2, side + 2, channels), jnp.float32)
    for row_off in range(3):
        for col_off in range(3):
            which = row_off * 3 + col_off
            piece = columns[..., which * channels : (which + 1) * channels]
            total = total + jnp.pad(
                piece, ((0, 0), (row_off, 2 - row_off), (col_off, 2 - col_off), (0, 0))
            )
    return total[:, 1:-1, 1:-1, :]


PAIRS = HEADS // 2
BLK = 128
NEG = -1e30


def dot_nn(a, b):
    return lax.dot_general(a, b, (((1,), (0,)), ((), ())), preferred_element_type=jnp.float32)


def dot_nt(a, b):
    return lax.dot_general(a, b, (((1,), (1,)), ((), ())), preferred_element_type=jnp.float32)


def split_heads(pair, scale):
    lane = lax.broadcasted_iota(jnp.int32, pair.shape, 1)
    vals = pair * jnp.asarray(scale, pair.dtype)
    zero = jnp.zeros_like(vals)
    return jnp.concatenate([jnp.where(lane < HDIM, vals, zero), jnp.where(lane < HDIM, zero, vals)], axis=0)


def join_heads(both):
    row = lax.broadcasted_iota(jnp.int32, (2 * HDIM, BLK), 0)
    return jnp.where(row < HDIM, both[:, :BLK], both[:, BLK:])


def bias_strips(table):
    rev = jnp.flip(table.astype(jnp.float32), axis=1)
    first, last = rev[:, 255:256], rev[:, 0:1]
    below = jnp.concatenate([jnp.broadcast_to(first, (HEADS, 129)), rev[:, 128:255]], axis=1)
    middle = jnp.concatenate([rev[:, 127:256], rev[:, 0:127]], axis=1)
    above = jnp.concatenate([last, rev[:, 0:127], jnp.broadcast_to(last, (HEADS, 128))], axis=1)
    low = jnp.broadcast_to(first, (HEADS, 256))
    high = jnp.broadcast_to(last, (HEADS, 256))
    return jnp.stack([low, below, middle, above, high], axis=1)


def table_from_strips(sums):
    low, below, middle, above, high = (sums[:, i] for i in range(5))
    total = jnp.concatenate([middle[:, 129:256], middle[:, 0:129]], axis=1)
    zero = jnp.zeros((HEADS, 127), jnp.float32)
    first = jnp.sum(low, axis=1, keepdims=True) + jnp.sum(below[:, :129], axis=1, keepdims=True)
    last = jnp.sum(high, axis=1, keepdims=True) + above[:, 0:1] + jnp.sum(above[:, 128:], axis=1, keepdims=True)
    total = total + jnp.concatenate([jnp.zeros((HEADS, 128), jnp.float32), below[:, 129:], first], axis=1)
    head = jnp.concatenate([above[:, 1:128], jnp.zeros((HEADS, 129), jnp.float32)], axis=1)
    total = total + head + jnp.concatenate([last, jnp.zeros((HEADS, 255), jnp.float32)], axis=1)
    return jnp.flip(total, axis=1)


def windows(segments):
    seg = segments.reshape(-1)
    starts = seg[::BLK]
    ends = seg[BLK - 1 :: BLK]
    low = jnp.sum((seg[None, :] < starts[:, None]).astype(jnp.int32), axis=1) // BLK
    high = (jnp.sum((seg[None, :] <= ends[:, None]).astype(jnp.int32), axis=1) + BLK - 1) // BLK
    return jnp.stack([low, high])


def attend_kernel(win, packed, segk, segq, strips, out, logsum, bias, vt, qm, acc, stat):
    i = pl.program_id(0)

    @pl.when(i == 0)
    def _():
        for hp in range(PAIRS):
            vt[pl.ds(hp * 128, 128), :] = packed[:, pl.ds(2 * D + hp * 128, 128)].T
            for d in range(5):
                for half in range(2):
                    row = strips[2 * hp + half, pl.ds(d, 1), :]
                    tile = jnp.broadcast_to(row, (BLK, 256))
                    if 0 < d < 4:
                        tile = pltpu.roll(tile, 0, 1, stride=1, stride_axis=0)
                    bias[hp, d, :, pl.ds(half * BLK, BLK)] = tile[:, :BLK]

    rows = pl.ds(pl.multiple_of(i * BLK, BLK), BLK)
    for hp in range(PAIRS):
        qm[hp] = split_heads(packed[rows, pl.ds(hp * 128, 128)], HDIM ** -0.5)
        acc[hp] = jnp.zeros((128, 256), jnp.float32)
        stat[hp, 0] = jnp.full((1, 256), NEG, jnp.float32)
        stat[hp, 1] = jnp.zeros((1, 256), jnp.float32)
    sq = segq[:, rows]
    sq2 = jnp.concatenate([sq, sq], axis=1)

    def body(kb, carry):
        keys = pl.ds(pl.multiple_of(kb * BLK, BLK), BLK)
        allowed = segk[keys, :] == sq2
        d = jnp.clip(kb - i, -2, 2) + 2
        for hp in range(PAIRS):
            s = dot_nt(packed[keys, pl.ds(D + hp * 128, 128)], qm[hp])
            s = jnp.where(allowed, s + bias[hp, d], NEG)
            old = stat[hp, 0]
            new = jnp.maximum(old, jnp.max(s, axis=0, keepdims=True))
            p = jnp.exp(s - new)
            alpha = jnp.exp(old - new)
            stat[hp, 0] = new
            stat[hp, 1] = stat[hp, 1] * alpha + jnp.sum(p, axis=0, keepdims=True)
            acc[hp] = acc[hp] * alpha + dot_nn(vt[pl.ds(hp * 128, 128), keys], p.astype(jnp.bfloat16))
        return carry

    lax.fori_loop(win[0, i], win[1, i], body, 0)
    for hp in range(PAIRS):
        total = stat[hp, 1]
        out[:, pl.ds(hp * 128, 128)] = join_heads(acc[hp] / total).T
        logsum[0, pl.ds(hp, 1), :] = stat[hp, 0] + jnp.log(total)


def attend(packed, segments, strips, win):
    length = packed.shape[0]
    blocks = length // BLK
    seg = segments.reshape(1, length)
    whole = lambda shape: pl.BlockSpec(shape, lambda i, w: (0,) * len(shape))
    return pl.pallas_call(
        attend_kernel,
        out_shape=(
            jax.ShapeDtypeStruct((length, D), jnp.float32),
            jax.ShapeDtypeStruct((blocks, PAIRS, 256), jnp.float32),
            jax.ShapeDtypeStruct((PAIRS, 5, BLK, 256), jnp.float32),
        ),
        grid_spec=pltpu.PrefetchScalarGridSpec(
            num_scalar_prefetch=1,
            grid=(blocks,),
            in_specs=[whole((length, 3 * D)), whole((length, 1)), whole((1, length)), whole((HEADS, 5, 256))],
            out_specs=(
                pl.BlockSpec((BLK, D), lambda i, w: (i, 0)),
                pl.BlockSpec((1, PAIRS, 256), lambda i, w: (i, 0, 0)),
                whole((PAIRS, 5, BLK, 256)),
            ),
            scratch_shapes=[
                pltpu.VMEM((D, length), jnp.bfloat16),
                pltpu.VMEM((PAIRS, 256, 128), jnp.bfloat16),
                pltpu.VMEM((PAIRS, 128, 256), jnp.float32),
                pltpu.VMEM((PAIRS, 2, 1, 256), jnp.float32),
            ],
        ),
        compiler_params=pltpu.CompilerParams(vmem_limit_bytes=48 * 2**20),
        cost_estimate=pl.CostEstimate(flops=2 * 10**10, bytes_accessed=10**7, transcendentals=6 * 10**6),
        name="attend",
    )(win, packed, seg.reshape(length, 1), seg, strips)


def unskew(tile):
    row = lax.broadcasted_iota(jnp.int32, tile.shape, 0)
    width = tile.shape[1]
    for bit in range(7):
        step = 1 << bit
        tile = jnp.where((row & step) != 0, pltpu.roll(tile, width - step, 1), tile)
    return tile


def attend_back_kernel(win, packed, grads, attended, segk, segq, bias, logsum, out, tab, kt, qm, om, dqt, dk, dv, gt):
    i = pl.program_id(0)
    last = pl.num_programs(0) - 1

    @pl.when(i == 0)
    def _():
        for hp in range(PAIRS):
            kt[pl.ds(hp * 128, 128), :] = packed[:, pl.ds(D + hp * 128, 128)].T
        dk[...] = jnp.zeros_like(dk)
        dv[...] = jnp.zeros_like(dv)
        gt[...] = jnp.zeros_like(gt)

    rows = pl.ds(pl.multiple_of(i * BLK, BLK), BLK)
    dots = []
    for hp in range(PAIRS):
        cols = pl.ds(hp * 128, 128)
        qm[hp] = split_heads(packed[rows, cols], HDIM ** -0.5)
        om[hp] = split_heads(grads[:, cols], 1.0)
        cross = (grads[:, cols].astype(jnp.float32) * attended[:, cols]).T
        dots.append(jnp.concatenate([
            jnp.sum(cross[:HDIM], axis=0, keepdims=True),
            jnp.sum(cross[HDIM:], axis=0, keepdims=True)], axis=1))
        dqt[hp] = jnp.zeros((128, 256), jnp.float32)
    sq = segq[:, rows]
    sq2 = jnp.concatenate([sq, sq], axis=1)

    def body(kb, carry):
        keys = pl.ds(pl.multiple_of(kb * BLK, BLK), BLK)
        allowed = segk[keys, :] == sq2
        d = jnp.clip(kb - i, -2, 2) + 2
        for hp in range(PAIRS):
            cols = pl.ds(hp * 128, 128)
            s = dot_nt(packed[keys, pl.ds(D + hp * 128, 128)], qm[hp]) + bias[hp, d]
            p = jnp.exp(jnp.where(allowed, s, NEG) - logsum[0, pl.ds(hp, 1), :])
            dp = dot_nt(packed[keys, pl.ds(2 * D + hp * 128, 128)], om[hp])
            ds = p * (dp - dots[hp])
            gt[hp, d] += ds
            low = ds.astype(jnp.bfloat16)
            dv[keys, cols] += dot_nn(p.astype(jnp.bfloat16), om[hp])
            dk[keys, cols] += dot_nn(low, qm[hp])
            dqt[hp] += dot_nn(kt[cols, keys], low)
        return carry

    lax.fori_loop(win[0, i], win[1, i], body, 0)
    for hp in range(PAIRS):
        out[rows, pl.ds(hp * 128, 128)] = (join_heads(dqt[hp]).T * (HDIM ** -0.5)).astype(jnp.bfloat16)

    @pl.when(i == last)
    def _():
        out[:, pl.ds(D, D)] = dk[...].astype(jnp.bfloat16)
        out[:, pl.ds(2 * D, D)] = dv[...].astype(jnp.bfloat16)
        for hp in range(PAIRS):
            for half in range(2):
                for d in range(5):
                    tile = gt[hp, d, :, pl.ds(half * BLK, BLK)]
                    tile = jnp.concatenate([tile, jnp.zeros_like(tile)], axis=1)
                    if 0 < d < 4:
                        tile = unskew(tile)
                    tab[2 * hp + half, pl.ds(d, 1), :] = jnp.sum(tile, axis=0, keepdims=True)


def attend_back(packed, grads, attended, segments, bias, logsum, win):
    length = packed.shape[0]
    blocks = length // BLK
    seg = segments.reshape(1, length)
    whole = lambda shape: pl.BlockSpec(shape, lambda i, w: (0,) * len(shape))
    return pl.pallas_call(
        attend_back_kernel,
        out_shape=(
            jax.ShapeDtypeStruct((length, 3 * D), jnp.bfloat16),
            jax.ShapeDtypeStruct((HEADS, 5, 256), jnp.float32),
        ),
        grid_spec=pltpu.PrefetchScalarGridSpec(
            num_scalar_prefetch=1,
            grid=(blocks,),
            in_specs=[
                whole((length, 3 * D)),
                pl.BlockSpec((BLK, D), lambda i, w: (i, 0)),
                pl.BlockSpec((BLK, D), lambda i, w: (i, 0)),
                whole((length, 1)),
                whole((1, length)),
                whole((PAIRS, 5, BLK, 256)),
                pl.BlockSpec((1, PAIRS, 256), lambda i, w: (i, 0, 0)),
            ],
            out_specs=(whole((length, 3 * D)), whole((HEADS, 5, 256))),
            scratch_shapes=[
                pltpu.VMEM((D, length), jnp.bfloat16),
                pltpu.VMEM((PAIRS, 256, 128), jnp.bfloat16),
                pltpu.VMEM((PAIRS, 256, 128), jnp.bfloat16),
                pltpu.VMEM((PAIRS, 128, 256), jnp.float32),
                pltpu.VMEM((length, D), jnp.float32),
                pltpu.VMEM((length, D), jnp.float32),
                pltpu.VMEM((PAIRS, 5, BLK, 256), jnp.float32),
            ],
        ),
        compiler_params=pltpu.CompilerParams(vmem_limit_bytes=56 * 2**20),
        cost_estimate=pl.CostEstimate(flops=5 * 10**10, bytes_accessed=2 * 10**7, transcendentals=6 * 10**6),
        name="attend_back",
    )(win, packed, grads, attended, seg.reshape(length, 1), seg, bias, logsum)


MESH = pl.DeviceIdType.MESH


class Place:
    def __init__(self, lines, rows):
        self.lines, self.rows = lines, rows
        wide, narrow = lax.axis_index("wide"), lax.axis_index("narrow")
        self.line, self.side = wide // 2, wide % 2
        self.row, self.core = narrow // 2, narrow % 2

    def device(self, line=None, side=None, row=None, core=None):
        line = self.line if line is None else line
        side = self.side if side is None else side
        row = self.row if row is None else row
        core = self.core if core is None else core
        return (line * 2 + side, row * 2 + core)

    def line_peer(self, k):
        return lax.rem(self.line + k, self.lines)

    def line_source(self, k):
        return lax.rem(self.line + self.lines - k, self.lines)

    def row_peer(self, k):
        return lax.rem(self.row + k, self.rows)

    def row_source(self, k):
        return lax.rem(self.row + self.rows - k, self.rows)

    def plane_peers(self):
        steps = [(k // self.rows, k % self.rows) for k in range(1, 2 * self.rows)]
        return [self.device(side=lax.rem(self.side + a, 2), row=self.row_peer(b)) for a, b in steps]

    def greet(self):
        barrier = pltpu.get_barrier_semaphore()
        targets = [self.device(line=self.line_peer(k)) for k in range(1, self.lines)]
        targets += self.plane_peers() + [self.device(core=1 - self.core)]
        for target in targets:
            pl.semaphore_signal(barrier, inc=1, device_id=target, device_id_type=MESH)
        pl.semaphore_wait(barrier, len(targets))


class Sends:
    def __init__(self, send_sems, recv_sems):
        self.send_sems, self.recv_sems, self.used = send_sems, recv_sems, 0
        self.started = []

    def start(self, src, dst, device):
        copy = pltpu.make_async_remote_copy(
            src_ref=src, dst_ref=dst, send_sem=self.send_sems.at[self.used], recv_sem=self.recv_sems.at[self.used],
            device_id=device, device_id_type=MESH)
        copy.start()
        self.used += 1
        self.started.append(copy)
        return copy

    def finish(self):
        for copy in self.started:
            copy.wait_send()


def gather_copies(lines, rows):
    return (lines - 1) + 1 + (rows - 1) + 1 + 1 + (rows - 1) + 1


class Gather:
    def __init__(self, place, sends, shard, out, local_sem, region, side_first):
        self.p, self.s, self.out, self.region = place, sends, out, region
        self.shard, self.local_sem, self.side_first = shard.at[region], local_sem, side_first
        self.cores = []

    def at(self, line, side, row):
        return self.out.at[(line, side, row, self.p.core) + self.region]

    def begin(self):
        p = self.p
        mine = self.at(p.line, p.side, p.row)
        self.local = pltpu.make_async_copy(self.shard, mine, self.local_sem)
        self.local.start()
        self.stage = [self.s.start(self.shard, mine, p.device(line=p.line_peer(k))) for k in range(1, p.lines)]

    def across(self, src):
        self.cores.append(self.s.start(src, src, self.p.device(core=1 - self.p.core)))

    def to_side(self, src):
        self.stage.append(self.s.start(src, src, self.p.device(side=1 - self.p.side)))

    def to_rows(self, src):
        p = self.p
        self.stage += [self.s.start(src, src, p.device(row=p.row_peer(k))) for k in range(1, p.rows)]

    def arrived(self):
        for copy in self.stage:
            copy.wait_recv()
        self.stage = []

    def second(self):
        p, every = self.p, slice(None)
        self.local.wait()
        self.arrived()
        mine = self.at(every, p.side, p.row)
        (self.to_side if self.side_first else self.to_rows)(mine)
        self.across(mine)

    def third(self):
        p, every = self.p, slice(None)
        self.arrived()
        if self.side_first:
            self.to_rows(self.at(every, every, p.row))
            self.across(self.at(every, 1 - p.side, p.row))
        else:
            self.to_side(self.at(every, p.side, every))
            for k in range(1, p.rows):
                self.across(self.at(every, p.side, p.row_source(k)))

    def fourth(self):
        p, every = self.p, slice(None)
        self.arrived()
        if self.side_first:
            for k in range(1, p.rows):
                self.across(self.at(every, every, p.row_source(k)))
        else:
            self.across(self.at(every, 1 - p.side, every))

    def last(self):
        for copy in self.cores:
            copy.wait_recv()


class HalfGather(Gather):
    def at(self, line, side, row):
        return self.out.at[line, side if self.side_first else row]

    def across(self, src):
        pass

    def third(self):
        self.arrived()

    def fourth(self):
        pass

    def last(self):
        pass


class Total:
    def __init__(self, place, sends, x, core_in, plane, line_in):
        self.p, self.s, self.x, self.core_in, self.plane, self.line_in = place, sends, x, core_in, plane, line_in

    def begin(self):
        p = self.p
        self.stage = [self.s.start(self.x, self.core_in, p.device(core=1 - p.core))]

    def second(self):
        p = self.p
        for copy in self.stage:
            copy.wait_recv()
        here = p.side * p.rows + p.row
        self.plane[here] = self.x[...] + self.core_in[...]
        self.stage = [self.s.start(self.plane.at[here], self.plane.at[here], t) for t in p.plane_peers()]

    def third(self):
        p = self.p
        for copy in self.stage:
            copy.wait_recv()
        total = self.plane[0]
        for k in range(1, 2 * p.rows):
            total = total + self.plane[k]
        self.line_in[p.line] = total
        mine = self.line_in.at[p.line]
        self.stage = [self.s.start(mine, mine, p.device(line=p.line_peer(k))) for k in range(1, p.lines)]

    def last(self):
        for copy in self.stage:
            copy.wait_recv()
        total = self.line_in[0]
        for k in range(1, self.p.lines):
            total = total + self.line_in[k]
        return total


def total_buffers(lines, rows, shape, dtype):
    return [
        pltpu.VMEM(shape, dtype),
        pltpu.VMEM(shape, dtype),
        pltpu.VMEM((2 * rows,) + shape, dtype),
        pltpu.VMEM((lines,) + shape, dtype),
    ]


def total_copies(lines, rows):
    return 2 * rows + lines - 1


def gelu(v):
    return 0.5 * v * (1.0 + jnp.tanh(0.7978845608028654 * (v + 0.044715 * (v * v * v))))


def spread(vector, me, total):
    n = vector.shape[1]
    lane = lax.broadcasted_iota(jnp.int32, (n, total), 1)
    row = lax.broadcasted_iota(jnp.int32, (n, total), 0)
    hot = jnp.where(lane == me * n + row, 1.0, 0.0).astype(jnp.bfloat16)
    return dot_nn(vector, hot)


def matrix(ref):
    block = ref[...].astype(jnp.float32)
    return block.reshape(-1, block.shape[-1]).astype(jnp.bfloat16)


def shifted(values, row_off, col_off, side):
    count = values.shape[0]
    step = row_off * side + col_off
    moved = pltpu.roll(values, (-step) % count, 0) if step % count else values
    patch = lax.broadcasted_iota(jnp.int32, (count, 1), 0)
    row, col = patch // side + row_off, lax.rem(patch, side) + col_off
    inside = (row >= 0) & (row < side) & (col >= 0) & (col < side)
    return jnp.where(inside, moved, 0.0)


FRONT_VECTORS = 7


def front_kernel(lines, rows, side, whole, pieces, number, *refs):
    refs = list(refs)

    def take(n):
        out = refs[:n]
        del refs[:n]
        return out

    (at,) = take(1)
    vectors = take(FRONT_VECTORS)
    (stem, tokens) = take(2)
    shards = take(number)
    held_outs, half_outs = take(FULL), take(number - FULL)
    (gains_out, pre_first_out, columns_out, pre_second_out, second_out, unit_out, inv) = take(7)
    (joined_out, start_out, normed_out, packed_out) = take(4)
    outs = take(FULL) + half_outs
    (gains, pre_first, columns, pre_second, second, unit, joined, start, normed, packed) = take(10)
    mats = take(5)
    (placing,) = take(1)
    held_bufs, sum_bufs = take(4), take(4)
    send_sems, recv_sems, local_sems, out_sems = take(4)
    place = Place(lines, rows)
    place.greet()
    sends = Sends(send_sems, recv_sems)

    me = (place.line * 2 + place.side) * (2 * rows) + place.row * 2 + place.core
    held = held_bufs[0]
    held[...] = jnp.zeros_like(held)
    devices = 4 * lines * rows

    parts = []
    for i, (which, region, side_first) in enumerate(pieces):
        region = tuple(pl.ds(*item) for item in region)
        kind = Gather if which < FULL else HalfGather
        parts.append(kind(place, sends, shards[which], outs[which], local_sems.at[i], region, side_first))
    batches = [[part for part, piece in zip(parts, pieces) if piece[0] in which] for which in ((0, 1), (2, 3), (4,), (5, 6, 7))]

    def run(batch, *names):
        for name in names:
            for part in batches[batch]:
                getattr(part, name)()

    copies_out = []

    def emit(value, out):
        copy = pltpu.make_async_copy(value, out, out_sems.at[len(copies_out)])
        copy.start()
        copies_out.append(copy)

    run(0, "begin")
    run(1, "begin")
    for v, (ref, row) in enumerate(zip(vectors[:6], (2, 3, 4, 5, 0, 1))):
        n = ref.shape[1]
        line = spread(ref[...], me, n * devices).astype(jnp.bfloat16)
        for k in range(0, n * devices, 1024):
            span = min(1024, n * devices - k)
            held[pl.ds(row + k // 1024, 1), pl.ds(0, span)] = line[:, k : k + span]
    table = spread(vectors[6][...], me, vectors[6].shape[1] * devices).astype(jnp.bfloat16)
    for h in range(HEADS):
        held[pl.ds(8 + h // 4, 1), pl.ds(h % 4 * 256, 256)] = table[h : h + 1, :]
    vector_total = Total(place, sends, *held_bufs)
    vector_total.begin()

    run(0, "second")
    vector_total.second()
    run(2, "begin")
    run(0, "third")
    run(1, "second")
    vector_total.third()
    run(0, "fourth")
    run(1, "third")
    run(2, "second")
    run(3, "begin")
    run(0, "last")
    count = side * side
    w_reduce, w_spatial, w_expand, w_embed, w_qkv = mats
    w_reduce[...] = matrix(outs[0])
    pre = dot_nn(stem[...], w_reduce[...])
    pre_first[...] = pre
    emit(pre_first, pre_first_out)
    first = gelu(pre).astype(jnp.bfloat16).astype(jnp.float32)
    channels = first.shape[1]
    for r in range(3):
        for c in range(3):
            k = r * 3 + c
            columns[:, pl.ds(k * channels, channels)] = shifted(first, r - 1, c - 1, side).astype(jnp.bfloat16)
    emit(columns, columns_out)
    w_spatial[...] = matrix(outs[1])
    pre = dot_nn(columns[...], w_spatial[...])
    pre_second[...] = pre
    emit(pre_second, pre_second_out)
    second[...] = gelu(pre).astype(jnp.bfloat16)
    emit(second, second_out)
    run(1, "fourth")
    run(2, "third")
    run(1, "last")
    w_expand[...] = matrix(outs[2])
    sums = sum_bufs[0]
    sums[...] = jnp.zeros_like(sums)

    def expand(cols):
        third = dot_nn(second[...], w_expand[:, cols])
        unit[:, cols] = third
        sums[pl.ds(0, 1), cols] = jnp.sum(third, axis=0, keepdims=True)
        sums[pl.ds(1, 1), cols] = jnp.sum(third * third, axis=0, keepdims=True)

    tile_loop(unit.shape[1], expand)
    norm_total = Total(place, sends, *sum_bufs)
    norm_total.begin()
    run(2, "fourth")
    norm_total.second()
    gains[...] = vector_total.last().astype(jnp.float32)
    emit(gains, gains_out)
    w_embed[...] = matrix(outs[3])
    norm_total.third()
    run(3, "second")
    for held_weight, out in zip(outs[:4], held_outs):
        emit(held_weight, out)
    totals = norm_total.last()
    mean = totals[0:1] / whole
    inv_std = lax.rsqrt(totals[1:2] / whole - mean * mean + epsilon)
    inv[...] = jnp.broadcast_to(inv_std, inv.shape)

    third_rows = count // 3

    def join(i, carry):
        at_rows = pl.ds(pl.multiple_of(i * third_rows, third_rows), third_rows)
        value = (unit[at_rows, :] - mean) * inv_std
        unit[at_rows, :] = value
        pre_joined = value * gains[0:1, :] + gains[1:2, :] + stem[at_rows, :].astype(jnp.float32)
        joined[at_rows, :] = gelu(pre_joined).astype(jnp.bfloat16)
        return carry

    lax.fori_loop(0, 3, join, 0)
    emit(unit, unit_out)
    emit(joined, joined_out)
    length, width = start.shape
    token = lax.broadcasted_iota(jnp.int32, (length, count), 0)
    patch = lax.broadcasted_iota(jnp.int32, (length, count), 1)
    placing[...] = jnp.where(token - patch == at[0], 1.0, 0.0).astype(jnp.bfloat16)

    def embed(cols):
        value = dot_nn(joined[...], w_embed[:, cols])
        high = value.astype(jnp.bfloat16)
        low = (value - high.astype(jnp.float32)).astype(jnp.bfloat16)
        moved = dot_nn(placing[...], high) + dot_nn(placing[...], low)
        start[:, cols] = tokens[:, cols].astype(jnp.float32) + moved

    tile_loop(width, embed)
    gain = gains[2:3, :width]

    def norm(i, carry):
        at_rows = pl.ds(pl.multiple_of(i * 128, 128), 128)
        value = start[at_rows, :]
        centred = value - jnp.mean(value, axis=-1, keepdims=True)
        scale = lax.rsqrt(jnp.mean(centred * centred, axis=-1, keepdims=True) + epsilon)
        normed[at_rows, :] = (centred * scale * gain).astype(jnp.bfloat16)
        return carry

    emit(start, start_out)
    lax.fori_loop(0, length // 128, norm, 0)
    emit(normed, normed_out)
    run(2, "last")
    emit(outs[4], held_outs[4])
    w_qkv[...] = matrix(outs[4])

    def project(cols):
        packed[:, cols] = dot_nn(normed[...], w_qkv[:, cols]).astype(jnp.bfloat16)

    tile_loop(packed.shape[1], project)
    emit(packed, packed_out)
    run(3, "third")
    sends.finish()
    for copy in copies_out:
        copy.wait()


FULL = 5


def front(first_at, vectors, stem, tokens, shards, side, collective_id):
    wide, narrow = lax.axis_size("wide"), lax.axis_size("narrow")
    lines, rows = wide // 2, narrow // 2
    devices = wide * narrow
    number = len(shards)
    pieces = []
    for i, item in enumerate(shards):
        r, c = item.shape
        if i == 4:
            pieces += [(i, ((0, r), (k * c // 2, c // 2)), k == 0) for k in range(2)]
        else:
            pieces.append((i, ((0, r), (0, c)), i in (0, 2, 5, 7)))
    copies = len(pieces) * gather_copies(lines, rows) + 2 * total_copies(lines, rows)
    count, length = side * side, tokens.shape[0]
    mid = shards[0].shape[1]
    wide_in = stem.shape[1]
    f32, bf16 = jnp.float32, jnp.bfloat16
    leads = [(lines, 2, rows, 2)] * FULL + [(lines, 2), (lines, rows), (lines, 2)]
    gathered = [jax.ShapeDtypeStruct(lead + s.shape, s.dtype) for lead, s in zip(leads, shards)]
    kept = [
        ((16, 1024), f32),
        ((count, mid), f32),
        ((count, 9 * mid), bf16),
        ((count, mid), f32),
        ((count, mid), bf16),
        ((count, wide_in), f32),
        ((8, wide_in), f32),
        ((count, wide_in), bf16),
        ((length, D), f32),
        ((length, D), bf16),
        ((length, 3 * D), bf16),
    ]
    vmem = pl.BlockSpec(memory_space=pltpu.VMEM)
    anywhere = pl.BlockSpec(memory_space=pl.ANY)
    scratch = [pltpu.VMEM(item.shape, item.dtype) for item in gathered[:FULL]]
    scratch += [pltpu.VMEM(shape, dtype) for k, (shape, dtype) in enumerate(kept) if k != 6]
    scratch += [pltpu.VMEM((s.shape[0] * devices, s.shape[1]), bf16) for s in shards[:5]]
    scratch += [pltpu.VMEM((length, count), bf16)]
    scratch += total_buffers(lines, rows, (16, 1024), bf16)
    scratch += total_buffers(lines, rows, (8, 1024), f32)
    scratch += [pltpu.SemaphoreType.DMA((copies,)), pltpu.SemaphoreType.DMA((copies,)), pltpu.SemaphoreType.DMA((len(pieces),)), pltpu.SemaphoreType.DMA((FULL + 10,))]
    results = pl.pallas_call(
        functools.partial(front_kernel, lines, rows, side, float(count * devices), pieces, number),
        out_shape=gathered + [jax.ShapeDtypeStruct(s, d) for s, d in kept],
        in_specs=[pl.BlockSpec(memory_space=pltpu.SMEM)] + [vmem] * (FRONT_VECTORS + 2) + [anywhere] * number,
        out_specs=[anywhere] * number + [vmem if k == 6 else anywhere for k in range(len(kept))],
        scratch_shapes=scratch,
        compiler_params=pltpu.CompilerParams(collective_id=collective_id, has_side_effects=True, vmem_limit_bytes=60 * 2**20),
        cost_estimate=pl.CostEstimate(flops=6 * 10**9, bytes_accessed=7 * 10**7, transcendentals=10**6),
        name="front",
    )(first_at, *vectors, stem, tokens, *shards)
    return results[:number], results[number:]


def gelu_slope(v):
    t = jnp.tanh(0.7978845608028654 * (v + 0.044715 * (v * v * v)))
    return 0.5 * (1.0 + t) + 0.5 * v * (1.0 - t * t) * (0.7978845608028654 * (1.0 + 0.134145 * (v * v)))


def row_mean(values):
    return jnp.mean(values, axis=-1, keepdims=True)


def unit_of(values):
    centred = values - row_mean(values)
    inv_std = lax.rsqrt(row_mean(centred * centred) + epsilon)
    return centred * inv_std, inv_std


def unit_back(weighted, unit_rows, inv_std):
    return inv_std * (weighted - row_mean(weighted) - unit_rows * row_mean(weighted * unit_rows))


def column_sum(values):
    return jnp.sum(values, axis=0, keepdims=True)


FTILE = 512


def middle_kernel(lines, rows, counts, *refs):
    refs = list(refs)

    def take(n):
        out = refs[:n]
        del refs[:n]
        return out

    attended, start, d_out, gains, scale = take(5)
    outs_in, ups_in, downs_in = take(counts[0]), take(counts[1]), take(counts[2])
    mixed, mixed_low, normed2, narrowed, grad_up, grad_middle, branch, grad_attended, sums = take(9)
    held = take(3)
    mats = take(3)
    pre, act, weighted = take(3)
    send_sems, recv_sems, local_sems = take(3)
    i = pl.program_id(0)
    w_out, w_up, w_down = mats
    width, hidden = w_up.shape

    @pl.when(i == 0)
    def _():
        place = Place(lines, rows)
        partner = place.device(core=1 - place.core)
        barrier = pltpu.get_barrier_semaphore()
        pl.semaphore_signal(barrier, inc=1, device_id=partner, device_id_type=MESH)
        pl.semaphore_wait(barrier, 1)
        sends = Sends(send_sems, recv_sems)
        waits = []
        for full, pieces in zip(held, (outs_in, ups_in, downs_in)):
            group = []
            for k, piece in enumerate(pieces):
                if full is held[1]:
                    side = place.side if k == 0 else 1 - place.side
                    spot = full.at[:, side, :, place.core]
                else:
                    spot = full.at[:, :, place.row_source(k), place.core]
                local = pltpu.make_async_copy(piece, spot, local_sems.at[sends.used])
                local.start()
                group.append((sends.start(piece, spot, partner), local))
            waits.append(group)
        for full, mat, group in zip(held, mats, waits):
            for copy, local in group:
                copy.wait_recv()
                local.wait()
            tall = mat.shape[0] // (2 * lines)

            def convert(k, carry, full=full, mat=mat, tall=tall):
                block = full[k // 2, lax.rem(k, 2)].astype(jnp.float32)
                mat[pl.ds(pl.multiple_of(k * tall, tall), tall), :] = block.reshape(tall, mat.shape[1]).astype(mat.dtype)
                return carry

            lax.fori_loop(0, 2 * lines, convert, 0)
        sends.finish()
        sums[...] = jnp.zeros_like(sums)

    gain_attn, gain_mid = gains[3:4, :width], gains[4:5, :width]
    scaled = attended[...] * scale[...]
    unit1, inv1 = unit_of(scaled)
    low = (unit1 * gain_attn).astype(jnp.bfloat16)
    mixed_low[...] = low
    middle = start[...] + dot_nn(low, w_out[...])
    unit2, inv2 = unit_of(middle)
    low2 = (unit2 * gain_mid).astype(jnp.bfloat16)
    normed2[...] = low2
    tiles = hidden // FTILE
    count = middle.shape[0]
    zero = jnp.zeros((count, 1), jnp.float32)

    def span(f):
        return pl.ds(pl.multiple_of(f * FTILE, FTILE), FTILE)

    def gain_of(f):
        per = 1024 // FTILE
        return gains[pl.ds(5 + f // per, 1), f % per * FTILE : (f % per + 1) * FTILE]

    total = zero
    for f in range(tiles):
        cols = pl.ds(f * FTILE, FTILE)
        value = dot_nn(low2, w_up[:, cols])
        pre[:, cols] = value
        value = gelu(value)
        act[:, cols] = value
        total = total + jnp.sum(value, axis=-1, keepdims=True)
    mean = total / hidden
    total = zero
    for f in range(tiles):
        cols = pl.ds(f * FTILE, FTILE)
        centred = act[:, cols] - mean
        total = total + jnp.sum(centred * centred, axis=-1, keepdims=True)
    inv3 = lax.rsqrt(total / hidden + epsilon)
    result = middle
    cross1, cross2 = zero, zero
    for f in range(tiles):
        cols = pl.ds(f * FTILE, FTILE)
        unit3 = (act[:, cols] - mean) * inv3
        act[:, cols] = unit3
        gain = gain_of(f)
        low3 = (unit3 * gain).astype(jnp.bfloat16)
        narrowed[:, cols] = low3
        result = result + dot_nn(low3, w_down[cols, :])
        grad = dot_nt(d_out[...], w_down[cols, :])
        sums[0:1, cols] += column_sum(grad * unit3)
        grad = grad * gain
        weighted[:, cols] = grad
        cross1 = cross1 + jnp.sum(grad, axis=-1, keepdims=True)
        cross2 = cross2 + jnp.sum(grad * unit3, axis=-1, keepdims=True)
    mixed[...] = result.astype(jnp.bfloat16)
    cross1, cross2 = cross1 / hidden, cross2 / hidden
    grad2 = jnp.zeros((count, width), jnp.float32)
    for f in range(tiles):
        cols = pl.ds(f * FTILE, FTILE)
        grad = inv3 * (weighted[:, cols] - cross1 - act[:, cols] * cross2)
        grad = (gelu_slope(pre[:, cols]) * grad).astype(jnp.bfloat16)
        grad_up[:, cols] = grad
        grad2 = grad2 + dot_nt(grad, w_up[:, cols])
    sums[1:2, :width] += column_sum(grad2 * unit2)
    grad_mid = d_out[...].astype(jnp.float32) + unit_back(grad2 * gain_mid, unit2, inv2)
    grad_middle[...] = grad_mid
    low = grad_mid.astype(jnp.bfloat16)
    branch[...] = low
    grad1 = dot_nt(low, w_out[...])
    sums[2:3, :width] += column_sum(grad1 * unit1)
    grad_scaled = unit_back(grad1 * gain_attn, unit1, inv1)
    sums[3:4, :width] += column_sum(grad_scaled * attended[...])
    grad_attended[...] = (grad_scaled * scale[...]).astype(jnp.bfloat16)


def middle_part(attended, start, d_out, gains, scale_row, outs_in, ups_in, downs_in, hidden, collective_id):
    wide, narrow = lax.axis_size("wide"), lax.axis_size("narrow")
    lines, rows = wide // 2, narrow // 2
    length, width = start.shape
    block = 256
    f32, bf16 = jnp.float32, jnp.bfloat16
    counts = (len(outs_in), len(ups_in), len(downs_in))
    copies = sum(counts)

    def by_token(columns):
        return pl.BlockSpec((block, columns), lambda i: (i, 0))

    def whole(shape):
        return pl.BlockSpec(shape, lambda i: (0,) * len(shape))

    anywhere = pl.BlockSpec(memory_space=pl.ANY)
    pieces = list(outs_in) + list(ups_in) + list(downs_in)
    results = [(width, bf16), (width, bf16), (width, bf16), (hidden, bf16), (hidden, bf16), (width, f32), (width, bf16), (width, bf16)]
    shapes = [(width, width), (width, hidden), (hidden, width)]
    devices = wide * narrow
    return pl.pallas_call(
        functools.partial(middle_kernel, lines, rows, counts),
        out_shape=[jax.ShapeDtypeStruct((length, c), d) for c, d in results] + [jax.ShapeDtypeStruct((8, hidden), f32)],
        grid=(length // block,),
        in_specs=[by_token(width), by_token(width), by_token(width), whole(gains.shape), whole(scale_row.shape)] + [anywhere] * copies,
        out_specs=[by_token(c) for c, _ in results] + [whole((8, hidden))],
        scratch_shapes=[pltpu.VMEM((lines, 2, rows, 2, m // devices, n), bf16) for m, n in shapes]
        + [pltpu.VMEM(shape, bf16) for shape in shapes]
        + [pltpu.VMEM((block, hidden), f32)] * 3
        + [pltpu.SemaphoreType.DMA((copies,))] * 3,
        compiler_params=pltpu.CompilerParams(collective_id=collective_id, has_side_effects=True, vmem_limit_bytes=60 * 2**20),
        cost_estimate=pl.CostEstimate(flops=22 * 10**9, bytes_accessed=6 * 10**7, transcendentals=7 * 10**6),
        name="middle_part",
    )(attended, start, d_out, gains, scale_row, *pieces)


def scatter_copies(lines, rows):
    return 1 + (rows - 1) + 1 + 1 + (rows - 1) + (lines - 1)


def add_loop(lead, fn):
    total = 1
    for size in lead:
        total *= size

    def body(i, carry):
        index = []
        for size in reversed(lead):
            index.append(lax.rem(i, size))
            i = i // size
        fn(tuple(reversed(index)))
        return carry

    lax.fori_loop(0, total, body, 0)


def plus(*terms):
    total = terms[0].astype(jnp.float32)
    for term in terms[1:]:
        total = total + term.astype(jnp.float32)
    return total


class Scatter:
    def __init__(self, place, sends, full, out, buffers):
        self.p, self.s, self.full, self.out = place, sends, full, out
        self.other, self.low1, self.high1, self.low2, self.high2, self.line0, self.lines_in = buffers
        cols = full.shape[-1]
        cut = cols // 256 * 128
        self.low, self.high = pl.ds(0, cut), pl.ds(cut, cols - cut)

    def begin(self):
        core = self.p.core
        self.stage = [self.s.start(self.full.at[:, :, :, 1 - core], self.other, self.p.device(core=1 - core))]

    def second(self):
        p, full, dtype = self.p, self.full, self.full.dtype
        for copy in self.stage:
            copy.wait_recv()

        def add(i):
            l, x, y = i
            full[l, x, y, p.core] = plus(full[l, x, y, p.core], self.other[l, x, y]).astype(dtype)

        add_loop(self.other.shape[:3], add)
        self.stage = [self.s.start(full.at[:, 1 - p.side, :, p.core, :, self.high], self.high1, p.device(side=1 - p.side))]
        for k in range(1, p.rows):
            to = p.row_peer(k)
            self.stage.append(self.s.start(full.at[:, :, to, p.core, :, self.low], self.low1.at[k - 1], p.device(row=to)))

    def third(self):
        p, full, dtype = self.p, self.full, self.full.dtype
        for copy in self.stage:
            copy.wait_recv()

        def add_low(i):
            l, x = i
            terms = [full[l, x, p.row, p.core, :, self.low]] + [self.low1[k, l, x] for k in range(p.rows - 1)]
            full[l, x, p.row, p.core, :, self.low] = plus(*terms).astype(dtype)

        def add_high(i):
            l, y = i
            full[l, p.side, y, p.core, :, self.high] = plus(full[l, p.side, y, p.core, :, self.high], self.high1[l, y]).astype(dtype)

        add_loop((p.lines, 2), add_low)
        add_loop((p.lines, p.rows), add_high)
        self.stage = [self.s.start(full.at[:, 1 - p.side, p.row, p.core, :, self.low], self.low2, p.device(side=1 - p.side))]
        for k in range(1, p.rows):
            to = p.row_peer(k)
            self.stage.append(self.s.start(full.at[:, p.side, to, p.core, :, self.high], self.high2.at[k - 1], p.device(row=to)))

    def fourth(self):
        p, full, dtype = self.p, self.full, self.full.dtype
        for copy in self.stage:
            copy.wait_recv()

        def add(i):
            (l,) = i
            self.line0[l, :, self.low] = plus(full[l, p.side, p.row, p.core, :, self.low], self.low2[l]).astype(dtype)
            terms = [full[l, p.side, p.row, p.core, :, self.high]] + [self.high2[k, l] for k in range(p.rows - 1)]
            self.line0[l, :, self.high] = plus(*terms).astype(dtype)

        add_loop((p.lines,), add)
        self.stage = []
        for k in range(1, p.lines):
            to = p.line_peer(k)
            self.stage.append(self.s.start(self.line0.at[to], self.lines_in.at[k - 1], p.device(line=to)))

    def last(self):
        p = self.p
        for copy in self.stage:
            copy.wait_recv()
        self.out[...] = plus(self.line0[p.line], *[self.lines_in[k] for k in range(p.lines - 1)])


def scatter_buffers(lines, rows, r, c, dtype):
    low = c // 256 * 128
    high = c - low
    return [
        pltpu.VMEM((lines, 2, rows, r, c), dtype),
        pltpu.VMEM((max(rows - 1, 1), lines, 2, r, low), dtype),
        pltpu.VMEM((lines, rows, r, high), dtype),
        pltpu.VMEM((lines, r, low), dtype),
        pltpu.VMEM((max(rows - 1, 1), lines, r, high), dtype),
        pltpu.VMEM((lines, r, c), dtype),
        pltpu.VMEM((max(lines - 1, 1), r, c), dtype),
    ]


NBUF = 7


def tile_loop(width, fn):
    full = width // 256

    def body(j, carry):
        fn(pl.ds(pl.multiple_of(j * 256, 256), 256))
        return carry

    lax.fori_loop(0, full, body, 0)
    if width % 256:
        fn(pl.ds(full * 256, width % 256))


def finish_kernel(lines, rows, products, given, *refs):
    refs = list(refs)

    def take(n):
        out = refs[:n]
        del refs[:n]
        return out

    number = len(products)
    lefts, rights, ready = take(number), take(number), take(given)
    count = number + given
    outs = take(count)
    fulls, buffers = take(count), take(count * NBUF)
    xbuf, gbuf, xsem, gsem, ready_sem, send_sems, recv_sems = refs
    place = Place(lines, rows)
    place.greet()
    sends = Sends(send_sems, recv_sems)
    parts = [Scatter(place, sends, fulls[i], outs[i], buffers[NBUF * i : NBUF * (i + 1)]) for i in range(count)]
    ready_copies = [pltpu.make_async_copy(ready[i], fulls[number + i], ready_sem.at[i]) for i in range(given)]
    for copy in ready_copies:
        copy.start()

    core = place.core
    tasks = []
    for a, (kind, width) in enumerate(products):
        if kind == "rows":
            tasks.append((a, 0, None, None))
        else:
            for c in (1 - core, core):
                for y in range(rows):
                    pitch = rights[a].shape[1] // rows
                    start = y * pitch + c * (pitch - width)
                    tasks.append((a, start, y, c))

    def fetch_right(t):
        a, start, y, c = tasks[t]
        width = products[a][1]
        start = pl.multiple_of(jnp.int32(start), 128)
        return pltpu.make_async_copy(rights[a].at[:, pl.ds(start, width)], gbuf.at[t % 2, :, pl.ds(0, width)], gsem.at[t % 2])

    def fetch_left(a):
        return pltpu.make_async_copy(lefts[a], xbuf.at[a % 2], xsem.at[a % 2])

    fetch_left(0).start()
    fetch_right(0).start()

    def multiply(t):
        a, start, y, c = tasks[t]
        kind, width = products[a]
        if t + 1 < len(tasks):
            fetch_right(t + 1).start()
            if tasks[t + 1][0] != a:
                fetch_left(a + 1).start()
        if t == 0 or tasks[t - 1][0] != a:
            fetch_left(a).wait()
        fetch_right(t).wait()
        full = fulls[a]

        def tile(cols):
            block = dot_nn(xbuf[a % 2], gbuf[t % 2, :, cols])
            n = block.shape[1]
            if kind == "rows":
                full[:, :, :, :, :, cols] = block.reshape(lines, 2, rows, 2, -1, n).astype(full.dtype)
            else:
                full[:, :, y, c, :, cols] = block.reshape(lines, 2, -1, n).astype(full.dtype)

        tile_loop(width, tile)

    order = [number + i for i in range(given)] + list(range(number))
    pending = []

    def advance():
        for item in list(pending):
            getattr(parts[item[0]], item[1].pop(0))()
            if not item[1]:
                pending.remove(item)

    for i in range(given):
        ready_copies[i].wait()
        parts[number + i].begin()
        pending.append((number + i, ["second", "third", "fourth", "last"]))
    for t, (a, start, y, c) in enumerate(tasks):
        multiply(t)
        sent = products[a][0] == "rows" or (c is not core and y == rows - 1)
        if sent:
            parts[a].begin()
        done = t + 1 == len(tasks) or tasks[t + 1][0] != a
        if done or sent:
            advance()
        if done:
            pending.append((a, ["second", "third", "fourth", "last"]))
    while pending:
        advance()
    sends.finish()


def finish(products, given, collective_id):
    wide, narrow = lax.axis_size("wide"), lax.axis_size("narrow")
    lines, rows = wide // 2, narrow // 2
    shapes, plan = [], []
    for left, right, kind in products:
        m, n = left.shape[0], right.shape[1]
        if kind == "rows":
            width = n
            shapes.append((lines, 2, rows, 2, m // (4 * lines * rows), n))
        else:
            width = -(-(n // (2 * rows)) // 128) * 128
            shapes.append((lines, 2, rows, 2, m // (2 * lines), width))
        plan.append((kind, width))
    shapes += [g.shape for g in given]
    count = len(shapes)
    copies = count * scatter_copies(lines, rows)
    dtype = jnp.bfloat16
    scratch = [pltpu.VMEM(s, dtype) for s in shapes]
    for s in shapes:
        scratch += scatter_buffers(lines, rows, s[-2], s[-1], dtype)
    m, t = products[0][0].shape
    widest = max(width for _, width in plan)
    scratch += [
        pltpu.VMEM((2, m, t), dtype),
        pltpu.VMEM((2, t, widest), dtype),
        pltpu.SemaphoreType.DMA((2,)),
        pltpu.SemaphoreType.DMA((2,)),
        pltpu.SemaphoreType.DMA((max(len(given), 1),)),
        pltpu.SemaphoreType.DMA((copies,)),
        pltpu.SemaphoreType.DMA((copies,)),
    ]
    ins = [p[0] for p in products] + [p[1] for p in products] + list(given)
    return pl.pallas_call(
        functools.partial(finish_kernel, lines, rows, plan, len(given)),
        out_shape=[jax.ShapeDtypeStruct(s[-2:], jnp.float32) for s in shapes],
        in_specs=[pl.BlockSpec(memory_space=pl.ANY)] * len(ins),
        out_specs=[pl.BlockSpec(memory_space=pltpu.VMEM)] * count,
        scratch_shapes=scratch,
        compiler_params=pltpu.CompilerParams(collective_id=collective_id, has_side_effects=True, vmem_limit_bytes=60 * 2**20),
        cost_estimate=pl.CostEstimate(flops=14 * 10**9, bytes_accessed=6 * 10**7, transcendentals=0),
        name="finish",
    )(*ins)


def total_kernel(lines, rows, x_ref, o_ref, core_in, plane, line_in, send_sems, recv_sems):
    p = Place(lines, rows)
    barrier = pltpu.get_barrier_semaphore()
    plane_peers = [(k // rows, k % rows) for k in range(1, 2 * rows)]
    targets = [p.device(core=1 - p.core)]
    targets += [p.device(side=lax.rem(p.side + a, 2), row=p.row_peer(b)) for a, b in plane_peers]
    targets += [p.device(line=p.line_peer(k)) for k in range(1, lines)]
    for target in targets:
        pl.semaphore_signal(barrier, inc=1, device_id=target, device_id_type=MESH)
    pl.semaphore_wait(barrier, len(targets))
    sends = Sends(send_sems, recv_sems)
    sends.start(x_ref, core_in, targets[0]).wait_recv()
    here = p.side * rows + p.row
    plane[here] = x_ref[...] + core_in[...]
    stage = [sends.start(plane.at[here], plane.at[here], t) for t in targets[1 : 2 * rows]]
    for copy in stage:
        copy.wait_recv()
    total = plane[0]
    for k in range(1, 2 * rows):
        total = total + plane[k]
    line_in[p.line] = total
    stage = [sends.start(line_in.at[p.line], line_in.at[p.line], t) for t in targets[2 * rows :]]
    for copy in stage:
        copy.wait_recv()
    total = line_in[0]
    for k in range(1, lines):
        total = total + line_in[k]
    o_ref[...] = total
    sends.finish()


def total_sum(x, collective_id):
    wide, narrow = lax.axis_size("wide"), lax.axis_size("narrow")
    lines, rows = wide // 2, narrow // 2
    copies = 1 + 2 * rows - 1 + lines - 1
    return pl.pallas_call(
        functools.partial(total_kernel, lines, rows),
        out_shape=jax.ShapeDtypeStruct(x.shape, x.dtype),
        in_specs=[pl.BlockSpec(memory_space=pltpu.VMEM)],
        out_specs=pl.BlockSpec(memory_space=pltpu.VMEM),
        scratch_shapes=[
            pltpu.VMEM(x.shape, x.dtype),
            pltpu.VMEM((2 * rows,) + x.shape, x.dtype),
            pltpu.VMEM((lines,) + x.shape, x.dtype),
            pltpu.SemaphoreType.DMA((copies,)),
            pltpu.SemaphoreType.DMA((copies,)),
        ],
        compiler_params=pltpu.CompilerParams(collective_id=collective_id, has_side_effects=True),
        cost_estimate=pl.CostEstimate(flops=0, bytes_accessed=10**6, transcendentals=0),
        name="total_sum",
    )(x)


def local(
    tokens,
    features,
    segments,
    positions,
    w_qkv,
    w_out,
    w_up,
    w_down,
    gain_pre,
    gain_attn,
    gain_mid,
    gain_ffn,
    rel_table,
    head_scale,
    w_reduce,
    w_spatial,
    w_expand,
    w_embed,
    bn_gain,
    bn_shift,
    d_out,
):
    both = ("wide", "narrow")
    devices = lax.axis_size(both)
    me = lax.axis_index("wide") * lax.axis_size("narrow") + lax.axis_index("narrow")
    rows, length = (segments.shape[0], segments.shape[1])
    images, side = (features.shape[0], features.shape[1])
    patch_count = images * side * side
    whole = patch_count * devices
    first_at = positions[0, 0]
    stem_in = features.reshape(patch_count, features.shape[3])
    vectors = [item.reshape(1, -1) for item in (gain_pre, gain_attn, gain_mid, gain_ffn, bn_gain, bn_shift)]
    gathered, kept = front(
        positions[0, :1],
        vectors + [rel_table],
        stem_in,
        tokens,
        [w_reduce, w_spatial, w_expand, w_embed, w_qkv, w_out, w_up, w_down],
        side,
        1,
    )
    full_reduce, full_spatial, full_expand, full_embed, full_qkv = (
        item.reshape(-1, item.shape[-1]) for item in gathered[:5]
    )
    planes = lax.axis_size("narrow") // 2

    def other_side(item):
        return lax.ppermute(item, "wide", [(w, w ^ 1) for w in range(devices // (2 * planes))])

    def next_row(item, k):
        return lax.ppermute(item, "narrow", [(n, (n + 2 * k) % (2 * planes)) for n in range(2 * planes)])

    def by_row(item):
        return [item] + [next_row(item, k) for k in range(1, planes)]

    outs_in, downs_in = by_row(gathered[5]), by_row(gathered[7])
    ups_in = [gathered[6], other_side(gathered[6])]
    gains, pre_first, columns, pre_second, second, bn_unit, bn_inv, joined, start, normed0_low, packed = kept
    full_bn_gain, full_bn_shift = gains[0], gains[1]
    full_pre, full_attn, full_mid = gains[2, :D], gains[3, :D], gains[4, :D]
    full_ffn = gains[5:8].reshape(-1)
    full_table = gains[8:11].reshape(HEADS, 2 * RSPAN)
    bn_inv = bn_inv[0]
    pre_joined = bn_unit * full_bn_gain + full_bn_shift + stem_in.astype(jnp.float32)
    unused, unit0, inv0 = layer_norm(start, full_pre)
    win = windows(segments)
    attended, logsums, bias = attend(packed, segments, bias_strips(full_table), win)
    scale_row = jnp.repeat(head_scale, HDIM)[None, :]
    hidden = w_up.shape[1]
    mixed, mixed_low, normed2_low, narrowed_low, grad_pre_up, grad_middle, grad_branch, grad_attended, sums = middle_part(
        attended, start, d_out, gains, scale_row, outs_in, ups_in, downs_in, hidden, 5
    )
    grad_gain_ffn, grad_gain_mid, grad_gain_attn = sums[0], sums[1, :D], sums[2, :D]
    grad_head_local = jnp.sum(sums[3, :D].reshape(HEADS, HDIM), axis=1)
    grad_packed, grad_strips = attend_back(packed, grad_attended, attended, segments, bias, logsums, win)
    grad_table = table_from_strips(grad_strips)
    grad_normed0 = product_nt(grad_packed, full_qkv)
    grad_start_in, grad_gain_pre = layer_norm_back(
        grad_normed0, unit0, inv0, full_pre.astype(jnp.float32)
    )
    grad_tokens = grad_middle + grad_start_in
    grad_embedded = lax.dynamic_slice_in_dim(grad_tokens, first_at, patch_count, 0).astype(jnp.bfloat16)
    grad_w_embed = product_tn(joined, grad_embedded)
    grad_joined = product_nt(grad_embedded, full_embed)
    grad_pre_joined = smooth_back(pre_joined, grad_joined)
    grad_bn_shift = jnp.sum(grad_pre_joined, axis=0)
    grad_bn_gain = jnp.sum(grad_pre_joined * bn_unit, axis=0)
    smalls = (
        grad_gain_pre,
        grad_gain_attn,
        grad_gain_mid,
        grad_gain_ffn,
        grad_bn_gain,
        grad_bn_shift,
        grad_table.reshape(-1),
        grad_head_local,
    )
    small = jnp.concatenate(smalls)
    small = jnp.pad(small, (0, -small.shape[0] % 1024)).reshape(-1, 128)
    small = total_sum(small, 4).reshape(-1)
    totals, at = [], 0
    for item in smalls:
        totals.append(small[at : at + item.shape[0]])
        at += item.shape[0]
    sum_pre, sum_attn, sum_mid, sum_ffn, sum_bn_gain, sum_bn_shift = (
        lax.dynamic_slice_in_dim(item, me * (item.shape[0] // devices), item.shape[0] // devices)
        for item in totals[:6]
    )
    breadth = 2 * RSPAN // devices
    sum_table = lax.dynamic_slice_in_dim(totals[6].reshape(HEADS, -1), me * breadth, breadth, 1)
    grad_head = totals[7]
    bn_gain_row = full_bn_gain.astype(jnp.float32)
    grad_unit = grad_pre_joined * bn_gain_row
    sum_unit, sum_cross = totals[5] * bn_gain_row, totals[4] * bn_gain_row
    grad_third = (bn_inv * (grad_unit - sum_unit / whole - bn_unit * (sum_cross / whole))).astype(
        jnp.bfloat16
    )
    grad_w_expand = product_tn(second, grad_third)
    grad_second = product_nt(grad_third, full_expand)
    grad_pre_second = smooth_back(pre_second, grad_second).astype(jnp.bfloat16)
    grad_w_spatial = product_tn(columns, grad_pre_second)
    grad_columns = product_nt(grad_pre_second, full_spatial)
    grad_first = fold(grad_columns.reshape(images, side, side, -1)).reshape(patch_count, -1)
    grad_pre_first = smooth_back(pre_first, grad_first).astype(jnp.bfloat16)
    grad_w_reduce = product_tn(stem_in, grad_pre_first)
    grad_features = (grad_pre_joined + product_nt(grad_pre_first, full_reduce)).reshape(
        features.shape
    )
    lines = lax.axis_size("wide") // 2

    def by_rows(grad):
        return grad.astype(jnp.bfloat16).reshape(lines, 2, planes, 2, -1, grad.shape[1])

    sum_down, sum_up, sum_qkv, sum_out, sum_embed, sum_expand, sum_spatial, sum_reduce = finish(
        [
            (d_out.T, narrowed_low, "blocks"),
            (normed2_low.T, grad_pre_up, "blocks"),
            (normed0_low.T, grad_packed, "blocks"),
            (mixed_low.T, grad_branch, "rows"),
        ],
        [by_rows(grad_w_embed), by_rows(grad_w_expand), by_rows(grad_w_spatial), by_rows(grad_w_reduce)],
        2,
    )
    sum_down = sum_down.T
    width = 3 * D // (2 * planes)
    sum_qkv = jnp.where(
        lax.axis_index("narrow") % 2 == 0, sum_qkv[:, :width], sum_qkv[:, sum_qkv.shape[1] - width :]
    )
    return (
        mixed,
        grad_tokens,
        grad_features,
        sum_qkv,
        sum_out,
        sum_up,
        sum_down,
        sum_pre,
        sum_attn,
        sum_mid,
        sum_ffn,
        sum_table,
        grad_head,
        sum_reduce,
        sum_spatial,
        sum_expand,
        sum_embed,
        sum_bn_gain,
        sum_bn_shift,
    )


def solution(mesh):
    placed = (
        P(("wide", "narrow"), None),
        P(("wide", "narrow"), None, None, None),
        P(("wide", "narrow"), None),
        P(("wide", "narrow"), None),
        P(("wide", "narrow"), None),
        P(("wide", "narrow"), None),
        P(("wide", "narrow"), None),
        P(("wide", "narrow"), None),
        P(("wide", "narrow")),
        P(("wide", "narrow")),
        P(("wide", "narrow")),
        P(("wide", "narrow")),
        P(None, ("wide", "narrow")),
        P(),
        P(("wide", "narrow"), None),
        P(("wide", "narrow"), None),
        P(("wide", "narrow"), None),
        P(("wide", "narrow"), None),
        P(("wide", "narrow")),
        P(("wide", "narrow")),
        P(("wide", "narrow"), None),
    )
    return jax.shard_map(
        local,
        mesh=mesh,
        in_specs=placed,
        out_specs=(
            P(("wide", "narrow"), None),
            P(("wide", "narrow"), None),
            P(("wide", "narrow"), None, None, None),
            P("wide", "narrow"),
            P(("wide", "narrow"), None),
            P("wide", "narrow"),
            P("narrow", "wide"),
            P(("wide", "narrow")),
            P(("wide", "narrow")),
            P(("wide", "narrow")),
            P(("wide", "narrow")),
            P(None, ("wide", "narrow")),
            P(),
            P(("wide", "narrow"), None),
            P(("wide", "narrow"), None),
            P(("wide", "narrow"), None),
            P(("wide", "narrow"), None),
            P(("wide", "narrow")),
            P(("wide", "narrow")),
        ),
        check_vma=False,
    )
```

```python
import functools

import jax
import jax.numpy as jnp
from jax import lax
from jax.experimental import pallas as pl
from jax.experimental.pallas import tpu as pltpu
from jax.sharding import PartitionSpec as P

D = 768
HEADS = 12
HDIM = 64
RSPAN = 128


epsilon = 1e-05


def product(lhs_matrix, rhs_matrix):
    return jnp.dot(lhs_matrix, rhs_matrix, preferred_element_type=jnp.float32)


def product_tn(lhs_matrix, rhs_matrix):
    return lax.dot_general(
        lhs_matrix, rhs_matrix, (((0,), (0,)), ((), ())), preferred_element_type=jnp.float32
    )


def product_nt(lhs_matrix, rhs_matrix):
    return lax.dot_general(
        lhs_matrix, rhs_matrix, (((1,), (1,)), ((), ())), preferred_element_type=jnp.float32
    )


def layer_norm(values, gain):
    average = jnp.mean(values, axis=-1, keepdims=True)
    centred = values - average
    inv_std = lax.rsqrt(jnp.mean(centred * centred, axis=-1, keepdims=True) + epsilon)
    unit_rows = centred * inv_std
    return (unit_rows * gain, unit_rows, inv_std)


def layer_norm_back(cotangent, unit_rows, inv_std, gain):
    weighted = cotangent * gain
    inner = (
        weighted
        - jnp.mean(weighted, axis=-1, keepdims=True)
        - unit_rows * jnp.mean(weighted * unit_rows, axis=-1, keepdims=True)
    )
    return (inv_std * inner, jnp.sum(cotangent * unit_rows, axis=0))


def smooth(values):
    return jax.nn.gelu(values, approximate=True)


def smooth_back(values, cotangent):
    unused, pullback = jax.vjp(smooth, values)
    return pullback(cotangent)[0]


def unfold(grid):
    side = grid.shape[1]
    padded = jnp.pad(grid, ((0, 0), (1, 1), (1, 1), (0, 0)))
    pieces = [
        padded[:, row_off : row_off + side, col_off : col_off + side, :]
        for row_off in range(3)
        for col_off in range(3)
    ]
    return jnp.concatenate(pieces, axis=-1)


def fold(columns):
    channels = columns.shape[-1] // 9
    side = columns.shape[1]
    total = jnp.zeros((columns.shape[0], side + 2, side + 2, channels), jnp.float32)
    for row_off in range(3):
        for col_off in range(3):
            which = row_off * 3 + col_off
            piece = columns[..., which * channels : (which + 1) * channels]
            total = total + jnp.pad(
                piece, ((0, 0), (row_off, 2 - row_off), (col_off, 2 - col_off), (0, 0))
            )
    return total[:, 1:-1, 1:-1, :]


PAIRS = HEADS // 2
BLK = 128
NEG = -1e30


def dot_nn(a, b):
    return lax.dot_general(a, b, (((1,), (0,)), ((), ())), preferred_element_type=jnp.float32)


def dot_nt(a, b):
    return lax.dot_general(a, b, (((1,), (1,)), ((), ())), preferred_element_type=jnp.float32)


def split_heads(pair, scale):
    lane = lax.broadcasted_iota(jnp.int32, pair.shape, 1)
    vals = pair * jnp.asarray(scale, pair.dtype)
    zero = jnp.zeros_like(vals)
    return jnp.concatenate([jnp.where(lane < HDIM, vals, zero), jnp.where(lane < HDIM, zero, vals)], axis=0)


def join_heads(both):
    row = lax.broadcasted_iota(jnp.int32, (2 * HDIM, BLK), 0)
    return jnp.where(row < HDIM, both[:, :BLK], both[:, BLK:])


def bias_strips(table):
    rev = jnp.flip(table.astype(jnp.float32), axis=1)
    first, last = rev[:, 255:256], rev[:, 0:1]
    below = jnp.concatenate([jnp.broadcast_to(first, (HEADS, 129)), rev[:, 128:255]], axis=1)
    middle = jnp.concatenate([rev[:, 127:256], rev[:, 0:127]], axis=1)
    above = jnp.concatenate([last, rev[:, 0:127], jnp.broadcast_to(last, (HEADS, 128))], axis=1)
    low = jnp.broadcast_to(first, (HEADS, 256))
    high = jnp.broadcast_to(last, (HEADS, 256))
    return jnp.stack([low, below, middle, above, high], axis=1)


def table_from_strips(sums):
    low, below, middle, above, high = (sums[:, i] for i in range(5))
    total = jnp.concatenate([middle[:, 129:256], middle[:, 0:129]], axis=1)
    zero = jnp.zeros((HEADS, 127), jnp.float32)
    first = jnp.sum(low, axis=1, keepdims=True) + jnp.sum(below[:, :129], axis=1, keepdims=True)
    last = jnp.sum(high, axis=1, keepdims=True) + above[:, 0:1] + jnp.sum(above[:, 128:], axis=1, keepdims=True)
    total = total + jnp.concatenate([jnp.zeros((HEADS, 128), jnp.float32), below[:, 129:], first], axis=1)
    head = jnp.concatenate([above[:, 1:128], jnp.zeros((HEADS, 129), jnp.float32)], axis=1)
    total = total + head + jnp.concatenate([last, jnp.zeros((HEADS, 255), jnp.float32)], axis=1)
    return jnp.flip(total, axis=1)


def windows(segments):
    seg = segments.reshape(-1)
    starts = seg[::BLK]
    ends = seg[BLK - 1 :: BLK]
    low = jnp.sum((seg[None, :] < starts[:, None]).astype(jnp.int32), axis=1) // BLK
    high = (jnp.sum((seg[None, :] <= ends[:, None]).astype(jnp.int32), axis=1) + BLK - 1) // BLK
    return jnp.stack([low, high])


def attend_kernel(win, packed, segk, segq, strips, out, logsum, bias, vt, qm, acc, stat):
    i = pl.program_id(0)

    @pl.when(i == 0)
    def _():
        for hp in range(PAIRS):
            vt[pl.ds(hp * 128, 128), :] = packed[:, pl.ds(2 * D + hp * 128, 128)].T
            for d in range(5):
                for half in range(2):
                    row = strips[2 * hp + half, pl.ds(d, 1), :]
                    tile = jnp.broadcast_to(row, (BLK, 256))
                    if 0 < d < 4:
                        tile = pltpu.roll(tile, 0, 1, stride=1, stride_axis=0)
                    bias[hp, d, :, pl.ds(half * BLK, BLK)] = tile[:, :BLK]

    rows = pl.ds(pl.multiple_of(i * BLK, BLK), BLK)
    for hp in range(PAIRS):
        qm[hp] = split_heads(packed[rows, pl.ds(hp * 128, 128)], HDIM ** -0.5)
        acc[hp] = jnp.zeros((128, 256), jnp.float32)
        stat[hp, 0] = jnp.full((1, 256), NEG, jnp.float32)
        stat[hp, 1] = jnp.zeros((1, 256), jnp.float32)
    sq = segq[:, rows]
    sq2 = jnp.concatenate([sq, sq], axis=1)

    def body(kb, carry):
        keys = pl.ds(pl.multiple_of(kb * BLK, BLK), BLK)
        allowed = segk[keys, :] == sq2
        d = jnp.clip(kb - i, -2, 2) + 2
        for hp in range(PAIRS):
            s = dot_nt(packed[keys, pl.ds(D + hp * 128, 128)], qm[hp])
            s = jnp.where(allowed, s + bias[hp, d], NEG)
            old = stat[hp, 0]
            new = jnp.maximum(old, jnp.max(s, axis=0, keepdims=True))
            p = jnp.exp(s - new)
            alpha = jnp.exp(old - new)
            stat[hp, 0] = new
            stat[hp, 1] = stat[hp, 1] * alpha + jnp.sum(p, axis=0, keepdims=True)
            acc[hp] = acc[hp] * alpha + dot_nn(vt[pl.ds(hp * 128, 128), keys], p.astype(jnp.bfloat16))
        return carry

    lax.fori_loop(win[0, i], win[1, i], body, 0)
    for hp in range(PAIRS):
        total = stat[hp, 1]
        out[:, pl.ds(hp * 128, 128)] = join_heads(acc[hp] / total).T
        logsum[0, pl.ds(hp, 1), :] = stat[hp, 0] + jnp.log(total)


def attend(packed, segments, strips, win):
    length = packed.shape[0]
    blocks = length // BLK
    seg = segments.reshape(1, length)
    whole = lambda shape: pl.BlockSpec(shape, lambda i, w: (0,) * len(shape))
    return pl.pallas_call(
        attend_kernel,
        out_shape=(
            jax.ShapeDtypeStruct((length, D), jnp.float32),
            jax.ShapeDtypeStruct((blocks, PAIRS, 256), jnp.float32),
            jax.ShapeDtypeStruct((PAIRS, 5, BLK, 256), jnp.float32),
        ),
        grid_spec=pltpu.PrefetchScalarGridSpec(
            num_scalar_prefetch=1,
            grid=(blocks,),
            in_specs=[whole((length, 3 * D)), whole((length, 1)), whole((1, length)), whole((HEADS, 5, 256))],
            out_specs=(
                pl.BlockSpec((BLK, D), lambda i, w: (i, 0)),
                pl.BlockSpec((1, PAIRS, 256), lambda i, w: (i, 0, 0)),
                whole((PAIRS, 5, BLK, 256)),
            ),
            scratch_shapes=[
                pltpu.VMEM((D, length), jnp.bfloat16),
                pltpu.VMEM((PAIRS, 256, 128), jnp.bfloat16),
                pltpu.VMEM((PAIRS, 128, 256), jnp.float32),
                pltpu.VMEM((PAIRS, 2, 1, 256), jnp.float32),
            ],
        ),
        compiler_params=pltpu.CompilerParams(vmem_limit_bytes=48 * 2**20),
        cost_estimate=pl.CostEstimate(flops=2 * 10**10, bytes_accessed=10**7, transcendentals=6 * 10**6),
        name="attend",
    )(win, packed, seg.reshape(length, 1), seg, strips)


def unskew(tile):
    row = lax.broadcasted_iota(jnp.int32, tile.shape, 0)
    width = tile.shape[1]
    for bit in range(7):
        step = 1 << bit
        tile = jnp.where((row & step) != 0, pltpu.roll(tile, width - step, 1), tile)
    return tile


def attend_back_kernel(win, packed, grads, attended, segk, segq, bias, logsum, out, tab, kt, qm, om, dqt, dk, dv, gt):
    i = pl.program_id(0)
    last = pl.num_programs(0) - 1

    @pl.when(i == 0)
    def _():
        for hp in range(PAIRS):
            kt[pl.ds(hp * 128, 128), :] = packed[:, pl.ds(D + hp * 128, 128)].T
        dk[...] = jnp.zeros_like(dk)
        dv[...] = jnp.zeros_like(dv)
        gt[...] = jnp.zeros_like(gt)

    rows = pl.ds(pl.multiple_of(i * BLK, BLK), BLK)
    dots = []
    for hp in range(PAIRS):
        cols = pl.ds(hp * 128, 128)
        qm[hp] = split_heads(packed[rows, cols], HDIM ** -0.5)
        om[hp] = split_heads(grads[:, cols], 1.0)
        cross = (grads[:, cols].astype(jnp.float32) * attended[:, cols]).T
        dots.append(jnp.concatenate([
            jnp.sum(cross[:HDIM], axis=0, keepdims=True),
            jnp.sum(cross[HDIM:], axis=0, keepdims=True)], axis=1))
        dqt[hp] = jnp.zeros((128, 256), jnp.float32)
    sq = segq[:, rows]
    sq2 = jnp.concatenate([sq, sq], axis=1)

    def body(kb, carry):
        keys = pl.ds(pl.multiple_of(kb * BLK, BLK), BLK)
        allowed = segk[keys, :] == sq2
        d = jnp.clip(kb - i, -2, 2) + 2
        for hp in range(PAIRS):
            cols = pl.ds(hp * 128, 128)
            s = dot_nt(packed[keys, pl.ds(D + hp * 128, 128)], qm[hp]) + bias[hp, d]
            p = jnp.exp(jnp.where(allowed, s, NEG) - logsum[0, pl.ds(hp, 1), :])
            dp = dot_nt(packed[keys, pl.ds(2 * D + hp * 128, 128)], om[hp])
            ds = p * (dp - dots[hp])
            gt[hp, d] += ds
            low = ds.astype(jnp.bfloat16)
            dv[keys, cols] += dot_nn(p.astype(jnp.bfloat16), om[hp])
            dk[keys, cols] += dot_nn(low, qm[hp])
            dqt[hp] += dot_nn(kt[cols, keys], low)
        return carry

    lax.fori_loop(win[0, i], win[1, i], body, 0)
    for hp in range(PAIRS):
        out[rows, pl.ds(hp * 128, 128)] = (join_heads(dqt[hp]).T * (HDIM ** -0.5)).astype(jnp.bfloat16)

    @pl.when(i == last)
    def _():
        out[:, pl.ds(D, D)] = dk[...].astype(jnp.bfloat16)
        out[:, pl.ds(2 * D, D)] = dv[...].astype(jnp.bfloat16)
        for hp in range(PAIRS):
            for half in range(2):
                for d in range(5):
                    tile = gt[hp, d, :, pl.ds(half * BLK, BLK)]
                    tile = jnp.concatenate([tile, jnp.zeros_like(tile)], axis=1)
                    if 0 < d < 4:
                        tile = unskew(tile)
                    tab[2 * hp + half, pl.ds(d, 1), :] = jnp.sum(tile, axis=0, keepdims=True)


def attend_back(packed, grads, attended, segments, bias, logsum, win):
    length = packed.shape[0]
    blocks = length // BLK
    seg = segments.reshape(1, length)
    whole = lambda shape: pl.BlockSpec(shape, lambda i, w: (0,) * len(shape))
    return pl.pallas_call(
        attend_back_kernel,
        out_shape=(
            jax.ShapeDtypeStruct((length, 3 * D), jnp.bfloat16),
            jax.ShapeDtypeStruct((HEADS, 5, 256), jnp.float32),
        ),
        grid_spec=pltpu.PrefetchScalarGridSpec(
            num_scalar_prefetch=1,
            grid=(blocks,),
            in_specs=[
                whole((length, 3 * D)),
                pl.BlockSpec((BLK, D), lambda i, w: (i, 0)),
                pl.BlockSpec((BLK, D), lambda i, w: (i, 0)),
                whole((length, 1)),
                whole((1, length)),
                whole((PAIRS, 5, BLK, 256)),
                pl.BlockSpec((1, PAIRS, 256), lambda i, w: (i, 0, 0)),
            ],
            out_specs=(whole((length, 3 * D)), whole((HEADS, 5, 256))),
            scratch_shapes=[
                pltpu.VMEM((D, length), jnp.bfloat16),
                pltpu.VMEM((PAIRS, 256, 128), jnp.bfloat16),
                pltpu.VMEM((PAIRS, 256, 128), jnp.bfloat16),
                pltpu.VMEM((PAIRS, 128, 256), jnp.float32),
                pltpu.VMEM((length, D), jnp.float32),
                pltpu.VMEM((length, D), jnp.float32),
                pltpu.VMEM((PAIRS, 5, BLK, 256), jnp.float32),
            ],
        ),
        compiler_params=pltpu.CompilerParams(vmem_limit_bytes=56 * 2**20),
        cost_estimate=pl.CostEstimate(flops=5 * 10**10, bytes_accessed=2 * 10**7, transcendentals=6 * 10**6),
        name="attend_back",
    )(win, packed, grads, attended, seg.reshape(length, 1), seg, bias, logsum)


MESH = pl.DeviceIdType.MESH


class Place:
    def __init__(self, lines, rows):
        self.lines, self.rows = lines, rows
        wide, narrow = lax.axis_index("wide"), lax.axis_index("narrow")
        self.line, self.side = wide // 2, wide % 2
        self.row, self.core = narrow // 2, narrow % 2

    def device(self, line=None, side=None, row=None, core=None):
        line = self.line if line is None else line
        side = self.side if side is None else side
        row = self.row if row is None else row
        core = self.core if core is None else core
        return (line * 2 + side, row * 2 + core)

    def line_peer(self, k):
        return lax.rem(self.line + k, self.lines)

    def line_source(self, k):
        return lax.rem(self.line + self.lines - k, self.lines)

    def row_peer(self, k):
        return lax.rem(self.row + k, self.rows)

    def row_source(self, k):
        return lax.rem(self.row + self.rows - k, self.rows)

    def plane_peers(self):
        steps = [(k // self.rows, k % self.rows) for k in range(1, 2 * self.rows)]
        return [self.device(side=lax.rem(self.side + a, 2), row=self.row_peer(b)) for a, b in steps]

    def greet(self):
        barrier = pltpu.get_barrier_semaphore()
        targets = [self.device(line=self.line_peer(k)) for k in range(1, self.lines)]
        targets += self.plane_peers() + [self.device(core=1 - self.core)]
        for target in targets:
            pl.semaphore_signal(barrier, inc=1, device_id=target, device_id_type=MESH)
        pl.semaphore_wait(barrier, len(targets))


class Sends:
    def __init__(self, send_sems, recv_sems):
        self.send_sems, self.recv_sems, self.used = send_sems, recv_sems, 0
        self.started = []

    def start(self, src, dst, device):
        copy = pltpu.make_async_remote_copy(
            src_ref=src, dst_ref=dst, send_sem=self.send_sems.at[self.used], recv_sem=self.recv_sems.at[self.used],
            device_id=device, device_id_type=MESH)
        copy.start()
        self.used += 1
        self.started.append(copy)
        return copy

    def finish(self):
        for copy in self.started:
            copy.wait_send()


def gather_copies(lines, rows):
    return (lines - 1) + 1 + (rows - 1) + 1 + 1 + (rows - 1) + 1


class Gather:
    def __init__(self, place, sends, shard, out, local_sem, region, side_first):
        self.p, self.s, self.out, self.region = place, sends, out, region
        self.shard, self.local_sem, self.side_first = shard.at[region], local_sem, side_first
        self.cores = []

    def at(self, line, side, row):
        return self.out.at[(line, side, row, self.p.core) + self.region]

    def begin(self):
        p = self.p
        mine = self.at(p.line, p.side, p.row)
        self.local = pltpu.make_async_copy(self.shard, mine, self.local_sem)
        self.local.start()
        self.stage = [self.s.start(self.shard, mine, p.device(line=p.line_peer(k))) for k in range(1, p.lines)]

    def across(self, src):
        self.cores.append(self.s.start(src, src, self.p.device(core=1 - self.p.core)))

    def to_side(self, src):
        self.stage.append(self.s.start(src, src, self.p.device(side=1 - self.p.side)))

    def to_rows(self, src):
        p = self.p
        self.stage += [self.s.start(src, src, p.device(row=p.row_peer(k))) for k in range(1, p.rows)]

    def arrived(self):
        for copy in self.stage:
            copy.wait_recv()
        self.stage = []

    def second(self):
        p, every = self.p, slice(None)
        self.local.wait()
        self.arrived()
        mine = self.at(every, p.side, p.row)
        (self.to_side if self.side_first else self.to_rows)(mine)
        self.across(mine)

    def third(self):
        p, every = self.p, slice(None)
        self.arrived()
        if self.side_first:
            self.to_rows(self.at(every, every, p.row))
            self.across(self.at(every, 1 - p.side, p.row))
        else:
            self.to_side(self.at(every, p.side, every))
            for k in range(1, p.rows):
                self.across(self.at(every, p.side, p.row_source(k)))

    def fourth(self):
        p, every = self.p, slice(None)
        self.arrived()
        if self.side_first:
            for k in range(1, p.rows):
                self.across(self.at(every, every, p.row_source(k)))
        else:
            self.across(self.at(every, 1 - p.side, every))

    def last(self):
        for copy in self.cores:
            copy.wait_recv()


class HalfGather(Gather):
    def at(self, line, side, row):
        return self.out.at[line, side if self.side_first else row]

    def across(self, src):
        pass

    def third(self):
        self.arrived()

    def fourth(self):
        pass

    def last(self):
        pass


class Total:
    def __init__(self, place, sends, x, core_in, plane, line_in):
        self.p, self.s, self.x, self.core_in, self.plane, self.line_in = place, sends, x, core_in, plane, line_in

    def begin(self):
        p = self.p
        self.stage = [self.s.start(self.x, self.core_in, p.device(core=1 - p.core))]

    def second(self):
        p = self.p
        for copy in self.stage:
            copy.wait_recv()
        here = p.side * p.rows + p.row
        self.plane[here] = self.x[...] + self.core_in[...]
        self.stage = [self.s.start(self.plane.at[here], self.plane.at[here], t) for t in p.plane_peers()]

    def third(self):
        p = self.p
        for copy in self.stage:
            copy.wait_recv()
        total = self.plane[0]
        for k in range(1, 2 * p.rows):
            total = total + self.plane[k]
        self.line_in[p.line] = total
        mine = self.line_in.at[p.line]
        self.stage = [self.s.start(mine, mine, p.device(line=p.line_peer(k))) for k in range(1, p.lines)]

    def last(self):
        for copy in self.stage:
            copy.wait_recv()
        total = self.line_in[0]
        for k in range(1, self.p.lines):
            total = total + self.line_in[k]
        return total


def total_buffers(lines, rows, shape, dtype):
    return [
        pltpu.VMEM(shape, dtype),
        pltpu.VMEM(shape, dtype),
        pltpu.VMEM((2 * rows,) + shape, dtype),
        pltpu.VMEM((lines,) + shape, dtype),
    ]


def total_copies(lines, rows):
    return 2 * rows + lines - 1


def gelu(v):
    return 0.5 * v * (1.0 + jnp.tanh(0.7978845608028654 * (v + 0.044715 * (v * v * v))))


def spread(vector, me, total):
    n = vector.shape[1]
    lane = lax.broadcasted_iota(jnp.int32, (n, total), 1)
    row = lax.broadcasted_iota(jnp.int32, (n, total), 0)
    hot = jnp.where(lane == me * n + row, 1.0, 0.0).astype(jnp.bfloat16)
    return dot_nn(vector, hot)


def matrix(ref):
    block = ref[...].astype(jnp.float32)
    return block.reshape(-1, block.shape[-1]).astype(jnp.bfloat16)


def shifted(values, row_off, col_off, side):
    count = values.shape[0]
    step = row_off * side + col_off
    moved = pltpu.roll(values, (-step) % count, 0) if step % count else values
    patch = lax.broadcasted_iota(jnp.int32, (count, 1), 0)
    row, col = patch // side + row_off, lax.rem(patch, side) + col_off
    inside = (row >= 0) & (row < side) & (col >= 0) & (col < side)
    return jnp.where(inside, moved, 0.0)


FRONT_VECTORS = 7


def front_kernel(lines, rows, side, whole, pieces, number, *refs):
    refs = list(refs)

    def take(n):
        out = refs[:n]
        del refs[:n]
        return out

    (at,) = take(1)
    vectors = take(FRONT_VECTORS)
    (stem, tokens) = take(2)
    shards = take(number)
    held_outs, half_outs = take(FULL), take(number - FULL)
    (gains_out, pre_first_out, columns_out, pre_second_out, second_out, unit_out, inv) = take(7)
    (joined_out, start_out, normed_out, packed_out) = take(4)
    outs = take(FULL) + half_outs
    (gains, pre_first, columns, pre_second, second, unit, joined, start, normed, packed) = take(10)
    mats = take(5)
    (placing,) = take(1)
    held_bufs, sum_bufs = take(4), take(4)
    send_sems, recv_sems, local_sems, out_sems = take(4)
    place = Place(lines, rows)
    place.greet()
    sends = Sends(send_sems, recv_sems)

    me = (place.line * 2 + place.side) * (2 * rows) + place.row * 2 + place.core
    held = held_bufs[0]
    held[...] = jnp.zeros_like(held)
    devices = 4 * lines * rows

    parts = []
    for i, (which, region, side_first) in enumerate(pieces):
        region = tuple(pl.ds(*item) for item in region)
        kind = Gather if which < FULL else HalfGather
        parts.append(kind(place, sends, shards[which], outs[which], local_sems.at[i], region, side_first))
    batches = [[part for part, piece in zip(parts, pieces) if piece[0] in which] for which in ((0, 1), (2, 3), (4,), (5, 6, 7))]

    def run(batch, *names):
        for name in names:
            for part in batches[batch]:
                getattr(part, name)()

    copies_out = []

    def emit(value, out):
        copy = pltpu.make_async_copy(value, out, out_sems.at[len(copies_out)])
        copy.start()
        copies_out.append(copy)

    run(0, "begin")
    run(1, "begin")
    for v, (ref, row) in enumerate(zip(vectors[:6], (2, 3, 4, 5, 0, 1))):
        n = ref.shape[1]
        line = spread(ref[...], me, n * devices).astype(jnp.bfloat16)
        for k in range(0, n * devices, 1024):
            span = min(1024, n * devices - k)
            held[pl.ds(row + k // 1024, 1), pl.ds(0, span)] = line[:, k : k + span]
    table = spread(vectors[6][...], me, vectors[6].shape[1] * devices).astype(jnp.bfloat16)
    for h in range(HEADS):
        held[pl.ds(8 + h // 4, 1), pl.ds(h % 4 * 256, 256)] = table[h : h + 1, :]
    vector_total = Total(place, sends, *held_bufs)
    vector_total.begin()

    run(0, "second")
    vector_total.second()
    run(2, "begin")
    run(0, "third")
    run(1, "second")
    vector_total.third()
    run(0, "fourth")
    run(1, "third")
    run(2, "second")
    run(3, "begin")
    run(0, "last")
    count = side * side
    w_reduce, w_spatial, w_expand, w_embed, w_qkv = mats
    w_reduce[...] = matrix(outs[0])
    pre = dot_nn(stem[...], w_reduce[...])
    pre_first[...] = pre
    emit(pre_first, pre_first_out)
    first = gelu(pre).astype(jnp.bfloat16).astype(jnp.float32)
    channels = first.shape[1]
    for r in range(3):
        for c in range(3):
            k = r * 3 + c
            columns[:, pl.ds(k * channels, channels)] = shifted(first, r - 1, c - 1, side).astype(jnp.bfloat16)
    emit(columns, columns_out)
    w_spatial[...] = matrix(outs[1])
    pre = dot_nn(columns[...], w_spatial[...])
    pre_second[...] = pre
    emit(pre_second, pre_second_out)
    second[...] = gelu(pre).astype(jnp.bfloat16)
    emit(second, second_out)
    run(1, "fourth")
    run(2, "third")
    run(1, "last")
    w_expand[...] = matrix(outs[2])
    sums = sum_bufs[0]
    sums[...] = jnp.zeros_like(sums)

    def expand(cols):
        third = dot_nn(second[...], w_expand[:, cols])
        unit[:, cols] = third
        sums[pl.ds(0, 1), cols] = jnp.sum(third, axis=0, keepdims=True)
        sums[pl.ds(1, 1), cols] = jnp.sum(third * third, axis=0, keepdims=True)

    tile_loop(unit.shape[1], expand)
    norm_total = Total(place, sends, *sum_bufs)
    norm_total.begin()
    run(2, "fourth")
    norm_total.second()
    gains[...] = vector_total.last().astype(jnp.float32)
    emit(gains, gains_out)
    w_embed[...] = matrix(outs[3])
    norm_total.third()
    run(3, "second")
    for held_weight, out in zip(outs[:4], held_outs):
        emit(held_weight, out)
    totals = norm_total.last()
    mean = totals[0:1] / whole
    inv_std = lax.rsqrt(totals[1:2] / whole - mean * mean + epsilon)
    inv[...] = jnp.broadcast_to(inv_std, inv.shape)

    third_rows = count // 3

    def join(i, carry):
        at_rows = pl.ds(pl.multiple_of(i * third_rows, third_rows), third_rows)
        value = (unit[at_rows, :] - mean) * inv_std
        unit[at_rows, :] = value
        pre_joined = value * gains[0:1, :] + gains[1:2, :] + stem[at_rows, :].astype(jnp.float32)
        joined[at_rows, :] = gelu(pre_joined).astype(jnp.bfloat16)
        return carry

    lax.fori_loop(0, 3, join, 0)
    emit(unit, unit_out)
    emit(joined, joined_out)
    length, width = start.shape
    token = lax.broadcasted_iota(jnp.int32, (length, count), 0)
    patch = lax.broadcasted_iota(jnp.int32, (length, count), 1)
    placing[...] = jnp.where(token - patch == at[0], 1.0, 0.0).astype(jnp.bfloat16)

    def embed(cols):
        value = dot_nn(joined[...], w_embed[:, cols])
        high = value.astype(jnp.bfloat16)
        low = (value - high.astype(jnp.float32)).astype(jnp.bfloat16)
        moved = dot_nn(placing[...], high) + dot_nn(placing[...], low)
        start[:, cols] = tokens[:, cols].astype(jnp.float32) + moved

    tile_loop(width, embed)
    gain = gains[2:3, :width]

    def norm(i, carry):
        at_rows = pl.ds(pl.multiple_of(i * 128, 128), 128)
        value = start[at_rows, :]
        centred = value - jnp.mean(value, axis=-1, keepdims=True)
        scale = lax.rsqrt(jnp.mean(centred * centred, axis=-1, keepdims=True) + epsilon)
        normed[at_rows, :] = (centred * scale * gain).astype(jnp.bfloat16)
        return carry

    emit(start, start_out)
    lax.fori_loop(0, length // 128, norm, 0)
    emit(normed, normed_out)
    run(2, "last")
    emit(outs[4], held_outs[4])
    w_qkv[...] = matrix(outs[4])

    def project(cols):
        packed[:, cols] = dot_nn(normed[...], w_qkv[:, cols]).astype(jnp.bfloat16)

    tile_loop(packed.shape[1], project)
    emit(packed, packed_out)
    run(3, "third")
    sends.finish()
    for copy in copies_out:
        copy.wait()


FULL = 5


def front(first_at, vectors, stem, tokens, shards, side, collective_id):
    wide, narrow = lax.axis_size("wide"), lax.axis_size("narrow")
    lines, rows = wide // 2, narrow // 2
    devices = wide * narrow
    number = len(shards)
    pieces = []
    for i, item in enumerate(shards):
        r, c = item.shape
        if i == 4:
            pieces += [(i, ((0, r), (k * c // 2, c // 2)), k == 0) for k in range(2)]
        else:
            pieces.append((i, ((0, r), (0, c)), i in (0, 2, 5, 7)))
    copies = len(pieces) * gather_copies(lines, rows) + 2 * total_copies(lines, rows)
    count, length = side * side, tokens.shape[0]
    mid = shards[0].shape[1]
    wide_in = stem.shape[1]
    f32, bf16 = jnp.float32, jnp.bfloat16
    leads = [(lines, 2, rows, 2)] * FULL + [(lines, 2), (lines, rows), (lines, 2)]
    gathered = [jax.ShapeDtypeStruct(lead + s.shape, s.dtype) for lead, s in zip(leads, shards)]
    kept = [
        ((16, 1024), f32),
        ((count, mid), f32),
        ((count, 9 * mid), bf16),
        ((count, mid), f32),
        ((count, mid), bf16),
        ((count, wide_in), f32),
        ((8, wide_in), f32),
        ((count, wide_in), bf16),
        ((length, D), f32),
        ((length, D), bf16),
        ((length, 3 * D), bf16),
    ]
    vmem = pl.BlockSpec(memory_space=pltpu.VMEM)
    anywhere = pl.BlockSpec(memory_space=pl.ANY)
    scratch = [pltpu.VMEM(item.shape, item.dtype) for item in gathered[:FULL]]
    scratch += [pltpu.VMEM(shape, dtype) for k, (shape, dtype) in enumerate(kept) if k != 6]
    scratch += [pltpu.VMEM((s.shape[0] * devices, s.shape[1]), bf16) for s in shards[:5]]
    scratch += [pltpu.VMEM((length, count), bf16)]
    scratch += total_buffers(lines, rows, (16, 1024), bf16)
    scratch += total_buffers(lines, rows, (8, 1024), f32)
    scratch += [pltpu.SemaphoreType.DMA((copies,)), pltpu.SemaphoreType.DMA((copies,)), pltpu.SemaphoreType.DMA((len(pieces),)), pltpu.SemaphoreType.DMA((FULL + 10,))]
    results = pl.pallas_call(
        functools.partial(front_kernel, lines, rows, side, float(count * devices), pieces, number),
        out_shape=gathered + [jax.ShapeDtypeStruct(s, d) for s, d in kept],
        in_specs=[pl.BlockSpec(memory_space=pltpu.SMEM)] + [vmem] * (FRONT_VECTORS + 2) + [anywhere] * number,
        out_specs=[anywhere] * number + [vmem if k == 6 else anywhere for k in range(len(kept))],
        scratch_shapes=scratch,
        compiler_params=pltpu.CompilerParams(collective_id=collective_id, has_side_effects=True, vmem_limit_bytes=60 * 2**20),
        cost_estimate=pl.CostEstimate(flops=6 * 10**9, bytes_accessed=7 * 10**7, transcendentals=10**6),
        name="front",
    )(first_at, *vectors, stem, tokens, *shards)
    return results[:number], results[number:]


def gelu_slope(v):
    t = jnp.tanh(0.7978845608028654 * (v + 0.044715 * (v * v * v)))
    return 0.5 * (1.0 + t) + 0.5 * v * (1.0 - t * t) * (0.7978845608028654 * (1.0 + 0.134145 * (v * v)))


def row_mean(values):
    return jnp.mean(values, axis=-1, keepdims=True)


def unit_of(values):
    centred = values - row_mean(values)
    inv_std = lax.rsqrt(row_mean(centred * centred) + epsilon)
    return centred * inv_std, inv_std


def unit_back(weighted, unit_rows, inv_std):
    return inv_std * (weighted - row_mean(weighted) - unit_rows * row_mean(weighted * unit_rows))


def column_sum(values):
    return jnp.sum(values, axis=0, keepdims=True)


FTILE = 512


def middle_kernel(lines, rows, counts, *refs):
    refs = list(refs)

    def take(n):
        out = refs[:n]
        del refs[:n]
        return out

    attended, start, d_out, gains, scale = take(5)
    outs_in, ups_in, downs_in = take(counts[0]), take(counts[1]), take(counts[2])
    mixed, mixed_low, normed2, narrowed, grad_up, grad_middle, branch, grad_attended, sums = take(9)
    held = take(3)
    mats = take(3)
    pre, act, weighted = take(3)
    send_sems, recv_sems, local_sems = take(3)
    i = pl.program_id(0)
    w_out, w_up, w_down = mats
    width, hidden = w_up.shape

    @pl.when(i == 0)
    def _():
        place = Place(lines, rows)
        partner = place.device(core=1 - place.core)
        barrier = pltpu.get_barrier_semaphore()
        pl.semaphore_signal(barrier, inc=1, device_id=partner, device_id_type=MESH)
        pl.semaphore_wait(barrier, 1)
        sends = Sends(send_sems, recv_sems)
        waits = []
        for full, pieces in zip(held, (outs_in, ups_in, downs_in)):
            group = []
            for k, piece in enumerate(pieces):
                if full is held[1]:
                    side = place.side if k == 0 else 1 - place.side
                    spot = full.at[:, side, :, place.core]
                else:
                    spot = full.at[:, :, place.row_source(k), place.core]
                local = pltpu.make_async_copy(piece, spot, local_sems.at[sends.used])
                local.start()
                group.append((sends.start(piece, spot, partner), local))
            waits.append(group)
        for full, mat, group in zip(held, mats, waits):
            for copy, local in group:
                copy.wait_recv()
                local.wait()
            tall = mat.shape[0] // (2 * lines)

            def convert(k, carry, full=full, mat=mat, tall=tall):
                block = full[k // 2, lax.rem(k, 2)].astype(jnp.float32)
                mat[pl.ds(pl.multiple_of(k * tall, tall), tall), :] = block.reshape(tall, mat.shape[1]).astype(mat.dtype)
                return carry

            lax.fori_loop(0, 2 * lines, convert, 0)
        sends.finish()
        sums[...] = jnp.zeros_like(sums)

    gain_attn, gain_mid = gains[3:4, :width], gains[4:5, :width]
    scaled = attended[...] * scale[...]
    unit1, inv1 = unit_of(scaled)
    low = (unit1 * gain_attn).astype(jnp.bfloat16)
    mixed_low[...] = low
    middle = start[...] + dot_nn(low, w_out[...])
    unit2, inv2 = unit_of(middle)
    low2 = (unit2 * gain_mid).astype(jnp.bfloat16)
    normed2[...] = low2
    tiles = hidden // FTILE
    count = middle.shape[0]
    zero = jnp.zeros((count, 1), jnp.float32)

    def span(f):
        return pl.ds(pl.multiple_of(f * FTILE, FTILE), FTILE)

    def gain_of(f):
        per = 1024 // FTILE
        return gains[pl.ds(5 + f // per, 1), f % per * FTILE : (f % per + 1) * FTILE]

    total = zero
    for f in range(tiles):
        cols = pl.ds(f * FTILE, FTILE)
        value = dot_nn(low2, w_up[:, cols])
        pre[:, cols] = value
        value = gelu(value)
        act[:, cols] = value
        total = total + jnp.sum(value, axis=-1, keepdims=True)
    mean = total / hidden
    total = zero
    for f in range(tiles):
        cols = pl.ds(f * FTILE, FTILE)
        centred = act[:, cols] - mean
        total = total + jnp.sum(centred * centred, axis=-1, keepdims=True)
    inv3 = lax.rsqrt(total / hidden + epsilon)
    result = middle
    cross1, cross2 = zero, zero
    for f in range(tiles):
        cols = pl.ds(f * FTILE, FTILE)
        unit3 = (act[:, cols] - mean) * inv3
        act[:, cols] = unit3
        gain = gain_of(f)
        low3 = (unit3 * gain).astype(jnp.bfloat16)
        narrowed[:, cols] = low3
        result = result + dot_nn(low3, w_down[cols, :])
        grad = dot_nt(d_out[...], w_down[cols, :])
        sums[0:1, cols] += column_sum(grad * unit3)
        grad = grad * gain
        weighted[:, cols] = grad
        cross1 = cross1 + jnp.sum(grad, axis=-1, keepdims=True)
        cross2 = cross2 + jnp.sum(grad * unit3, axis=-1, keepdims=True)
    mixed[...] = result.astype(jnp.bfloat16)
    cross1, cross2 = cross1 / hidden, cross2 / hidden
    grad2 = jnp.zeros((count, width), jnp.float32)
    for f in range(tiles):
        cols = pl.ds(f * FTILE, FTILE)
        grad = inv3 * (weighted[:, cols] - cross1 - act[:, cols] * cross2)
        grad = (gelu_slope(pre[:, cols]) * grad).astype(jnp.bfloat16)
        grad_up[:, cols] = grad
        grad2 = grad2 + dot_nt(grad, w_up[:, cols])
    sums[1:2, :width] += column_sum(grad2 * unit2)
    grad_mid = d_out[...].astype(jnp.float32) + unit_back(grad2 * gain_mid, unit2, inv2)
    grad_middle[...] = grad_mid
    low = grad_mid.astype(jnp.bfloat16)
    branch[...] = low
    grad1 = dot_nt(low, w_out[...])
    sums[2:3, :width] += column_sum(grad1 * unit1)
    grad_scaled = unit_back(grad1 * gain_attn, unit1, inv1)
    sums[3:4, :width] += column_sum(grad_scaled * attended[...])
    grad_attended[...] = (grad_scaled * scale[...]).astype(jnp.bfloat16)


def middle_part(attended, start, d_out, gains, scale_row, outs_in, ups_in, downs_in, hidden, collective_id):
    wide, narrow = lax.axis_size("wide"), lax.axis_size("narrow")
    lines, rows = wide // 2, narrow // 2
    length, width = start.shape
    block = 256
    f32, bf16 = jnp.float32, jnp.bfloat16
    counts = (len(outs_in), len(ups_in), len(downs_in))
    copies = sum(counts)

    def by_token(columns):
        return pl.BlockSpec((block, columns), lambda i: (i, 0))

    def whole(shape):
        return pl.BlockSpec(shape, lambda i: (0,) * len(shape))

    anywhere = pl.BlockSpec(memory_space=pl.ANY)
    pieces = list(outs_in) + list(ups_in) + list(downs_in)
    results = [(width, bf16), (width, bf16), (width, bf16), (hidden, bf16), (hidden, bf16), (width, f32), (width, bf16), (width, bf16)]
    shapes = [(width, width), (width, hidden), (hidden, width)]
    devices = wide * narrow
    return pl.pallas_call(
        functools.partial(middle_kernel, lines, rows, counts),
        out_shape=[jax.ShapeDtypeStruct((length, c), d) for c, d in results] + [jax.ShapeDtypeStruct((8, hidden), f32)],
        grid=(length // block,),
        in_specs=[by_token(width), by_token(width), by_token(width), whole(gains.shape), whole(scale_row.shape)] + [anywhere] * copies,
        out_specs=[by_token(c) for c, _ in results] + [whole((8, hidden))],
        scratch_shapes=[pltpu.VMEM((lines, 2, rows, 2, m // devices, n), bf16) for m, n in shapes]
        + [pltpu.VMEM(shape, bf16) for shape in shapes]
        + [pltpu.VMEM((block, hidden), f32)] * 3
        + [pltpu.SemaphoreType.DMA((copies,))] * 3,
        compiler_params=pltpu.CompilerParams(collective_id=collective_id, has_side_effects=True, vmem_limit_bytes=60 * 2**20),
        cost_estimate=pl.CostEstimate(flops=22 * 10**9, bytes_accessed=6 * 10**7, transcendentals=7 * 10**6),
        name="middle_part",
    )(attended, start, d_out, gains, scale_row, *pieces)


def scatter_copies(lines, rows):
    return 1 + (rows - 1) + 1 + 1 + (rows - 1) + (lines - 1)


def add_loop(lead, fn):
    total = 1
    for size in lead:
        total *= size

    def body(i, carry):
        index = []
        for size in reversed(lead):
            index.append(lax.rem(i, size))
            i = i // size
        fn(tuple(reversed(index)))
        return carry

    lax.fori_loop(0, total, body, 0)


def plus(*terms):
    total = terms[0].astype(jnp.float32)
    for term in terms[1:]:
        total = total + term.astype(jnp.float32)
    return total


class Scatter:
    def __init__(self, place, sends, full, out, buffers):
        self.p, self.s, self.full, self.out = place, sends, full, out
        self.other, self.low1, self.high1, self.low2, self.high2, self.line0, self.lines_in = buffers
        cols = full.shape[-1]
        cut = cols // 256 * 128
        self.low, self.high = pl.ds(0, cut), pl.ds(cut, cols - cut)

    def begin(self):
        core = self.p.core
        self.stage = [self.s.start(self.full.at[:, :, :, 1 - core], self.other, self.p.device(core=1 - core))]

    def second(self):
        p, full, dtype = self.p, self.full, self.full.dtype
        for copy in self.stage:
            copy.wait_recv()

        def add(i):
            l, x, y = i
            full[l, x, y, p.core] = plus(full[l, x, y, p.core], self.other[l, x, y]).astype(dtype)

        add_loop(self.other.shape[:3], add)
        self.stage = [self.s.start(full.at[:, 1 - p.side, :, p.core, :, self.high], self.high1, p.device(side=1 - p.side))]
        for k in range(1, p.rows):
            to = p.row_peer(k)
            self.stage.append(self.s.start(full.at[:, :, to, p.core, :, self.low], self.low1.at[k - 1], p.device(row=to)))

    def third(self):
        p, full, dtype = self.p, self.full, self.full.dtype
        for copy in self.stage:
            copy.wait_recv()

        def add_low(i):
            l, x = i
            terms = [full[l, x, p.row, p.core, :, self.low]] + [self.low1[k, l, x] for k in range(p.rows - 1)]
            full[l, x, p.row, p.core, :, self.low] = plus(*terms).astype(dtype)

        def add_high(i):
            l, y = i
            full[l, p.side, y, p.core, :, self.high] = plus(full[l, p.side, y, p.core, :, self.high], self.high1[l, y]).astype(dtype)

        add_loop((p.lines, 2), add_low)
        add_loop((p.lines, p.rows), add_high)
        self.stage = [self.s.start(full.at[:, 1 - p.side, p.row, p.core, :, self.low], self.low2, p.device(side=1 - p.side))]
        for k in range(1, p.rows):
            to = p.row_peer(k)
            self.stage.append(self.s.start(full.at[:, p.side, to, p.core, :, self.high], self.high2.at[k - 1], p.device(row=to)))

    def fourth(self):
        p, full, dtype = self.p, self.full, self.full.dtype
        for copy in self.stage:
            copy.wait_recv()

        def add(i):
            (l,) = i
            self.line0[l, :, self.low] = plus(full[l, p.side, p.row, p.core, :, self.low], self.low2[l]).astype(dtype)
            terms = [full[l, p.side, p.row, p.core, :, self.high]] + [self.high2[k, l] for k in range(p.rows - 1)]
            self.line0[l, :, self.high] = plus(*terms).astype(dtype)

        add_loop((p.lines,), add)
        self.stage = []
        for k in range(1, p.lines):
            to = p.line_peer(k)
            self.stage.append(self.s.start(self.line0.at[to], self.lines_in.at[k - 1], p.device(line=to)))

    def last(self):
        p = self.p
        for copy in self.stage:
            copy.wait_recv()
        self.out[...] = plus(self.line0[p.line], *[self.lines_in[k] for k in range(p.lines - 1)])


def scatter_buffers(lines, rows, r, c, dtype):
    low = c // 256 * 128
    high = c - low
    return [
        pltpu.VMEM((lines, 2, rows, r, c), dtype),
        pltpu.VMEM((max(rows - 1, 1), lines, 2, r, low), dtype),
        pltpu.VMEM((lines, rows, r, high), dtype),
        pltpu.VMEM((lines, r, low), dtype),
        pltpu.VMEM((max(rows - 1, 1), lines, r, high), dtype),
        pltpu.VMEM((lines, r, c), dtype),
        pltpu.VMEM((max(lines - 1, 1), r, c), dtype),
    ]


NBUF = 7


def tile_loop(width, fn):
    full = width // 256

    def body(j, carry):
        fn(pl.ds(pl.multiple_of(j * 256, 256), 256))
        return carry

    lax.fori_loop(0, full, body, 0)
    if width % 256:
        fn(pl.ds(full * 256, width % 256))


def finish_kernel(lines, rows, products, side, whole, *refs):
    refs = list(refs)

    def take(n):
        out = refs[:n]
        del refs[:n]
        return out

    number, stems = len(products), 4
    lefts, rights = take(number), take(number)
    (embed_in, grad_joined, columns, stem) = take(4)
    (unit, gains, inv, pre_second, pre_first, second, w_expand, w_spatial, w_reduce, partial, pre_row, table) = take(12)
    count = number + stems
    outs = take(count)
    (features_out, totals_out) = take(2)
    fulls, buffers = take(count), take(count * NBUF)
    (xraw, xbuf, gbuf, third, tall, grad_second, grad_first, block) = take(8)
    sum_bufs = take(4)
    (xsem, gsem, in_sems, block_sems, send_sems, recv_sems) = take(6)
    place = Place(lines, rows)
    place.greet()
    sends = Sends(send_sems, recv_sems)
    parts = [Scatter(place, sends, fulls[i], outs[i], buffers[NBUF * i : NBUF * (i + 1)]) for i in range(count)]
    ready = [
        pltpu.make_async_copy(grad_joined, features_out, in_sems.at[0]),
        pltpu.make_async_copy(embed_in, fulls[number], in_sems.at[1]),
    ]
    for copy in ready:
        copy.start()

    core = place.core
    tasks = []
    for a, (kind, width) in enumerate(products):
        if kind == "rows":
            tasks += [(a, 0, None, None), (a, width, None, None)]
        else:
            for c in (1 - core, core):
                for y in range(rows):
                    pitch = rights[a].shape[1] // rows
                    first = y * pitch + c * (pitch - width)
                    tasks.append((a, first, y, c))

    def fetch_right(t):
        a, first, y, c = tasks[t]
        width = products[a][1]
        first = pl.multiple_of(jnp.int32(first), 128)
        return pltpu.make_async_copy(rights[a].at[:, pl.ds(first, width)], gbuf.at[t % 2, :, pl.ds(0, width)], gsem.at[t % 2])

    def fetch_left(a):
        return pltpu.make_async_copy(lefts[a], xraw, xsem.at[0])

    fetch_left(0).start()
    fetch_right(0).start()
    at_task = [0]

    def multiply():
        t = at_task[0]
        at_task[0] += 1
        a, first, y, c = tasks[t]
        kind, width = products[a]
        if t + 1 < len(tasks):
            fetch_right(t + 1).start()
        if t == 0 or tasks[t - 1][0] != a:
            fetch_left(a).wait()

            def turn(cols):
                xbuf[cols, :] = xraw[:, cols].T

            tile_loop(xraw.shape[1], turn)
            if a + 1 < number:
                fetch_left(a + 1).start()
        fetch_right(t).wait()
        full = fulls[a]

        def tile(cols):
            value = dot_nn(xbuf[...], gbuf[t % 2, :, cols])
            n = value.shape[1]
            if kind == "rows":
                spot = pl.ds(pl.multiple_of(cols.start + tasks[t][1], 128), n)
                full[:, :, :, :, :, spot] = value.reshape(lines, 2, rows, 2, -1, n).astype(full.dtype)
            else:
                full[:, :, y, c, :, cols] = value.reshape(lines, 2, -1, n).astype(full.dtype)

        tile_loop(width, tile)

    def product(a):
        if products[a][0] == "rows":
            multiply()
            multiply()
            parts[a].begin()
            return
        for _ in range(rows):
            multiply()
        parts[a].begin()
        for _ in range(rows):
            multiply()

    def from_tall(full):
        shards = full.shape[1:]
        span = shards[0] * shards[1] * shards[2] * shards[3]

        def move(i):
            (l,) = i
            value = tall[pl.ds(pl.multiple_of(l * span, span), span), :]
            full[l] = value.reshape(shards).astype(full.dtype)

        add_loop((lines,), move)

    patches, wide_in = unit.shape
    small = sum_bufs[0]
    width = pre_row.shape[1]
    small[...] = jnp.zeros_like(small)
    small[2:3, :width] = pre_row[...]
    small[3:4, :width] = partial[2:3, :width]
    small[4:5, :width] = partial[1:2, :width]
    for k in range(3):
        small[5 + k : 6 + k, :] = partial[0:1, k * 1024 : (k + 1) * 1024]
    small[8:11, :] = table[...]
    small[11:12, :width] = partial[3:4, :width]
    ready[0].wait()

    def channel_sums(cols):
        grad = features_out[:, cols]
        small[0:1, cols] = column_sum(grad)
        small[1:2, cols] = column_sum(grad * unit[:, cols])

    tile_loop(wide_in, channel_sums)
    total = Total(place, sends, *sum_bufs)
    total.begin()
    down, up, qkv, out, embed, expand, spatial, reduce_ = parts
    product(0)
    total.second()
    down.second()
    total.third()
    ready[1].wait()
    product(1)
    down.third()
    up.second()
    sums = total.last()
    totals_out[...] = sums
    shift, scale = sums[0:1] / whole, sums[1:2] / whole

    def third_tile(cols):
        gain = gains[0:1, cols]
        unit_cols = unit[:, cols]
        low = inv[0:1, cols] * gain * (features_out[:, cols] - shift_ref[0:1, cols] - unit_cols * shift_ref[1:2, cols])
        low = low.astype(jnp.bfloat16)
        third[:, cols] = low
        value = dot_nn(second[...].T, low)
        fulls[number + 1][:, :, :, :, :, cols] = value.reshape(lines, 2, rows, 2, -1, value.shape[1]).astype(jnp.bfloat16)

    shift_ref = sum_bufs[1]
    shift_ref[0:1, :] = shift
    shift_ref[1:2, :] = scale
    tile_loop(wide_in, third_tile)
    expand.begin()
    embed.begin()
    grad_second[...] = (gelu_slope(pre_second[...]) * dot_nt(third[...], w_expand[...])).astype(jnp.bfloat16)
    down.fourth()
    up.third()

    channels = grad_second.shape[1]

    def fetch_block(source, k):
        return pltpu.make_async_copy(source.at[:, pl.ds(k * channels, channels)], block.at[k % 2], block_sems.at[k % 2])

    fetch_block(columns, 0).start()
    patch = lax.broadcasted_iota(jnp.int32, (patches, 1), 0)
    for k in range(9):
        if k < 8:
            fetch_block(columns, k + 1).start()
        fetch_block(columns, k).wait()
        kernel_rows = pl.ds(k * channels, channels)
        tall[kernel_rows, :] = dot_nn(block[k % 2].T, grad_second[...])
        back = dot_nt(grad_second[...], w_spatial[kernel_rows, :])
        row_off, col_off = k // 3 - 1, k % 3 - 1
        row, col = patch // side + row_off, lax.rem(patch, side) + col_off
        inside = (row >= 0) & (row < side) & (col >= 0) & (col < side)
        step = (row_off * side + col_off) % patches
        back = jnp.where(inside, back, 0.0)
        back = pltpu.roll(back, step, 0) if step else back
        grad_first[...] = back if k == 0 else grad_first[...] + back
    from_tall(fulls[number + 2])
    spatial.begin()
    expand.second()
    embed.second()
    product(2)
    up.fourth()
    low = (gelu_slope(pre_first[...]) * grad_first[...]).astype(jnp.bfloat16)
    grad_second[...] = low

    fetch_block(stem, 0).start()
    for k in range(wide_in // channels):
        if (k + 1) * channels < wide_in:
            fetch_block(stem, k + 1).start()
        fetch_block(stem, k).wait()
        tall[pl.ds(k * channels, channels), :] = dot_nn(block[k % 2].T, grad_second[...])
    from_tall(fulls[number + 3])
    reduce_.begin()
    spatial.second()
    expand.third()
    embed.third()
    qkv.second()
    product(3)

    def feature_tile(cols):
        features_out[:, cols] += dot_nt(grad_second[...], w_reduce[cols, :])

    reduce_.second()
    tile_loop(wide_in, feature_tile)
    spatial.third()
    expand.fourth()
    embed.fourth()
    qkv.third()
    out.second()
    reduce_.third()
    spatial.fourth()
    down.last()
    up.last()
    qkv.fourth()
    out.third()
    reduce_.fourth()
    expand.last()
    embed.last()
    out.fourth()
    spatial.last()
    qkv.last()
    reduce_.last()
    out.last()
    sends.finish()


def finish(products, stem_grads, inputs, side, collective_id):
    wide, narrow = lax.axis_size("wide"), lax.axis_size("narrow")
    lines, rows = wide // 2, narrow // 2
    devices = wide * narrow
    shapes, plan = [], []
    for left, right, kind in products:
        m, n = left.shape[1], right.shape[1]
        if kind == "rows":
            width = n // 2
            shapes.append((lines, 2, rows, 2, m // devices, n))
        else:
            width = -(-(n // (2 * rows)) // 128) * 128
            shapes.append((lines, 2, rows, 2, m // (2 * lines), width))
        plan.append((kind, width))
    embed, grad_joined, columns, stem = stem_grads
    w_expand, w_spatial, w_reduce = inputs[6:9]
    shapes.append(embed.shape)
    for item in (w_expand, w_spatial, w_reduce):
        shapes.append((lines, 2, rows, 2, item.shape[0] // devices, item.shape[1]))
    count = len(shapes)
    copies = count * scatter_copies(lines, rows) + total_copies(lines, rows)
    f32, dtype = jnp.float32, jnp.bfloat16
    scratch = [pltpu.VMEM(s, dtype) for s in shapes]
    for s in shapes:
        scratch += scatter_buffers(lines, rows, s[-2], s[-1], dtype)
    t, m = products[0][0].shape
    widest = max(width for _, width in plan)
    patches, mid = grad_joined.shape[0], w_reduce.shape[1]
    scratch += [
        pltpu.VMEM((t, m), dtype),
        pltpu.VMEM((m, t), dtype),
        pltpu.VMEM((2, t, widest), dtype),
        pltpu.VMEM(grad_joined.shape, dtype),
        pltpu.VMEM(w_spatial.shape, f32),
        pltpu.VMEM((patches, mid), dtype),
        pltpu.VMEM((patches, mid), f32),
        pltpu.VMEM((2, patches, mid), dtype),
    ]
    scratch += total_buffers(lines, rows, (16, 1024), f32)
    scratch += [
        pltpu.SemaphoreType.DMA((1,)),
        pltpu.SemaphoreType.DMA((2,)),
        pltpu.SemaphoreType.DMA((2,)),
        pltpu.SemaphoreType.DMA((2,)),
        pltpu.SemaphoreType.DMA((copies,)),
        pltpu.SemaphoreType.DMA((copies,)),
    ]
    far = [p[0] for p in products] + [p[1] for p in products] + list(stem_grads)
    vmem = pl.BlockSpec(memory_space=pltpu.VMEM)
    results = pl.pallas_call(
        functools.partial(finish_kernel, lines, rows, plan, side, float(patches * devices)),
        out_shape=[jax.ShapeDtypeStruct(s[-2:], f32) for s in shapes]
        + [jax.ShapeDtypeStruct(grad_joined.shape, f32), jax.ShapeDtypeStruct((16, 1024), f32)],
        in_specs=[pl.BlockSpec(memory_space=pl.ANY)] * len(far) + [vmem] * len(inputs),
        out_specs=[vmem] * (count + 2),
        scratch_shapes=scratch,
        compiler_params=pltpu.CompilerParams(collective_id=collective_id, has_side_effects=True, vmem_limit_bytes=127 * 2**19),
        cost_estimate=pl.CostEstimate(flops=20 * 10**9, bytes_accessed=8 * 10**7, transcendentals=10**6),
        name="finish",
    )(*far, *inputs)
    return results


def local(
    tokens,
    features,
    segments,
    positions,
    w_qkv,
    w_out,
    w_up,
    w_down,
    gain_pre,
    gain_attn,
    gain_mid,
    gain_ffn,
    rel_table,
    head_scale,
    w_reduce,
    w_spatial,
    w_expand,
    w_embed,
    bn_gain,
    bn_shift,
    d_out,
):
    both = ("wide", "narrow")
    devices = lax.axis_size(both)
    me = lax.axis_index("wide") * lax.axis_size("narrow") + lax.axis_index("narrow")
    rows, length = (segments.shape[0], segments.shape[1])
    images, side = (features.shape[0], features.shape[1])
    patch_count = images * side * side
    whole = patch_count * devices
    first_at = positions[0, 0]
    stem_in = features.reshape(patch_count, features.shape[3])
    vectors = [item.reshape(1, -1) for item in (gain_pre, gain_attn, gain_mid, gain_ffn, bn_gain, bn_shift)]
    gathered, kept = front(
        positions[0, :1],
        vectors + [rel_table],
        stem_in,
        tokens,
        [w_reduce, w_spatial, w_expand, w_embed, w_qkv, w_out, w_up, w_down],
        side,
        1,
    )
    full_reduce, full_spatial, full_expand, full_embed, full_qkv = (
        item.reshape(-1, item.shape[-1]) for item in gathered[:5]
    )
    planes = lax.axis_size("narrow") // 2

    def other_side(item):
        return lax.ppermute(item, "wide", [(w, w ^ 1) for w in range(devices // (2 * planes))])

    def next_row(item, k):
        return lax.ppermute(item, "narrow", [(n, (n + 2 * k) % (2 * planes)) for n in range(2 * planes)])

    def by_row(item):
        return [item] + [next_row(item, k) for k in range(1, planes)]

    outs_in, downs_in = by_row(gathered[5]), by_row(gathered[7])
    ups_in = [gathered[6], other_side(gathered[6])]
    gains, pre_first, columns, pre_second, second, bn_unit, bn_inv, joined, start, normed0_low, packed = kept
    full_bn_gain, full_bn_shift = gains[0], gains[1]
    full_pre, full_attn, full_mid = gains[2, :D], gains[3, :D], gains[4, :D]
    full_ffn = gains[5:8].reshape(-1)
    full_table = gains[8:11].reshape(HEADS, 2 * RSPAN)
    pre_joined = bn_unit * full_bn_gain + full_bn_shift + stem_in.astype(jnp.float32)
    unused, unit0, inv0 = layer_norm(start, full_pre)
    win = windows(segments)
    attended, logsums, bias = attend(packed, segments, bias_strips(full_table), win)
    scale_row = jnp.repeat(head_scale, HDIM)[None, :]
    hidden = w_up.shape[1]
    mixed, mixed_low, normed2_low, narrowed_low, grad_pre_up, grad_middle, grad_branch, grad_attended, sums = middle_part(
        attended, start, d_out, gains, scale_row, outs_in, ups_in, downs_in, hidden, 5
    )
    grad_packed, grad_strips = attend_back(packed, grad_attended, attended, segments, bias, logsums, win)
    grad_table = table_from_strips(grad_strips)
    grad_normed0 = product_nt(grad_packed, full_qkv)
    grad_start_in, grad_gain_pre = layer_norm_back(
        grad_normed0, unit0, inv0, full_pre.astype(jnp.float32)
    )
    grad_tokens = grad_middle + grad_start_in
    grad_embedded = lax.dynamic_slice_in_dim(grad_tokens, first_at, patch_count, 0).astype(jnp.bfloat16)
    grad_w_embed = product_tn(joined, grad_embedded)
    grad_joined = product_nt(grad_embedded, full_embed)
    grad_pre_joined = smooth_back(pre_joined, grad_joined)
    lines = lax.axis_size("wide") // 2
    grad_w_embed = grad_w_embed.astype(jnp.bfloat16).reshape(lines, 2, planes, 2, -1, D)
    results = finish(
        [
            (d_out, narrowed_low, "blocks"),
            (normed2_low, grad_pre_up, "blocks"),
            (normed0_low, grad_packed, "blocks"),
            (mixed_low, grad_branch, "rows"),
        ],
        (grad_w_embed, grad_pre_joined, columns, stem_in),
        [
            bn_unit,
            gains,
            bn_inv,
            pre_second,
            pre_first,
            second,
            full_expand,
            full_spatial,
            full_reduce,
            sums,
            grad_gain_pre.reshape(1, -1),
            grad_table.reshape(3, -1),
        ],
        side,
        2,
    )
    sum_down, sum_up, sum_qkv, sum_out, sum_embed, sum_expand, sum_spatial, sum_reduce, grad_features, small = results
    grad_features = grad_features.reshape(features.shape)
    sum_down = sum_down.T
    width = 3 * D // (2 * planes)
    sum_qkv = jnp.where(
        lax.axis_index("narrow") % 2 == 0, sum_qkv[:, :width], sum_qkv[:, sum_qkv.shape[1] - width :]
    )

    def own(item):
        part = item.shape[0] // devices
        return lax.dynamic_slice_in_dim(item, me * part, part)

    sum_bn_shift, sum_bn_gain = own(small[0]), own(small[1])
    sum_pre, sum_attn, sum_mid = own(small[2, :D]), own(small[3, :D]), own(small[4, :D])
    sum_ffn = own(small[5:8].reshape(-1))
    breadth = 2 * RSPAN // devices
    sum_table = lax.dynamic_slice_in_dim(small[8:11].reshape(HEADS, -1), me * breadth, breadth, 1)
    grad_head = jnp.sum(small[11, :D].reshape(HEADS, HDIM), axis=1)
    return (
        mixed,
        grad_tokens,
        grad_features,
        sum_qkv,
        sum_out,
        sum_up,
        sum_down,
        sum_pre,
        sum_attn,
        sum_mid,
        sum_ffn,
        sum_table,
        grad_head,
        sum_reduce,
        sum_spatial,
        sum_expand,
        sum_embed,
        sum_bn_gain,
        sum_bn_shift,
    )


def solution(mesh):
    placed = (
        P(("wide", "narrow"), None),
        P(("wide", "narrow"), None, None, None),
        P(("wide", "narrow"), None),
        P(("wide", "narrow"), None),
        P(("wide", "narrow"), None),
        P(("wide", "narrow"), None),
        P(("wide", "narrow"), None),
        P(("wide", "narrow"), None),
        P(("wide", "narrow")),
        P(("wide", "narrow")),
        P(("wide", "narrow")),
        P(("wide", "narrow")),
        P(None, ("wide", "narrow")),
        P(),
        P(("wide", "narrow"), None),
        P(("wide", "narrow"), None),
        P(("wide", "narrow"), None),
        P(("wide", "narrow"), None),
        P(("wide", "narrow")),
        P(("wide", "narrow")),
        P(("wide", "narrow"), None),
    )
    return jax.shard_map(
        local,
        mesh=mesh,
        in_specs=placed,
        out_specs=(
            P(("wide", "narrow"), None),
            P(("wide", "narrow"), None),
            P(("wide", "narrow"), None, None, None),
            P("wide", "narrow"),
            P(("wide", "narrow"), None),
            P("wide", "narrow"),
            P("narrow", "wide"),
            P(("wide", "narrow")),
            P(("wide", "narrow")),
            P(("wide", "narrow")),
            P(("wide", "narrow")),
            P(None, ("wide", "narrow")),
            P(),
            P(("wide", "narrow"), None),
            P(("wide", "narrow"), None),
            P(("wide", "narrow"), None),
            P(("wide", "narrow"), None),
            P(("wide", "narrow")),
            P(("wide", "narrow")),
        ),
        check_vma=False,
    )
```

```python
import functools

import jax
import jax.numpy as jnp
from jax import lax
from jax.experimental import pallas as pl
from jax.experimental.pallas import tpu as pltpu
from jax.sharding import PartitionSpec as P

D = 768
HEADS = 12
HDIM = 64
RSPAN = 128


epsilon = 1e-05


def product(lhs_matrix, rhs_matrix):
    return jnp.dot(lhs_matrix, rhs_matrix, preferred_element_type=jnp.float32)


def product_tn(lhs_matrix, rhs_matrix):
    return lax.dot_general(
        lhs_matrix, rhs_matrix, (((0,), (0,)), ((), ())), preferred_element_type=jnp.float32
    )


def product_nt(lhs_matrix, rhs_matrix):
    return lax.dot_general(
        lhs_matrix, rhs_matrix, (((1,), (1,)), ((), ())), preferred_element_type=jnp.float32
    )


def layer_norm(values, gain):
    average = jnp.mean(values, axis=-1, keepdims=True)
    centred = values - average
    inv_std = lax.rsqrt(jnp.mean(centred * centred, axis=-1, keepdims=True) + epsilon)
    unit_rows = centred * inv_std
    return (unit_rows * gain, unit_rows, inv_std)


def layer_norm_back(cotangent, unit_rows, inv_std, gain):
    weighted = cotangent * gain
    inner = (
        weighted
        - jnp.mean(weighted, axis=-1, keepdims=True)
        - unit_rows * jnp.mean(weighted * unit_rows, axis=-1, keepdims=True)
    )
    return (inv_std * inner, jnp.sum(cotangent * unit_rows, axis=0))


def smooth(values):
    return jax.nn.gelu(values, approximate=True)


def smooth_back(values, cotangent):
    unused, pullback = jax.vjp(smooth, values)
    return pullback(cotangent)[0]


def unfold(grid):
    side = grid.shape[1]
    padded = jnp.pad(grid, ((0, 0), (1, 1), (1, 1), (0, 0)))
    pieces = [
        padded[:, row_off : row_off + side, col_off : col_off + side, :]
        for row_off in range(3)
        for col_off in range(3)
    ]
    return jnp.concatenate(pieces, axis=-1)


def fold(columns):
    channels = columns.shape[-1] // 9
    side = columns.shape[1]
    total = jnp.zeros((columns.shape[0], side + 2, side + 2, channels), jnp.float32)
    for row_off in range(3):
        for col_off in range(3):
            which = row_off * 3 + col_off
            piece = columns[..., which * channels : (which + 1) * channels]
            total = total + jnp.pad(
                piece, ((0, 0), (row_off, 2 - row_off), (col_off, 2 - col_off), (0, 0))
            )
    return total[:, 1:-1, 1:-1, :]


PAIRS = HEADS // 2
BLK = 128
NEG = -1e30


def dot_nn(a, b):
    return lax.dot_general(a, b, (((1,), (0,)), ((), ())), preferred_element_type=jnp.float32)


def dot_nt(a, b):
    return lax.dot_general(a, b, (((1,), (1,)), ((), ())), preferred_element_type=jnp.float32)


def split_heads(pair, scale):
    lane = lax.broadcasted_iota(jnp.int32, pair.shape, 1)
    vals = pair * jnp.asarray(scale, pair.dtype)
    zero = jnp.zeros_like(vals)
    return jnp.concatenate([jnp.where(lane < HDIM, vals, zero), jnp.where(lane < HDIM, zero, vals)], axis=0)


def join_heads(both):
    row = lax.broadcasted_iota(jnp.int32, (2 * HDIM, BLK), 0)
    return jnp.where(row < HDIM, both[:, :BLK], both[:, BLK:])


def bias_strips(table):
    rev = jnp.flip(table.astype(jnp.float32), axis=1)
    first, last = rev[:, 255:256], rev[:, 0:1]
    below = jnp.concatenate([jnp.broadcast_to(first, (HEADS, 129)), rev[:, 128:255]], axis=1)
    middle = jnp.concatenate([rev[:, 127:256], rev[:, 0:127]], axis=1)
    above = jnp.concatenate([last, rev[:, 0:127], jnp.broadcast_to(last, (HEADS, 128))], axis=1)
    low = jnp.broadcast_to(first, (HEADS, 256))
    high = jnp.broadcast_to(last, (HEADS, 256))
    return jnp.stack([low, below, middle, above, high], axis=1)


def table_from_strips(sums):
    low, below, middle, above, high = (sums[:, i] for i in range(5))
    total = jnp.concatenate([middle[:, 129:256], middle[:, 0:129]], axis=1)
    zero = jnp.zeros((HEADS, 127), jnp.float32)
    first = jnp.sum(low, axis=1, keepdims=True) + jnp.sum(below[:, :129], axis=1, keepdims=True)
    last = jnp.sum(high, axis=1, keepdims=True) + above[:, 0:1] + jnp.sum(above[:, 128:], axis=1, keepdims=True)
    total = total + jnp.concatenate([jnp.zeros((HEADS, 128), jnp.float32), below[:, 129:], first], axis=1)
    head = jnp.concatenate([above[:, 1:128], jnp.zeros((HEADS, 129), jnp.float32)], axis=1)
    total = total + head + jnp.concatenate([last, jnp.zeros((HEADS, 255), jnp.float32)], axis=1)
    return jnp.flip(total, axis=1)


def windows(segments):
    seg = segments.reshape(-1)
    starts = seg[::BLK]
    ends = seg[BLK - 1 :: BLK]
    low = jnp.sum((seg[None, :] < starts[:, None]).astype(jnp.int32), axis=1) // BLK
    high = (jnp.sum((seg[None, :] <= ends[:, None]).astype(jnp.int32), axis=1) + BLK - 1) // BLK
    return jnp.stack([low, high])


def over_chunks(low, high, chunk):
    def body(j, carry):
        chunk(low + 2 * j, 2)
        return carry

    lax.fori_loop(0, (high - low) // 2, body, 0)

    @pl.when((high - low) % 2 == 1)
    def _():
        chunk(high - 1, 1)


def attend_kernel(win, packed, segk, segq, strips, out, logsum, bias, vt, qm, acc, stat):
    i = pl.program_id(0)

    @pl.when(i == 0)
    def _():
        for hp in range(PAIRS):
            vt[pl.ds(hp * 128, 128), :] = packed[:, pl.ds(2 * D + hp * 128, 128)].T
            for d in range(5):
                for half in range(2):
                    row = strips[2 * hp + half, pl.ds(d, 1), :]
                    tile = jnp.broadcast_to(row, (BLK, 256))
                    if 0 < d < 4:
                        tile = pltpu.roll(tile, 0, 1, stride=1, stride_axis=0)
                    bias[hp, d, :, pl.ds(half * BLK, BLK)] = tile[:, :BLK]

    rows = pl.ds(pl.multiple_of(i * BLK, BLK), BLK)
    for hp in range(PAIRS):
        qm[hp] = split_heads(packed[rows, pl.ds(hp * 128, 128)], HDIM ** -0.5)
        acc[hp] = jnp.zeros((128, 256), jnp.float32)
        stat[hp, 0] = jnp.full((1, 256), NEG, jnp.float32)
        stat[hp, 1] = jnp.zeros((1, 256), jnp.float32)
    sq = segq[:, rows]
    sq2 = jnp.concatenate([sq, sq], axis=1)

    def body(kb, carry):
        keys = pl.ds(pl.multiple_of(kb * BLK, BLK), BLK)
        allowed = segk[keys, :] == sq2
        d = jnp.clip(kb - i, -2, 2) + 2
        for hp in range(PAIRS):
            s = dot_nt(packed[keys, pl.ds(D + hp * 128, 128)], qm[hp])
            s = jnp.where(allowed, s + bias[hp, d], NEG)
            old = stat[hp, 0]
            new = jnp.maximum(old, jnp.max(s, axis=0, keepdims=True))
            p = jnp.exp(s - new)
            alpha = jnp.exp(old - new)
            stat[hp, 0] = new
            stat[hp, 1] = stat[hp, 1] * alpha + jnp.sum(p, axis=0, keepdims=True)
            acc[hp] = acc[hp] * alpha + dot_nn(vt[pl.ds(hp * 128, 128), keys], p.astype(jnp.bfloat16))
        return carry

    lax.fori_loop(win[0, i], win[1, i], body, 0)
    for hp in range(PAIRS):
        total = stat[hp, 1]
        out[:, pl.ds(hp * 128, 128)] = join_heads(acc[hp] / total).T
        logsum[0, pl.ds(hp, 1), :] = stat[hp, 0] + jnp.log(total)


def attend(packed, segments, strips, win):
    length = packed.shape[0]
    blocks = length // BLK
    seg = segments.reshape(1, length)
    whole = lambda shape: pl.BlockSpec(shape, lambda i, w: (0,) * len(shape))
    return pl.pallas_call(
        attend_kernel,
        out_shape=(
            jax.ShapeDtypeStruct((length, D), jnp.float32),
            jax.ShapeDtypeStruct((blocks, PAIRS, 256), jnp.float32),
            jax.ShapeDtypeStruct((PAIRS, 5, BLK, 256), jnp.float32),
        ),
        grid_spec=pltpu.PrefetchScalarGridSpec(
            num_scalar_prefetch=1,
            grid=(blocks,),
            in_specs=[whole((length, 3 * D)), whole((length, 1)), whole((1, length)), whole((HEADS, 5, 256))],
            out_specs=(
                pl.BlockSpec((BLK, D), lambda i, w: (i, 0)),
                pl.BlockSpec((1, PAIRS, 256), lambda i, w: (i, 0, 0)),
                whole((PAIRS, 5, BLK, 256)),
            ),
            scratch_shapes=[
                pltpu.VMEM((D, length), jnp.bfloat16),
                pltpu.VMEM((PAIRS, 256, 128), jnp.bfloat16),
                pltpu.VMEM((PAIRS, 128, 256), jnp.float32),
                pltpu.VMEM((PAIRS, 2, 1, 256), jnp.float32),
            ],
        ),
        compiler_params=pltpu.CompilerParams(vmem_limit_bytes=48 * 2**20),
        cost_estimate=pl.CostEstimate(flops=2 * 10**10, bytes_accessed=10**7, transcendentals=6 * 10**6),
        name="attend",
    )(win, packed, seg.reshape(length, 1), seg, strips)


def reverse_rows(tile):
    count = tile.shape[0]
    row = lax.broadcasted_iota(jnp.int32, (count, count), 0)
    col = lax.broadcasted_iota(jnp.int32, (count, count), 1)
    turn = jnp.where(row + col == count - 1, 1.0, 0.0).astype(jnp.bfloat16)
    high = tile.astype(jnp.bfloat16)
    low = (tile - high.astype(jnp.float32)).astype(jnp.bfloat16)
    return dot_nn(turn, high) + dot_nn(turn, low)


def attend_back_kernel(win, packed, grads, attended, segk, segq, bias, logsum, out, tab, kt, qm, om, dqt, dk, dv, gt):
    i = pl.program_id(0)
    last = pl.num_programs(0) - 1

    @pl.when(i == 0)
    def _():
        for hp in range(PAIRS):
            kt[pl.ds(hp * 128, 128), :] = packed[:, pl.ds(D + hp * 128, 128)].T
        dk[...] = jnp.zeros_like(dk)
        dv[...] = jnp.zeros_like(dv)
        gt[...] = jnp.zeros_like(gt)

    rows = pl.ds(pl.multiple_of(i * BLK, BLK), BLK)
    dots = []
    for hp in range(PAIRS):
        cols = pl.ds(hp * 128, 128)
        qm[hp] = split_heads(packed[rows, cols], HDIM ** -0.5)
        om[hp] = split_heads(grads[:, cols], 1.0)
        cross = (grads[:, cols].astype(jnp.float32) * attended[:, cols]).T
        dots.append(jnp.concatenate([
            jnp.sum(cross[:HDIM], axis=0, keepdims=True),
            jnp.sum(cross[HDIM:], axis=0, keepdims=True)], axis=1))
        dqt[hp] = jnp.zeros((128, 256), jnp.float32)
    sq = segq[:, rows]
    sq2 = jnp.concatenate([sq, sq], axis=1)

    def chunk(kb, size):
        keys = pl.ds(pl.multiple_of(kb * BLK, BLK), size * BLK)
        allowed = segk[keys, :] == sq2
        near = [jnp.clip(kb + n - i, -2, 2) + 2 for n in range(size)]
        for hp in range(PAIRS):
            cols = pl.ds(hp * 128, 128)
            s = dot_nt(packed[keys, pl.ds(D + hp * 128, 128)], qm[hp])
            s = s + jnp.concatenate([bias[hp, d] for d in near], axis=0)
            p = jnp.exp(jnp.where(allowed, s, NEG) - logsum[0, pl.ds(hp, 1), :])
            dp = dot_nt(packed[keys, pl.ds(2 * D + hp * 128, 128)], om[hp])
            ds = p * (dp - dots[hp])
            for n, d in enumerate(near):
                gt[hp, d] += ds[n * BLK : (n + 1) * BLK]
            low = ds.astype(jnp.bfloat16)
            dv[keys, cols] += dot_nn(p.astype(jnp.bfloat16), om[hp])
            dk[keys, cols] += dot_nn(low, qm[hp])
            dqt[hp] += dot_nn(kt[cols, keys], low)

    over_chunks(win[0, i], win[1, i], chunk)
    for hp in range(PAIRS):
        out[rows, pl.ds(hp * 128, 128)] = (join_heads(dqt[hp]).T * (HDIM ** -0.5)).astype(jnp.bfloat16)

    @pl.when(i == last)
    def _():
        out[:, pl.ds(D, D)] = dk[...].astype(jnp.bfloat16)
        out[:, pl.ds(2 * D, D)] = dv[...].astype(jnp.bfloat16)
        for hp in range(PAIRS):
            for d in range(5):
                pair = gt[hp, d] if d in (0, 4) else reverse_rows(gt[hp, d])
                for half in range(2):
                    tile = pair[:, half * BLK : (half + 1) * BLK]
                    if d in (0, 4):
                        total = jnp.sum(tile, axis=0, keepdims=True)
                        total = jnp.concatenate([total, jnp.zeros_like(total)], axis=1)
                    else:
                        tile = jnp.concatenate([tile, jnp.zeros_like(tile)], axis=1)
                        tile = pltpu.roll(tile, 2 * BLK - (BLK - 1), 1, stride=1, stride_axis=0)
                        total = jnp.sum(tile, axis=0, keepdims=True)
                    tab[2 * hp + half, pl.ds(d, 1), :] = total


def attend_back(packed, grads, attended, segments, bias, logsum, win):
    length = packed.shape[0]
    blocks = length // BLK
    seg = segments.reshape(1, length)
    whole = lambda shape: pl.BlockSpec(shape, lambda i, w: (0,) * len(shape))
    return pl.pallas_call(
        attend_back_kernel,
        out_shape=(
            jax.ShapeDtypeStruct((length, 3 * D), jnp.bfloat16),
            jax.ShapeDtypeStruct((HEADS, 5, 256), jnp.float32),
        ),
        grid_spec=pltpu.PrefetchScalarGridSpec(
            num_scalar_prefetch=1,
            grid=(blocks,),
            in_specs=[
                whole((length, 3 * D)),
                pl.BlockSpec((BLK, D), lambda i, w: (i, 0)),
                pl.BlockSpec((BLK, D), lambda i, w: (i, 0)),
                whole((length, 1)),
                whole((1, length)),
                whole((PAIRS, 5, BLK, 256)),
                pl.BlockSpec((1, PAIRS, 256), lambda i, w: (i, 0, 0)),
            ],
            out_specs=(whole((length, 3 * D)), whole((HEADS, 5, 256))),
            scratch_shapes=[
                pltpu.VMEM((D, length), jnp.bfloat16),
                pltpu.VMEM((PAIRS, 256, 128), jnp.bfloat16),
                pltpu.VMEM((PAIRS, 256, 128), jnp.bfloat16),
                pltpu.VMEM((PAIRS, 128, 256), jnp.float32),
                pltpu.VMEM((length, D), jnp.float32),
                pltpu.VMEM((length, D), jnp.float32),
                pltpu.VMEM((PAIRS, 5, BLK, 256), jnp.float32),
            ],
        ),
        compiler_params=pltpu.CompilerParams(vmem_limit_bytes=56 * 2**20),
        cost_estimate=pl.CostEstimate(flops=5 * 10**10, bytes_accessed=2 * 10**7, transcendentals=6 * 10**6),
        name="attend_back",
    )(win, packed, grads, attended, seg.reshape(length, 1), seg, bias, logsum)


MESH = pl.DeviceIdType.MESH


class Place:
    def __init__(self, lines, rows):
        self.lines, self.rows = lines, rows
        wide, narrow = lax.axis_index("wide"), lax.axis_index("narrow")
        self.line, self.side = wide // 2, wide % 2
        self.row, self.core = narrow // 2, narrow % 2

    def device(self, line=None, side=None, row=None, core=None):
        line = self.line if line is None else line
        side = self.side if side is None else side
        row = self.row if row is None else row
        core = self.core if core is None else core
        return (line * 2 + side, row * 2 + core)

    def line_peer(self, k):
        return lax.rem(self.line + k, self.lines)

    def line_source(self, k):
        return lax.rem(self.line + self.lines - k, self.lines)

    def row_peer(self, k):
        return lax.rem(self.row + k, self.rows)

    def row_source(self, k):
        return lax.rem(self.row + self.rows - k, self.rows)

    def plane_peers(self):
        steps = [(k // self.rows, k % self.rows) for k in range(1, 2 * self.rows)]
        return [self.device(side=lax.rem(self.side + a, 2), row=self.row_peer(b)) for a, b in steps]

    def greet(self):
        barrier = pltpu.get_barrier_semaphore()
        targets = [self.device(line=self.line_peer(k)) for k in range(1, self.lines)]
        targets += self.plane_peers() + [self.device(core=1 - self.core)]
        for target in targets:
            pl.semaphore_signal(barrier, inc=1, device_id=target, device_id_type=MESH)
        pl.semaphore_wait(barrier, len(targets))


class Sends:
    def __init__(self, send_sems, recv_sems):
        self.send_sems, self.recv_sems, self.used = send_sems, recv_sems, 0
        self.started = []

    def start(self, src, dst, device):
        copy = pltpu.make_async_remote_copy(
            src_ref=src, dst_ref=dst, send_sem=self.send_sems.at[self.used], recv_sem=self.recv_sems.at[self.used],
            device_id=device, device_id_type=MESH)
        copy.start()
        self.used += 1
        self.started.append(copy)
        return copy

    def finish(self):
        for copy in self.started:
            copy.wait_send()


def gather_copies(lines, rows):
    return (lines - 1) + 1 + (rows - 1) + 1 + 1 + (rows - 1) + 1


class Gather:
    def __init__(self, place, sends, shard, out, local_sem, region, side_first):
        self.p, self.s, self.out, self.region = place, sends, out, region
        self.shard, self.local_sem, self.side_first = shard.at[region], local_sem, side_first
        self.cores = []

    def at(self, line, side, row):
        return self.out.at[(line, side, row, self.p.core) + self.region]

    def begin(self):
        p = self.p
        mine = self.at(p.line, p.side, p.row)
        self.local = pltpu.make_async_copy(self.shard, mine, self.local_sem)
        self.local.start()
        self.stage = [self.s.start(self.shard, mine, p.device(line=p.line_peer(k))) for k in range(1, p.lines)]

    def across(self, src):
        self.cores.append(self.s.start(src, src, self.p.device(core=1 - self.p.core)))

    def to_side(self, src):
        self.stage.append(self.s.start(src, src, self.p.device(side=1 - self.p.side)))

    def to_rows(self, src):
        p = self.p
        self.stage += [self.s.start(src, src, p.device(row=p.row_peer(k))) for k in range(1, p.rows)]

    def arrived(self):
        for copy in self.stage:
            copy.wait_recv()
        self.stage = []

    def second(self):
        p, every = self.p, slice(None)
        self.local.wait()
        self.arrived()
        mine = self.at(every, p.side, p.row)
        (self.to_side if self.side_first else self.to_rows)(mine)
        self.across(mine)

    def third(self):
        p, every = self.p, slice(None)
        self.arrived()
        if self.side_first:
            self.to_rows(self.at(every, every, p.row))
            self.across(self.at(every, 1 - p.side, p.row))
        else:
            self.to_side(self.at(every, p.side, every))
            for k in range(1, p.rows):
                self.across(self.at(every, p.side, p.row_source(k)))

    def fourth(self):
        p, every = self.p, slice(None)
        self.arrived()
        if self.side_first:
            for k in range(1, p.rows):
                self.across(self.at(every, every, p.row_source(k)))
        else:
            self.across(self.at(every, 1 - p.side, every))

    def last(self):
        for copy in self.cores:
            copy.wait_recv()


class HalfGather(Gather):
    def at(self, line, side, row):
        return self.out.at[line, side if self.side_first else row]

    def across(self, src):
        pass

    def third(self):
        self.arrived()

    def fourth(self):
        pass

    def last(self):
        pass


class Total:
    def __init__(self, place, sends, x, core_in, plane, line_in):
        self.p, self.s, self.x, self.core_in, self.plane, self.line_in = place, sends, x, core_in, plane, line_in

    def begin(self):
        p = self.p
        self.stage = [self.s.start(self.x, self.core_in, p.device(core=1 - p.core))]

    def second(self):
        p = self.p
        for copy in self.stage:
            copy.wait_recv()
        here = p.side * p.rows + p.row
        self.plane[here] = self.x[...] + self.core_in[...]
        self.stage = [self.s.start(self.plane.at[here], self.plane.at[here], t) for t in p.plane_peers()]

    def third(self):
        p = self.p
        for copy in self.stage:
            copy.wait_recv()
        total = self.plane[0]
        for k in range(1, 2 * p.rows):
            total = total + self.plane[k]
        self.line_in[p.line] = total
        mine = self.line_in.at[p.line]
        self.stage = [self.s.start(mine, mine, p.device(line=p.line_peer(k))) for k in range(1, p.lines)]

    def last(self):
        for copy in self.stage:
            copy.wait_recv()
        total = self.line_in[0]
        for k in range(1, self.p.lines):
            total = total + self.line_in[k]
        return total


def total_buffers(lines, rows, shape, dtype):
    return [
        pltpu.VMEM(shape, dtype),
        pltpu.VMEM(shape, dtype),
        pltpu.VMEM((2 * rows,) + shape, dtype),
        pltpu.VMEM((lines,) + shape, dtype),
    ]


def total_copies(lines, rows):
    return 2 * rows + lines - 1


def gelu(v):
    return 0.5 * v * (1.0 + jnp.tanh(0.7978845608028654 * (v + 0.044715 * (v * v * v))))


def spread(vector, me, total):
    n = vector.shape[1]
    lane = lax.broadcasted_iota(jnp.int32, (n, total), 1)
    row = lax.broadcasted_iota(jnp.int32, (n, total), 0)
    hot = jnp.where(lane == me * n + row, 1.0, 0.0).astype(jnp.bfloat16)
    return dot_nn(vector, hot)


def matrix(ref):
    block = ref[...].astype(jnp.float32)
    return block.reshape(-1, block.shape[-1]).astype(jnp.bfloat16)


def shifted(values, row_off, col_off, side):
    count = values.shape[0]
    step = row_off * side + col_off
    moved = pltpu.roll(values, (-step) % count, 0) if step % count else values
    patch = lax.broadcasted_iota(jnp.int32, (count, 1), 0)
    row, col = patch // side + row_off, lax.rem(patch, side) + col_off
    inside = (row >= 0) & (row < side) & (col >= 0) & (col < side)
    return jnp.where(inside, moved, 0.0)


FRONT_VECTORS = 7


def front_kernel(lines, rows, side, whole, pieces, number, *refs):
    refs = list(refs)

    def take(n):
        out = refs[:n]
        del refs[:n]
        return out

    (at,) = take(1)
    vectors = take(FRONT_VECTORS)
    (stem, tokens) = take(2)
    shards = take(number)
    held_outs, half_outs = take(FULL), take(number - FULL)
    (gains_out, pre_first_out, columns_out, pre_second_out, second_out, unit_out, inv) = take(7)
    (joined_out, start_out, normed_out, packed_out) = take(4)
    outs = take(FULL) + half_outs
    (gains, pre_first, columns, pre_second, second, unit, joined, start, normed, packed) = take(10)
    mats = take(5)
    (placing,) = take(1)
    held_bufs, sum_bufs = take(4), take(4)
    send_sems, recv_sems, local_sems, out_sems = take(4)
    place = Place(lines, rows)
    place.greet()
    sends = Sends(send_sems, recv_sems)

    me = (place.line * 2 + place.side) * (2 * rows) + place.row * 2 + place.core
    held = held_bufs[0]
    held[...] = jnp.zeros_like(held)
    devices = 4 * lines * rows

    parts = []
    for i, (which, region, side_first) in enumerate(pieces):
        region = tuple(pl.ds(*item) for item in region)
        kind = Gather if which < FULL else HalfGather
        parts.append(kind(place, sends, shards[which], outs[which], local_sems.at[i], region, side_first))
    batches = [[part for part, piece in zip(parts, pieces) if piece[0] in which] for which in ((0, 1), (2, 3), (4,), (5, 6, 7))]

    def run(batch, *names):
        for name in names:
            for part in batches[batch]:
                getattr(part, name)()

    copies_out = []

    def emit(value, out):
        copy = pltpu.make_async_copy(value, out, out_sems.at[len(copies_out)])
        copy.start()
        copies_out.append(copy)

    run(0, "begin")
    run(1, "begin")
    for v, (ref, row) in enumerate(zip(vectors[:6], (2, 3, 4, 5, 0, 1))):
        n = ref.shape[1]
        line = spread(ref[...], me, n * devices).astype(jnp.bfloat16)
        for k in range(0, n * devices, 1024):
            span = min(1024, n * devices - k)
            held[pl.ds(row + k // 1024, 1), pl.ds(0, span)] = line[:, k : k + span]
    table = spread(vectors[6][...], me, vectors[6].shape[1] * devices).astype(jnp.bfloat16)
    for h in range(HEADS):
        held[pl.ds(8 + h // 4, 1), pl.ds(h % 4 * 256, 256)] = table[h : h + 1, :]
    vector_total = Total(place, sends, *held_bufs)
    vector_total.begin()

    run(0, "second")
    vector_total.second()
    run(2, "begin")
    run(0, "third")
    run(1, "second")
    vector_total.third()
    run(0, "fourth")
    run(1, "third")
    run(2, "second")
    run(3, "begin")
    run(0, "last")
    count = side * side
    w_reduce, w_spatial, w_expand, w_embed, w_qkv = mats
    w_reduce[...] = matrix(outs[0])
    pre = dot_nn(stem[...], w_reduce[...])
    pre_first[...] = pre
    emit(pre_first, pre_first_out)
    first = gelu(pre).astype(jnp.bfloat16).astype(jnp.float32)
    channels = first.shape[1]
    for r in range(3):
        for c in range(3):
            k = r * 3 + c
            columns[:, pl.ds(k * channels, channels)] = shifted(first, r - 1, c - 1, side).astype(jnp.bfloat16)
    emit(columns, columns_out)
    w_spatial[...] = matrix(outs[1])
    pre = dot_nn(columns[...], w_spatial[...])
    pre_second[...] = pre
    emit(pre_second, pre_second_out)
    second[...] = gelu(pre).astype(jnp.bfloat16)
    emit(second, second_out)
    run(1, "fourth")
    run(2, "third")
    run(1, "last")
    w_expand[...] = matrix(outs[2])
    sums = sum_bufs[0]
    sums[...] = jnp.zeros_like(sums)

    def expand(cols):
        third = dot_nn(second[...], w_expand[:, cols])
        unit[:, cols] = third
        sums[pl.ds(0, 1), cols] = jnp.sum(third, axis=0, keepdims=True)
        sums[pl.ds(1, 1), cols] = jnp.sum(third * third, axis=0, keepdims=True)

    tile_loop(unit.shape[1], expand)
    norm_total = Total(place, sends, *sum_bufs)
    norm_total.begin()
    run(2, "fourth")
    norm_total.second()
    gains[...] = vector_total.last().astype(jnp.float32)
    emit(gains, gains_out)
    w_embed[...] = matrix(outs[3])
    norm_total.third()
    run(3, "second")
    for held_weight, out in zip(outs[:4], held_outs):
        emit(held_weight, out)
    totals = norm_total.last()
    mean = totals[0:1] / whole
    inv_std = lax.rsqrt(totals[1:2] / whole - mean * mean + epsilon)
    inv[...] = jnp.broadcast_to(inv_std, inv.shape)

    third_rows = count // 3

    def join(i, carry):
        at_rows = pl.ds(pl.multiple_of(i * third_rows, third_rows), third_rows)
        value = (unit[at_rows, :] - mean) * inv_std
        unit[at_rows, :] = value
        pre_joined = value * gains[0:1, :] + gains[1:2, :] + stem[at_rows, :].astype(jnp.float32)
        joined[at_rows, :] = gelu(pre_joined).astype(jnp.bfloat16)
        return carry

    lax.fori_loop(0, 3, join, 0)
    emit(unit, unit_out)
    emit(joined, joined_out)
    length, width = start.shape
    token = lax.broadcasted_iota(jnp.int32, (length, count), 0)
    patch = lax.broadcasted_iota(jnp.int32, (length, count), 1)
    placing[...] = jnp.where(token - patch == at[0], 1.0, 0.0).astype(jnp.bfloat16)

    def embed(cols):
        value = dot_nn(joined[...], w_embed[:, cols])
        high = value.astype(jnp.bfloat16)
        low = (value - high.astype(jnp.float32)).astype(jnp.bfloat16)
        moved = dot_nn(placing[...], high) + dot_nn(placing[...], low)
        start[:, cols] = tokens[:, cols].astype(jnp.float32) + moved

    tile_loop(width, embed)
    gain = gains[2:3, :width]

    def norm(i, carry):
        at_rows = pl.ds(pl.multiple_of(i * 128, 128), 128)
        value = start[at_rows, :]
        centred = value - jnp.mean(value, axis=-1, keepdims=True)
        scale = lax.rsqrt(jnp.mean(centred * centred, axis=-1, keepdims=True) + epsilon)
        normed[at_rows, :] = (centred * scale * gain).astype(jnp.bfloat16)
        return carry

    emit(start, start_out)
    lax.fori_loop(0, length // 128, norm, 0)
    emit(normed, normed_out)
    run(2, "last")
    emit(outs[4], held_outs[4])
    w_qkv[...] = matrix(outs[4])

    def project(cols):
        packed[:, cols] = dot_nn(normed[...], w_qkv[:, cols]).astype(jnp.bfloat16)

    tile_loop(packed.shape[1], project)
    emit(packed, packed_out)
    run(3, "third")
    sends.finish()
    for copy in copies_out:
        copy.wait()


FULL = 5


def front(first_at, vectors, stem, tokens, shards, side, collective_id):
    wide, narrow = lax.axis_size("wide"), lax.axis_size("narrow")
    lines, rows = wide // 2, narrow // 2
    devices = wide * narrow
    number = len(shards)
    pieces = []
    for i, item in enumerate(shards):
        r, c = item.shape
        if i == 4:
            pieces += [(i, ((0, r), (k * c // 2, c // 2)), k == 0) for k in range(2)]
        else:
            pieces.append((i, ((0, r), (0, c)), i in (0, 2, 5, 7)))
    copies = len(pieces) * gather_copies(lines, rows) + 2 * total_copies(lines, rows)
    count, length = side * side, tokens.shape[0]
    mid = shards[0].shape[1]
    wide_in = stem.shape[1]
    f32, bf16 = jnp.float32, jnp.bfloat16
    leads = [(lines, 2, rows, 2)] * FULL + [(lines, 2), (lines, rows), (lines, 2)]
    gathered = [jax.ShapeDtypeStruct(lead + s.shape, s.dtype) for lead, s in zip(leads, shards)]
    kept = [
        ((16, 1024), f32),
        ((count, mid), f32),
        ((count, 9 * mid), bf16),
        ((count, mid), f32),
        ((count, mid), bf16),
        ((count, wide_in), f32),
        ((8, wide_in), f32),
        ((count, wide_in), bf16),
        ((length, D), f32),
        ((length, D), bf16),
        ((length, 3 * D), bf16),
    ]
    vmem = pl.BlockSpec(memory_space=pltpu.VMEM)
    anywhere = pl.BlockSpec(memory_space=pl.ANY)
    scratch = [pltpu.VMEM(item.shape, item.dtype) for item in gathered[:FULL]]
    scratch += [pltpu.VMEM(shape, dtype) for k, (shape, dtype) in enumerate(kept) if k != 6]
    scratch += [pltpu.VMEM((s.shape[0] * devices, s.shape[1]), bf16) for s in shards[:5]]
    scratch += [pltpu.VMEM((length, count), bf16)]
    scratch += total_buffers(lines, rows, (16, 1024), bf16)
    scratch += total_buffers(lines, rows, (8, 1024), f32)
    scratch += [pltpu.SemaphoreType.DMA((copies,)), pltpu.SemaphoreType.DMA((copies,)), pltpu.SemaphoreType.DMA((len(pieces),)), pltpu.SemaphoreType.DMA((FULL + 10,))]
    results = pl.pallas_call(
        functools.partial(front_kernel, lines, rows, side, float(count * devices), pieces, number),
        out_shape=gathered + [jax.ShapeDtypeStruct(s, d) for s, d in kept],
        in_specs=[pl.BlockSpec(memory_space=pltpu.SMEM)] + [vmem] * (FRONT_VECTORS + 2) + [anywhere] * number,
        out_specs=[anywhere] * number + [vmem if k == 6 else anywhere for k in range(len(kept))],
        scratch_shapes=scratch,
        compiler_params=pltpu.CompilerParams(collective_id=collective_id, has_side_effects=True, vmem_limit_bytes=60 * 2**20),
        cost_estimate=pl.CostEstimate(flops=6 * 10**9, bytes_accessed=7 * 10**7, transcendentals=10**6),
        name="front",
    )(first_at, *vectors, stem, tokens, *shards)
    return results[:number], results[number:]


def gelu_slope(v):
    t = jnp.tanh(0.7978845608028654 * (v + 0.044715 * (v * v * v)))
    return 0.5 * (1.0 + t) + 0.5 * v * (1.0 - t * t) * (0.7978845608028654 * (1.0 + 0.134145 * (v * v)))


def row_mean(values):
    return jnp.mean(values, axis=-1, keepdims=True)


def unit_of(values):
    centred = values - row_mean(values)
    inv_std = lax.rsqrt(row_mean(centred * centred) + epsilon)
    return centred * inv_std, inv_std


def unit_back(weighted, unit_rows, inv_std):
    return inv_std * (weighted - row_mean(weighted) - unit_rows * row_mean(weighted * unit_rows))


def column_sum(values):
    return jnp.sum(values, axis=0, keepdims=True)


FTILE = 512


def middle_kernel(lines, rows, counts, *refs):
    refs = list(refs)

    def take(n):
        out = refs[:n]
        del refs[:n]
        return out

    attended, start, d_out, gains, scale = take(5)
    outs_in, ups_in, downs_in = take(counts[0]), take(counts[1]), take(counts[2])
    mixed, mixed_low, normed2, narrowed, grad_up, grad_middle, branch, grad_attended, sums = take(9)
    held = take(3)
    mats = take(3)
    pre, act, weighted = take(3)
    send_sems, recv_sems, local_sems = take(3)
    i = pl.program_id(0)
    w_out, w_up, w_down = mats
    width, hidden = w_up.shape

    @pl.when(i == 0)
    def _():
        place = Place(lines, rows)
        partner = place.device(core=1 - place.core)
        barrier = pltpu.get_barrier_semaphore()
        pl.semaphore_signal(barrier, inc=1, device_id=partner, device_id_type=MESH)
        pl.semaphore_wait(barrier, 1)
        sends = Sends(send_sems, recv_sems)
        waits = []
        for full, pieces in zip(held, (outs_in, ups_in, downs_in)):
            group = []
            for k, piece in enumerate(pieces):
                if full is held[1]:
                    side = place.side if k == 0 else 1 - place.side
                    spot = full.at[:, side, :, place.core]
                else:
                    spot = full.at[:, :, place.row_source(k), place.core]
                local = pltpu.make_async_copy(piece, spot, local_sems.at[sends.used])
                local.start()
                group.append((sends.start(piece, spot, partner), local))
            waits.append(group)
        for full, mat, group in zip(held, mats, waits):
            for copy, local in group:
                copy.wait_recv()
                local.wait()
            tall = mat.shape[0] // (2 * lines)

            def convert(k, carry, full=full, mat=mat, tall=tall):
                block = full[k // 2, lax.rem(k, 2)].astype(jnp.float32)
                mat[pl.ds(pl.multiple_of(k * tall, tall), tall), :] = block.reshape(tall, mat.shape[1]).astype(mat.dtype)
                return carry

            lax.fori_loop(0, 2 * lines, convert, 0)
        sends.finish()
        sums[...] = jnp.zeros_like(sums)

    gain_attn, gain_mid = gains[3:4, :width], gains[4:5, :width]
    scaled = attended[...] * scale[...]
    unit1, inv1 = unit_of(scaled)
    low = (unit1 * gain_attn).astype(jnp.bfloat16)
    mixed_low[...] = low
    middle = start[...] + dot_nn(low, w_out[...])
    unit2, inv2 = unit_of(middle)
    low2 = (unit2 * gain_mid).astype(jnp.bfloat16)
    normed2[...] = low2
    tiles = hidden // FTILE
    count = middle.shape[0]
    zero = jnp.zeros((count, 1), jnp.float32)

    def span(f):
        return pl.ds(pl.multiple_of(f * FTILE, FTILE), FTILE)

    def gain_of(f):
        per = 1024 // FTILE
        return gains[pl.ds(5 + f // per, 1), f % per * FTILE : (f % per + 1) * FTILE]

    total = zero
    for f in range(tiles):
        cols = pl.ds(f * FTILE, FTILE)
        value = dot_nn(low2, w_up[:, cols])
        pre[:, cols] = value
        value = gelu(value)
        act[:, cols] = value
        total = total + jnp.sum(value, axis=-1, keepdims=True)
    mean = total / hidden
    total = zero
    for f in range(tiles):
        cols = pl.ds(f * FTILE, FTILE)
        centred = act[:, cols] - mean
        total = total + jnp.sum(centred * centred, axis=-1, keepdims=True)
    inv3 = lax.rsqrt(total / hidden + epsilon)
    result = middle
    cross1, cross2 = zero, zero
    for f in range(tiles):
        cols = pl.ds(f * FTILE, FTILE)
        unit3 = (act[:, cols] - mean) * inv3
        act[:, cols] = unit3
        gain = gain_of(f)
        low3 = (unit3 * gain).astype(jnp.bfloat16)
        narrowed[:, cols] = low3
        result = result + dot_nn(low3, w_down[cols, :])
        grad = dot_nt(d_out[...], w_down[cols, :])
        sums[0:1, cols] += column_sum(grad * unit3)
        grad = grad * gain
        weighted[:, cols] = grad
        cross1 = cross1 + jnp.sum(grad, axis=-1, keepdims=True)
        cross2 = cross2 + jnp.sum(grad * unit3, axis=-1, keepdims=True)
    mixed[...] = result.astype(jnp.bfloat16)
    cross1, cross2 = cross1 / hidden, cross2 / hidden
    grad2 = jnp.zeros((count, width), jnp.float32)
    for f in range(tiles):
        cols = pl.ds(f * FTILE, FTILE)
        grad = inv3 * (weighted[:, cols] - cross1 - act[:, cols] * cross2)
        grad = (gelu_slope(pre[:, cols]) * grad).astype(jnp.bfloat16)
        grad_up[:, cols] = grad
        grad2 = grad2 + dot_nt(grad, w_up[:, cols])
    sums[1:2, :width] += column_sum(grad2 * unit2)
    grad_mid = d_out[...].astype(jnp.float32) + unit_back(grad2 * gain_mid, unit2, inv2)
    grad_middle[...] = grad_mid
    low = grad_mid.astype(jnp.bfloat16)
    branch[...] = low
    grad1 = dot_nt(low, w_out[...])
    sums[2:3, :width] += column_sum(grad1 * unit1)
    grad_scaled = unit_back(grad1 * gain_attn, unit1, inv1)
    sums[3:4, :width] += column_sum(grad_scaled * attended[...])
    grad_attended[...] = (grad_scaled * scale[...]).astype(jnp.bfloat16)


def middle_part(attended, start, d_out, gains, scale_row, outs_in, ups_in, downs_in, hidden, collective_id):
    wide, narrow = lax.axis_size("wide"), lax.axis_size("narrow")
    lines, rows = wide // 2, narrow // 2
    length, width = start.shape
    block = 256
    f32, bf16 = jnp.float32, jnp.bfloat16
    counts = (len(outs_in), len(ups_in), len(downs_in))
    copies = sum(counts)

    def by_token(columns):
        return pl.BlockSpec((block, columns), lambda i: (i, 0))

    def whole(shape):
        return pl.BlockSpec(shape, lambda i: (0,) * len(shape))

    anywhere = pl.BlockSpec(memory_space=pl.ANY)
    pieces = list(outs_in) + list(ups_in) + list(downs_in)
    results = [(width, bf16), (width, bf16), (width, bf16), (hidden, bf16), (hidden, bf16), (width, f32), (width, bf16), (width, bf16)]
    shapes = [(width, width), (width, hidden), (hidden, width)]
    devices = wide * narrow
    return pl.pallas_call(
        functools.partial(middle_kernel, lines, rows, counts),
        out_shape=[jax.ShapeDtypeStruct((length, c), d) for c, d in results] + [jax.ShapeDtypeStruct((8, hidden), f32)],
        grid=(length // block,),
        in_specs=[by_token(width), by_token(width), by_token(width), whole(gains.shape), whole(scale_row.shape)] + [anywhere] * copies,
        out_specs=[by_token(c) for c, _ in results] + [whole((8, hidden))],
        scratch_shapes=[pltpu.VMEM((lines, 2, rows, 2, m // devices, n), bf16) for m, n in shapes]
        + [pltpu.VMEM(shape, bf16) for shape in shapes]
        + [pltpu.VMEM((block, hidden), f32)] * 3
        + [pltpu.SemaphoreType.DMA((copies,))] * 3,
        compiler_params=pltpu.CompilerParams(collective_id=collective_id, has_side_effects=True, vmem_limit_bytes=60 * 2**20),
        cost_estimate=pl.CostEstimate(flops=22 * 10**9, bytes_accessed=6 * 10**7, transcendentals=7 * 10**6),
        name="middle_part",
    )(attended, start, d_out, gains, scale_row, *pieces)


def scatter_copies(lines, rows):
    return 1 + (rows - 1) + 1 + 1 + (rows - 1) + (lines - 1)


def add_loop(lead, fn):
    total = 1
    for size in lead:
        total *= size

    def body(i, carry):
        index = []
        for size in reversed(lead):
            index.append(lax.rem(i, size))
            i = i // size
        fn(tuple(reversed(index)))
        return carry

    lax.fori_loop(0, total, body, 0)


def plus(*terms):
    total = terms[0].astype(jnp.float32)
    for term in terms[1:]:
        total = total + term.astype(jnp.float32)
    return total


class Scatter:
    def __init__(self, place, sends, full, out, buffers):
        self.p, self.s, self.full, self.out = place, sends, full, out
        self.other, self.low1, self.high1, self.low2, self.high2, self.line0, self.lines_in = buffers
        cols = full.shape[-1]
        cut = cols // 256 * 128
        self.low, self.high = pl.ds(0, cut), pl.ds(cut, cols - cut)

    def begin(self):
        core = self.p.core
        self.stage = [self.s.start(self.full.at[:, :, :, 1 - core], self.other, self.p.device(core=1 - core))]

    def second(self):
        p, full, dtype = self.p, self.full, self.full.dtype
        for copy in self.stage:
            copy.wait_recv()

        def add(i):
            l, x, y = i
            full[l, x, y, p.core] = plus(full[l, x, y, p.core], self.other[l, x, y]).astype(dtype)

        add_loop(self.other.shape[:3], add)
        self.stage = [self.s.start(full.at[:, 1 - p.side, :, p.core, :, self.high], self.high1, p.device(side=1 - p.side))]
        for k in range(1, p.rows):
            to = p.row_peer(k)
            self.stage.append(self.s.start(full.at[:, :, to, p.core, :, self.low], self.low1.at[k - 1], p.device(row=to)))

    def third(self):
        p, full, dtype = self.p, self.full, self.full.dtype
        for copy in self.stage:
            copy.wait_recv()

        def add_low(i):
            l, x = i
            terms = [full[l, x, p.row, p.core, :, self.low]] + [self.low1[k, l, x] for k in range(p.rows - 1)]
            full[l, x, p.row, p.core, :, self.low] = plus(*terms).astype(dtype)

        def add_high(i):
            l, y = i
            full[l, p.side, y, p.core, :, self.high] = plus(full[l, p.side, y, p.core, :, self.high], self.high1[l, y]).astype(dtype)

        add_loop((p.lines, 2), add_low)
        add_loop((p.lines, p.rows), add_high)
        self.stage = [self.s.start(full.at[:, 1 - p.side, p.row, p.core, :, self.low], self.low2, p.device(side=1 - p.side))]
        for k in range(1, p.rows):
            to = p.row_peer(k)
            self.stage.append(self.s.start(full.at[:, p.side, to, p.core, :, self.high], self.high2.at[k - 1], p.device(row=to)))

    def fourth(self):
        p, full, dtype = self.p, self.full, self.full.dtype
        for copy in self.stage:
            copy.wait_recv()

        def add(i):
            (l,) = i
            self.line0[l, :, self.low] = plus(full[l, p.side, p.row, p.core, :, self.low], self.low2[l]).astype(dtype)
            terms = [full[l, p.side, p.row, p.core, :, self.high]] + [self.high2[k, l] for k in range(p.rows - 1)]
            self.line0[l, :, self.high] = plus(*terms).astype(dtype)

        add_loop((p.lines,), add)
        self.stage = []
        for k in range(1, p.lines):
            to = p.line_peer(k)
            self.stage.append(self.s.start(self.line0.at[to], self.lines_in.at[k - 1], p.device(line=to)))

    def last(self):
        p = self.p
        for copy in self.stage:
            copy.wait_recv()
        self.out[...] = plus(self.line0[p.line], *[self.lines_in[k] for k in range(p.lines - 1)])


def scatter_buffers(lines, rows, r, c, dtype):
    low = c // 256 * 128
    high = c - low
    return [
        pltpu.VMEM((lines, 2, rows, r, c), dtype),
        pltpu.VMEM((max(rows - 1, 1), lines, 2, r, low), dtype),
        pltpu.VMEM((lines, rows, r, high), dtype),
        pltpu.VMEM((lines, r, low), dtype),
        pltpu.VMEM((max(rows - 1, 1), lines, r, high), dtype),
        pltpu.VMEM((lines, r, c), dtype),
        pltpu.VMEM((max(lines - 1, 1), r, c), dtype),
    ]


NBUF = 7


def tile_loop(width, fn):
    full = width // 256

    def body(j, carry):
        fn(pl.ds(pl.multiple_of(j * 256, 256), 256))
        return carry

    lax.fori_loop(0, full, body, 0)
    if width % 256:
        fn(pl.ds(full * 256, width % 256))


def finish_kernel(lines, rows, products, side, whole, *refs):
    refs = list(refs)

    def take(n):
        out = refs[:n]
        del refs[:n]
        return out

    number, stems = len(products), 4
    lefts, rights = take(number), take(number)
    (embed_in, grad_joined, columns, stem) = take(4)
    (unit, gains, inv, pre_second, pre_first, second, w_expand, w_spatial, w_reduce, partial, pre_row, table) = take(12)
    count = number + stems
    outs = take(count)
    (features_out, totals_out) = take(2)
    fulls, buffers = take(count), take(count * NBUF)
    (xraw, xbuf, gbuf, third, tall, grad_second, grad_first, block) = take(8)
    sum_bufs = take(4)
    (xsem, gsem, in_sems, block_sems, send_sems, recv_sems) = take(6)
    place = Place(lines, rows)
    place.greet()
    sends = Sends(send_sems, recv_sems)
    parts = [Scatter(place, sends, fulls[i], outs[i], buffers[NBUF * i : NBUF * (i + 1)]) for i in range(count)]
    ready = [
        pltpu.make_async_copy(grad_joined, features_out, in_sems.at[0]),
        pltpu.make_async_copy(embed_in, fulls[number], in_sems.at[1]),
    ]
    for copy in ready:
        copy.start()

    core = place.core
    tasks = []
    for a, (kind, width) in enumerate(products):
        if kind == "rows":
            tasks += [(a, 0, None, None), (a, width, None, None)]
        else:
            for c in (1 - core, core):
                for y in range(rows):
                    pitch = rights[a].shape[1] // rows
                    first = y * pitch + c * (pitch - width)
                    tasks.append((a, first, y, c))

    def fetch_right(t):
        a, first, y, c = tasks[t]
        width = products[a][1]
        first = pl.multiple_of(jnp.int32(first), 128)
        return pltpu.make_async_copy(rights[a].at[:, pl.ds(first, width)], gbuf.at[t % 2, :, pl.ds(0, width)], gsem.at[t % 2])

    def fetch_left(a):
        return pltpu.make_async_copy(lefts[a], xraw, xsem.at[0])

    fetch_left(0).start()
    fetch_right(0).start()
    at_task = [0]

    def multiply():
        t = at_task[0]
        at_task[0] += 1
        a, first, y, c = tasks[t]
        kind, width = products[a]
        if t + 1 < len(tasks):
            fetch_right(t + 1).start()
        if t == 0 or tasks[t - 1][0] != a:
            fetch_left(a).wait()

            def turn(cols):
                xbuf[cols, :] = xraw[:, cols].T

            tile_loop(xraw.shape[1], turn)
            if a + 1 < number:
                fetch_left(a + 1).start()
        fetch_right(t).wait()
        full = fulls[a]

        def tile(cols):
            value = dot_nn(xbuf[...], gbuf[t % 2, :, cols])
            n = value.shape[1]
            if kind == "rows":
                spot = pl.ds(pl.multiple_of(cols.start + tasks[t][1], 128), n)
                full[:, :, :, :, :, spot] = value.reshape(lines, 2, rows, 2, -1, n).astype(full.dtype)
            else:
                full[:, :, y, c, :, cols] = value.reshape(lines, 2, -1, n).astype(full.dtype)

        tile_loop(width, tile)

    def from_tall(full):
        shards = full.shape[1:]
        span = shards[0] * shards[1] * shards[2] * shards[3]

        def move(i):
            (l,) = i
            value = tall[pl.ds(pl.multiple_of(l * span, span), span), :]
            full[l] = value.reshape(shards).astype(full.dtype)

        add_loop((lines,), move)

    patches, wide_in = unit.shape
    small = sum_bufs[0]
    width = pre_row.shape[1]
    small[...] = jnp.zeros_like(small)
    small[2:3, :width] = pre_row[...]
    small[3:4, :width] = partial[2:3, :width]
    small[4:5, :width] = partial[1:2, :width]
    for k in range(3):
        small[5 + k : 6 + k, :] = partial[0:1, k * 1024 : (k + 1) * 1024]
    small[8:11, :] = table[...]
    small[11:12, :width] = partial[3:4, :width]
    ready[0].wait()

    def channel_sums(cols):
        grad = features_out[:, cols]
        small[0:1, cols] = column_sum(grad)
        small[1:2, cols] = column_sum(grad * unit[:, cols])

    tile_loop(wide_in, channel_sums)
    total = Total(place, sends, *sum_bufs)
    channels = grad_second.shape[1]
    patch = lax.broadcasted_iota(jnp.int32, (patches, 1), 0)
    factors = sum_bufs[1]

    def fetch_block(source, k):
        return pltpu.make_async_copy(source.at[:, pl.ds(k * channels, channels)], block.at[k % 2], block_sems.at[k % 2])

    def windows_of():
        for _ in range(rows):
            multiply()

    def both_halves():
        multiply()
        multiply()

    def third_grads():
        sums = total.last()
        totals_out[...] = sums
        factors[...] = sums / whole

        def tile(cols):
            low = features_out[:, cols] - factors[0:1, cols] - unit[:, cols] * factors[1:2, cols]
            low = (inv[0:1, cols] * gains[0:1, cols] * low).astype(jnp.bfloat16)
            third[:, cols] = low
            value = dot_nn(second[...].T, low)
            fulls[number + 1][:, :, :, :, :, cols] = value.reshape(lines, 2, rows, 2, -1, value.shape[1]).astype(jnp.bfloat16)

        tile_loop(wide_in, tile)

    def second_grads():
        grad_second[...] = (gelu_slope(pre_second[...]) * dot_nt(third[...], w_expand[...])).astype(jnp.bfloat16)

    def taps(begin, end):
        if begin == 0:
            fetch_block(columns, 0).start()
        for k in range(begin, end):
            if k < 8:
                fetch_block(columns, k + 1).start()
            fetch_block(columns, k).wait()
            kernel_rows = pl.ds(k * channels, channels)
            tall[kernel_rows, :] = dot_nn(block[k % 2].T, grad_second[...])
            back = dot_nt(grad_second[...], w_spatial[kernel_rows, :])
            row_off, col_off = k // 3 - 1, k % 3 - 1
            row, col = patch // side + row_off, lax.rem(patch, side) + col_off
            inside = (row >= 0) & (row < side) & (col >= 0) & (col < side)
            step = (row_off * side + col_off) % patches
            back = jnp.where(inside, back, 0.0)
            back = pltpu.roll(back, step, 0) if step else back
            grad_first[...] = back if k == 0 else grad_first[...] + back
        if end == 9:
            from_tall(fulls[number + 2])

    def first_grads():
        low = (gelu_slope(pre_first[...]) * grad_first[...]).astype(jnp.bfloat16)
        grad_second[...] = low
        fetch_block(stem, 0).start()
        for k in range(wide_in // channels):
            if (k + 1) * channels < wide_in:
                fetch_block(stem, k + 1).start()
            fetch_block(stem, k).wait()
            tall[pl.ds(k * channels, channels), :] = dot_nn(block[k % 2].T, grad_second[...])
        from_tall(fulls[number + 3])

    def feature_grads():
        def tile(cols):
            features_out[:, cols] += dot_nt(grad_second[...], w_reduce[cols, :])

        tile_loop(wide_in, tile)

    down, up, qkv, out, embed, expand, spatial, reduce_ = parts
    total.begin()
    ready[1].wait()
    embed.begin()
    windows_of()
    down.begin()
    windows_of()
    total.second()
    embed.second()
    down.second()
    total.third()
    windows_of()
    up.begin()
    windows_of()
    third_grads()
    expand.begin()
    up.second()
    embed.third()
    second_grads()
    taps(0, 3)
    down.third()
    expand.second()
    taps(3, 6)
    taps(6, 9)
    spatial.begin()
    embed.fourth()
    windows_of()
    qkv.begin()
    up.third()
    spatial.second()
    windows_of()
    down.fourth()
    expand.third()
    first_grads()
    reduce_.begin()
    qkv.second()
    both_halves()
    out.begin()
    feature_grads()
    up.fourth()
    reduce_.second()
    spatial.third()
    out.second()
    expand.fourth()
    qkv.third()
    embed.last()
    down.last()
    reduce_.third()
    spatial.fourth()
    out.third()
    up.last()
    qkv.fourth()
    reduce_.fourth()
    out.fourth()
    expand.last()
    spatial.last()
    reduce_.last()
    qkv.last()
    out.last()
    sends.finish()


def finish(products, stem_grads, inputs, side, collective_id):
    wide, narrow = lax.axis_size("wide"), lax.axis_size("narrow")
    lines, rows = wide // 2, narrow // 2
    devices = wide * narrow
    shapes, plan = [], []
    for left, right, kind in products:
        m, n = left.shape[1], right.shape[1]
        if kind == "rows":
            width = n // 2
            shapes.append((lines, 2, rows, 2, m // devices, n))
        else:
            width = -(-(n // (2 * rows)) // 128) * 128
            shapes.append((lines, 2, rows, 2, m // (2 * lines), width))
        plan.append((kind, width))
    embed, grad_joined, columns, stem = stem_grads
    w_expand, w_spatial, w_reduce = inputs[6:9]
    shapes.append(embed.shape)
    for item in (w_expand, w_spatial, w_reduce):
        shapes.append((lines, 2, rows, 2, item.shape[0] // devices, item.shape[1]))
    count = len(shapes)
    copies = count * scatter_copies(lines, rows) + total_copies(lines, rows)
    f32, dtype = jnp.float32, jnp.bfloat16
    scratch = [pltpu.VMEM(s, dtype) for s in shapes]
    for s in shapes:
        scratch += scatter_buffers(lines, rows, s[-2], s[-1], dtype)
    t, m = products[0][0].shape
    widest = max(width for _, width in plan)
    patches, mid = grad_joined.shape[0], w_reduce.shape[1]
    scratch += [
        pltpu.VMEM((t, m), dtype),
        pltpu.VMEM((m, t), dtype),
        pltpu.VMEM((2, t, widest), dtype),
        pltpu.VMEM(grad_joined.shape, dtype),
        pltpu.VMEM(w_spatial.shape, f32),
        pltpu.VMEM((patches, mid), dtype),
        pltpu.VMEM((patches, mid), f32),
        pltpu.VMEM((2, patches, mid), dtype),
    ]
    scratch += total_buffers(lines, rows, (16, 1024), f32)
    scratch += [
        pltpu.SemaphoreType.DMA((1,)),
        pltpu.SemaphoreType.DMA((2,)),
        pltpu.SemaphoreType.DMA((2,)),
        pltpu.SemaphoreType.DMA((2,)),
        pltpu.SemaphoreType.DMA((copies,)),
        pltpu.SemaphoreType.DMA((copies,)),
    ]
    far = [p[0] for p in products] + [p[1] for p in products] + list(stem_grads)
    vmem = pl.BlockSpec(memory_space=pltpu.VMEM)
    results = pl.pallas_call(
        functools.partial(finish_kernel, lines, rows, plan, side, float(patches * devices)),
        out_shape=[jax.ShapeDtypeStruct(s[-2:], f32) for s in shapes]
        + [jax.ShapeDtypeStruct(grad_joined.shape, f32), jax.ShapeDtypeStruct((16, 1024), f32)],
        in_specs=[pl.BlockSpec(memory_space=pl.ANY)] * len(far) + [vmem] * len(inputs),
        out_specs=[vmem] * (count + 2),
        scratch_shapes=scratch,
        compiler_params=pltpu.CompilerParams(collective_id=collective_id, has_side_effects=True, vmem_limit_bytes=127 * 2**19),
        cost_estimate=pl.CostEstimate(flops=20 * 10**9, bytes_accessed=8 * 10**7, transcendentals=10**6),
        name="finish",
    )(*far, *inputs)
    return results


def local(
    tokens,
    features,
    segments,
    positions,
    w_qkv,
    w_out,
    w_up,
    w_down,
    gain_pre,
    gain_attn,
    gain_mid,
    gain_ffn,
    rel_table,
    head_scale,
    w_reduce,
    w_spatial,
    w_expand,
    w_embed,
    bn_gain,
    bn_shift,
    d_out,
):
    both = ("wide", "narrow")
    devices = lax.axis_size(both)
    me = lax.axis_index("wide") * lax.axis_size("narrow") + lax.axis_index("narrow")
    rows, length = (segments.shape[0], segments.shape[1])
    images, side = (features.shape[0], features.shape[1])
    patch_count = images * side * side
    whole = patch_count * devices
    first_at = positions[0, 0]
    stem_in = features.reshape(patch_count, features.shape[3])
    vectors = [item.reshape(1, -1) for item in (gain_pre, gain_attn, gain_mid, gain_ffn, bn_gain, bn_shift)]
    gathered, kept = front(
        positions[0, :1],
        vectors + [rel_table],
        stem_in,
        tokens,
        [w_reduce, w_spatial, w_expand, w_embed, w_qkv, w_out, w_up, w_down],
        side,
        1,
    )
    full_reduce, full_spatial, full_expand, full_embed, full_qkv = (
        item.reshape(-1, item.shape[-1]) for item in gathered[:5]
    )
    planes = lax.axis_size("narrow") // 2

    def other_side(item):
        return lax.ppermute(item, "wide", [(w, w ^ 1) for w in range(devices // (2 * planes))])

    def next_row(item, k):
        return lax.ppermute(item, "narrow", [(n, (n + 2 * k) % (2 * planes)) for n in range(2 * planes)])

    def by_row(item):
        return [item] + [next_row(item, k) for k in range(1, planes)]

    outs_in, downs_in = by_row(gathered[5]), by_row(gathered[7])
    ups_in = [gathered[6], other_side(gathered[6])]
    gains, pre_first, columns, pre_second, second, bn_unit, bn_inv, joined, start, normed0_low, packed = kept
    full_bn_gain, full_bn_shift = gains[0], gains[1]
    full_pre, full_attn, full_mid = gains[2, :D], gains[3, :D], gains[4, :D]
    full_ffn = gains[5:8].reshape(-1)
    full_table = gains[8:11].reshape(HEADS, 2 * RSPAN)
    pre_joined = bn_unit * full_bn_gain + full_bn_shift + stem_in.astype(jnp.float32)
    unused, unit0, inv0 = layer_norm(start, full_pre)
    win = windows(segments)
    attended, logsums, bias = attend(packed, segments, bias_strips(full_table), win)
    scale_row = jnp.repeat(head_scale, HDIM)[None, :]
    hidden = w_up.shape[1]
    mixed, mixed_low, normed2_low, narrowed_low, grad_pre_up, grad_middle, grad_branch, grad_attended, sums = middle_part(
        attended, start, d_out, gains, scale_row, outs_in, ups_in, downs_in, hidden, 5
    )
    grad_packed, grad_strips = attend_back(packed, grad_attended, attended, segments, bias, logsums, win)
    grad_table = table_from_strips(grad_strips)
    grad_normed0 = product_nt(grad_packed, full_qkv)
    grad_start_in, grad_gain_pre = layer_norm_back(
        grad_normed0, unit0, inv0, full_pre.astype(jnp.float32)
    )
    grad_tokens = grad_middle + grad_start_in
    grad_embedded = lax.dynamic_slice_in_dim(grad_tokens, first_at, patch_count, 0).astype(jnp.bfloat16)
    grad_w_embed = product_tn(joined, grad_embedded)
    grad_joined = product_nt(grad_embedded, full_embed)
    grad_pre_joined = smooth_back(pre_joined, grad_joined)
    lines = lax.axis_size("wide") // 2
    grad_w_embed = grad_w_embed.astype(jnp.bfloat16).reshape(lines, 2, planes, 2, -1, D)
    results = finish(
        [
            (d_out, narrowed_low, "blocks"),
            (normed2_low, grad_pre_up, "blocks"),
            (normed0_low, grad_packed, "blocks"),
            (mixed_low, grad_branch, "rows"),
        ],
        (grad_w_embed, grad_pre_joined, columns, stem_in),
        [
            bn_unit,
            gains,
            bn_inv,
            pre_second,
            pre_first,
            second,
            full_expand,
            full_spatial,
            full_reduce,
            sums,
            grad_gain_pre.reshape(1, -1),
            grad_table.reshape(3, -1),
        ],
        side,
        2,
    )
    sum_down, sum_up, sum_qkv, sum_out, sum_embed, sum_expand, sum_spatial, sum_reduce, grad_features, small = results
    grad_features = grad_features.reshape(features.shape)
    sum_down = sum_down.T
    width = 3 * D // (2 * planes)
    sum_qkv = jnp.where(
        lax.axis_index("narrow") % 2 == 0, sum_qkv[:, :width], sum_qkv[:, sum_qkv.shape[1] - width :]
    )

    def own(item):
        part = item.shape[0] // devices
        return lax.dynamic_slice_in_dim(item, me * part, part)

    sum_bn_shift, sum_bn_gain = own(small[0]), own(small[1])
    sum_pre, sum_attn, sum_mid = own(small[2, :D]), own(small[3, :D]), own(small[4, :D])
    sum_ffn = own(small[5:8].reshape(-1))
    breadth = 2 * RSPAN // devices
    sum_table = lax.dynamic_slice_in_dim(small[8:11].reshape(HEADS, -1), me * breadth, breadth, 1)
    grad_head = jnp.sum(small[11, :D].reshape(HEADS, HDIM), axis=1)
    return (
        mixed,
        grad_tokens,
        grad_features,
        sum_qkv,
        sum_out,
        sum_up,
        sum_down,
        sum_pre,
        sum_attn,
        sum_mid,
        sum_ffn,
        sum_table,
        grad_head,
        sum_reduce,
        sum_spatial,
        sum_expand,
        sum_embed,
        sum_bn_gain,
        sum_bn_shift,
    )


def solution(mesh):
    placed = (
        P(("wide", "narrow"), None),
        P(("wide", "narrow"), None, None, None),
        P(("wide", "narrow"), None),
        P(("wide", "narrow"), None),
        P(("wide", "narrow"), None),
        P(("wide", "narrow"), None),
        P(("wide", "narrow"), None),
        P(("wide", "narrow"), None),
        P(("wide", "narrow")),
        P(("wide", "narrow")),
        P(("wide", "narrow")),
        P(("wide", "narrow")),
        P(None, ("wide", "narrow")),
        P(),
        P(("wide", "narrow"), None),
        P(("wide", "narrow"), None),
        P(("wide", "narrow"), None),
        P(("wide", "narrow"), None),
        P(("wide", "narrow")),
        P(("wide", "narrow")),
        P(("wide", "narrow"), None),
    )
    return jax.shard_map(
        local,
        mesh=mesh,
        in_specs=placed,
        out_specs=(
            P(("wide", "narrow"), None),
            P(("wide", "narrow"), None),
            P(("wide", "narrow"), None, None, None),
            P("wide", "narrow"),
            P(("wide", "narrow"), None),
            P("wide", "narrow"),
            P("narrow", "wide"),
            P(("wide", "narrow")),
            P(("wide", "narrow")),
            P(("wide", "narrow")),
            P(("wide", "narrow")),
            P(None, ("wide", "narrow")),
            P(),
            P(("wide", "narrow"), None),
            P(("wide", "narrow"), None),
            P(("wide", "narrow"), None),
            P(("wide", "narrow"), None),
            P(("wide", "narrow")),
            P(("wide", "narrow")),
        ),
        check_vma=False,
    )
```
